512 devices in a mesh: bx: 8 (over z), by: 16 (over y, core), freq: 4 (over x).
Axes of the slice: x: 4, y: 8, z: 8, core: 2. Of those that a mesh axis runs over, the one named last changes fastest.
Arguments:
- leaf_maps: float32 [32, 16, 256, 256], P(('freq', 'bx'), 'by'), parts along dimension 0, as said below
- leaf_operator: float32 [472, 472], replicated, as said below
- region_eps: float32 [8, 472], replicated, may hold values from 1 to 12
- wave_sq: float32 [4], P('freq'), parts along dimension 0, may hold values from 0.01 to 0.06
- region_labels: int32 [8, 16], P('bx', 'by'), may hold values from 0 to 7
- build_flags: int32 [8, 16], P('bx', 'by'), may hold values from 0 to 1, as said below
Outputs:
- dtn_rows: float32 [32, 16, 96, 768], P(('freq', 'bx'), 'by'), parts along dimension 0
The draws below stay inside these ranges and needn't reach their ends.
There are 4 independent parts, one for each index of `freq`. The reference program is written for one: setup_inputs(seed, part) draws one part's arguments, and reference() takes and returns one part's arrays. A program takes and returns all parts, laid end to end along the dimension named above; an argument that names none is the same for every part. Nothing has to cross between parts.
Inputs may be any that keep to these rules, and one draw needn't show every extreme that they name: Every leaf_maps[i, j] is symmetric up to rounding with all eigenvalues 1 or more. leaf_operator is symmetric up to rounding, and leaf_operator minus any diagonal matrix with entries below 1 is positive definite. `build_flags`: exactly max(1, 16) leaves are flagged.
All inputs are finite; a program needn't handle non-finite values.
Results may differ from the reference program's by a relative error of at most 0.0003.
Values sent between devices are 32-bit elements; how exact they have to be, the bound alone decides.
No kernel may reach another device: no remote copies, remote signals or barrier semaphores. Data moves between devices by JAX's collectives and lax.ppermute only.
A program may use at most 64 MiB of HBM per device.

```python
import math
import jax
import jax.numpy as jnp
from jax import lax

ORDER = 8
REGIONS = 8
LEAF = 256
PTS = 472
N_BX = 8
N_BY = 16


def positive_blocks(key, leading, size, low_gain, high_gain, low_floor, high_floor):
    sign_key, gain_key, floor_key = jax.random.split(key, 3)
    signs = jnp.where(jax.random.bernoulli(sign_key, 0.5, leading + (size, size)), 1.0, -1.0).astype(jnp.float32) / math.sqrt(size)
    gains = jnp.exp(jax.random.uniform(gain_key, leading + (size,), jnp.float32, math.log(low_gain), math.log(high_gain)))
    floors = jax.random.uniform(floor_key, leading + (size,), jnp.float32, low_floor, high_floor)
    coupled = jnp.einsum('...ik,...jk->...ij', signs * gains[..., None, :], signs, precision=lax.Precision.HIGHEST)
    return coupled + floors[..., :, None] * jnp.eye(size, dtype=jnp.float32)


def draw_leaf_maps(key, part):
    key = jax.random.fold_in(key, 11)
    return positive_blocks(key, (N_BX, N_BY), LEAF, 0.01, 30.0, 1.0, 2.0)


def draw_leaf_operator(key, part):
    key = jax.random.fold_in(key, 23)
    return positive_blocks(key, (), PTS, 0.01, 30.0, 1.0, 2.0)


def draw_build_flags(key, part):
    key = jax.random.fold_in(key, 37)
    total = N_BX * N_BY
    chosen = max(1, total // 8)
    order = jax.random.permutation(key, total)
    return (order < chosen).astype(jnp.int32).reshape((N_BX, N_BY))


def place_ends(result, key, least, top_value):
    longest = result.shape.index(max(result.shape))
    spots = []
    for shift in (0, 1):
        where = [jax.random.randint(jax.random.fold_in(key, axis), (), 0, length) for axis, length in enumerate(result.shape)]
        where[longest] = (where[longest] + shift) % result.shape[longest]
        spots.append(tuple(where))
    return result.at[spots[0]].set(least).at[spots[1]].set(top_value)


def setup_inputs(seed: int = 0, part: int = 0) -> dict:
    splits = jax.random.split(jax.random.key(seed), 7)
    part_splits = jax.random.split(jax.random.fold_in(splits[6], part), 7)
    return {
        "leaf_maps": draw_leaf_maps(jax.random.fold_in(jax.random.fold_in(splits[6], part), 71), part),
        "leaf_operator": draw_leaf_operator(jax.random.fold_in(splits[6], 71), part),
        "region_eps": jnp.clip(jax.random.uniform(splits[2], (REGIONS, PTS), jnp.float32, 1.0, 12.0), 1.0, 12.0),
        "wave_sq": jnp.clip(jnp.exp(jax.random.uniform(part_splits[3], (1,), jnp.float32, math.log(0.01), math.log(0.06))), 0.01, 0.06),
        "region_labels": place_ends(jax.random.randint(splits[4], (N_BX, N_BY), 0, REGIONS), jax.random.fold_in(splits[4], 1), 0, REGIONS - 1).astype(jnp.int32),
        "build_flags": draw_build_flags(jax.random.fold_in(splits[6], 71), part),
    }


first_level = (((3, 4),), ((0, 3),), ((2, 3),), ((0, 2), (3, 4)))
second_level = (((1, 2), (4, 5)), ((0, 1), (2, 4), (5, 6)), ((0, 1), (3, 4)), ((1, 3), (4, 6)))
third_level = (((3, 4), (7, 8)), ((0, 3), (4, 7)), ((1, 2), (5, 6)), ((0, 1), (2, 5), (6, 8)))

def pick(matrix, spans, axis, face):
    pieces = [lax.slice_in_dim(matrix, lower * face, upper * face, axis=axis) for lower, upper in spans]
    return jnp.concatenate(pieces, axis=axis)

def interface_solve(alpha_rows, beta_rows, level, face):
    system = pick(alpha_rows, level[0], 1, face) + pick(beta_rows, level[2], 1, face)
    right = jnp.concatenate([pick(alpha_rows, level[1], 1, face), pick(beta_rows, level[3], 1, face)], axis=1)
    factor = jnp.linalg.cholesky(system)
    return jax.scipy.linalg.cho_solve((factor, True), right)

def outer_rows(ext_rows, solved, level, face, is_alpha):
    coupling = jnp.where(is_alpha, pick(ext_rows, level[0], 1, face), pick(ext_rows, level[2], 1, face))
    direct = jnp.where(is_alpha, pick(ext_rows, level[1], 1, face), pick(ext_rows, level[3], 1, face))
    blank = jnp.zeros_like(direct)
    block = jnp.where(is_alpha, jnp.concatenate([direct, blank], axis=1), jnp.concatenate([blank, direct], axis=1))
    return block - jnp.dot(coupling, solved, precision=lax.Precision.HIGHEST)

def full_merge(alpha_map, beta_map, level, face):
    solved = interface_solve(pick(alpha_map, level[0], 0, face), pick(beta_map, level[2], 0, face), level, face)
    upper = outer_rows(pick(alpha_map, level[1], 0, face), solved, level, face, True)
    lower = outer_rows(pick(beta_map, level[3], 0, face), solved, level, face, False)
    return jnp.concatenate([upper, lower], axis=0)

def merge_pairs(alpha_maps, beta_maps, level, face):
    leading = alpha_maps.shape[:-2]
    size = alpha_maps.shape[-1]
    merged = jax.vmap(lambda left, right: full_merge(left, right, level, face))(alpha_maps.reshape((-1, size, size)), beta_maps.reshape((-1, size, size)))
    return merged.reshape(leading + merged.shape[-2:])

def build_map(operator, table, label, wave, leaf):
    shift = wave * table[label]
    inner = operator[leaf:, leaf:] - jnp.diag(shift[leaf:])
    factor = jnp.linalg.cholesky(inner)
    solved = jax.scipy.linalg.cho_solve((factor, True), operator[leaf:, :leaf])
    edge = operator[:leaf, :leaf] - jnp.diag(shift[:leaf])
    return edge - jnp.dot(operator[:leaf, leaf:], solved, precision=lax.Precision.HIGHEST)

def reference(leaf_maps, leaf_operator, region_eps, wave_sq, region_labels, build_flags):
    face = ORDER * ORDER
    leaf = 4 * face
    wave = wave_sq[0]
    flat_maps = leaf_maps.reshape((N_BX * N_BY, leaf, leaf))
    flat_flags = build_flags.reshape((N_BX * N_BY,))
    flat_labels = region_labels.reshape((N_BX * N_BY,))

    def settle(item):
        given, flag, label = item
        return lax.cond(flag > 0, lambda: build_map(leaf_operator, region_eps, label, wave, leaf), lambda: given)
    maps = lax.map(settle, (flat_maps, flat_flags, flat_labels))
    maps = maps.reshape((N_BX, N_BY // 2, 2, leaf, leaf))
    first = merge_pairs(maps[:, :, 0], maps[:, :, 1], first_level, face)
    size_one = 6 * face
    first = first.reshape((N_BX // 2, 2, N_BY // 2, size_one, size_one))
    second = merge_pairs(first[:, 0], first[:, 1], second_level, face)
    size_two = 8 * face
    second = second.reshape((N_BX // 2, N_BY // 4, 2, size_two, size_two))
    third = merge_pairs(second[:, :, 0], second[:, :, 1], third_level, face)
    size_three = 12 * face
    rows = size_three // 8
    third = third.reshape((N_BX // 2, N_BY // 4, 2, 2, 2, rows, size_three))
    third = jnp.transpose(third, (0, 3, 1, 2, 4, 5, 6))
    return third.reshape((N_BX, N_BY, rows, size_three))
```

```python
import functools

import jax
import jax.numpy as jnp
from jax import lax
from jax.experimental import pallas as pl
from jax.experimental.pallas import tpu as pltpu
from jax.sharding import PartitionSpec as P

FACE = 64
LEAF = 4 * FACE
F32 = jnp.float32
BF16 = jnp.bfloat16


def swapped(shard, axis, stride):
    return lax.ppermute(shard, axis, [(i, i ^ 1 << stride) for i in range(lax.axis_size(axis))])


def split(x):
    high = x.astype(BF16)
    return high, (x - high.astype(F32)).astype(BF16)


def dot(a, b):
    return jnp.dot(a, b, preferred_element_type=F32)


def product(a, b):
    (a_high, a_low), (b_high, b_low) = a, b
    if a_high.shape[1] > 128:
        return dot(a_high, b_high) + (dot(a_high, b_low) + dot(a_low, b_high))
    twice = dot(
        jnp.concatenate([a_high, a_low], axis=1), jnp.concatenate([b_high, b_high], axis=0)
    )
    return twice + dot(a_high, b_low)


def spd_inverse(matrix):
    size = matrix.shape[0]
    shape = (8, size)
    count = size // 8
    tiles = [matrix[8 * g : 8 * g + 8] for g in range(count)]
    lane = lax.broadcasted_iota(jnp.int32, shape, 1)
    sub = lax.broadcasted_iota(jnp.int32, shape, 0)

    def column(tile, c):
        return jnp.broadcast_to(tile[:, c : c + 1], shape)

    def row(tile, r):
        return jnp.broadcast_to(tile[r : r + 1, :], shape)

    for k in range(count):
        first = 8 * k
        inside = (lane >= first) & (lane < first + 8)
        pivot = tiles[k]
        columns = [column(pivot, first + j) for j in range(8)]
        element = {(i, j): row(columns[i], j) for i in range(8) for j in range(i + 1)}
        element = {(j, i): v for (i, j), v in element.items()}
        cleared = jnp.where(inside, (lane - first == sub).astype(F32), pivot)
        rows = [row(cleared, i) for i in range(8)]
        inverse = [None] * 8
        lower = {}
        for p in range(8):
            inverse[p] = pl.reciprocal(element[p, p])
            for i in range(p + 1, 8):
                lower[i, p] = element[p, i] * inverse[p]
            for i in range(p + 1, 8):
                for j in range(i, 8):
                    element[i, j] = element[i, j] - lower[i, p] * element[p, j]
                rows[i] = rows[i] - lower[i, p] * rows[p]
        for p in reversed(range(8)):
            value = rows[p] * inverse[p]
            for i in range(p + 1, 8):
                value = value - lower[i, p] * rows[i]
            rows[p] = value
        for g in range(count):
            if g == k:
                new = rows[0]
                for i in range(1, 8):
                    new = jnp.where(sub == i, rows[i], new)
            else:
                new = jnp.where(inside, 0.0, tiles[g])
                for j in range(8):
                    new = new - column(tiles[g], first + j) * rows[j]
            tiles[g] = new
    return jnp.concatenate(tiles, axis=0)


def build_kernel(label, flag, wave, given, operator, table, out):
    flagged = flag[0, 0] > 0

    @pl.when(jnp.logical_not(flagged))
    def _():
        out[...] = given[...]

    @pl.when(flagged)
    def _():
        shift = wave[0] * table[pl.ds(label[0, 0], 1), :]
        size = operator.shape[0]
        middle = LEAF + 128
        edge, one, two = slice(0, LEAF), slice(LEAF, middle), slice(middle, size)

        def shifted(span):
            block = operator[span, span]
            ids = lax.broadcasted_iota(jnp.int32, block.shape, 0)
            diagonal = ids == lax.broadcasted_iota(jnp.int32, block.shape, 1)
            return block - jnp.where(diagonal, shift[:, span], 0.0)

        inverse = spd_inverse(shifted(one))
        right = split(operator[one, edge]), split(operator[one, two])
        solved = [split(product(split(inverse), r)) for r in right]
        left = split(operator[two, one])
        inner = shifted(two) - product(left, solved[1])
        coupled = operator[two, edge] - product(left, solved[0])
        left = split(operator[edge, one])
        border = shifted(edge) - product(left, solved[0])
        across = operator[edge, two] - product(left, solved[1])
        inverse = spd_inverse(inner)
        solved = split(product(split(inverse), split(coupled)))
        out[...] = border - product(split(across), solved)


def halves(shape):
    return lax.broadcasted_iota(jnp.int32, shape, 1) < FACE


def turn(tile):
    return pltpu.roll(tile, FACE, 1)


def first_kernel(place, mine, theirs, out, message, direct, coupling):
    across, third, lead = place[0], place[1], place[2]
    is_alpha = lead == 0
    left = halves((FACE, 128))
    near = jnp.where(across == 0, 1, 0)

    def load(alpha, block, tile):
        spot = pl.ds(pl.multiple_of(block * FACE, FACE), FACE)
        span = slice(128 * tile, 128 * tile + 128)
        own = is_alpha if alpha else jnp.logical_not(is_alpha)
        return jnp.where(own, mine[spot, span], theirs[spot, span])

    def alpha_rows(block):
        sides = load(True, block, 0)
        ends = load(True, block, 1)
        sides = jnp.where(across == 0, turn(sides), sides)
        tiles = (
            jnp.where(left, sides, 0.0),
            jnp.where(left, jnp.where(third == 0, 0.0, ends), sides),
            jnp.where(left & (third == 0), ends, 0.0),
        )
        return tiles, turn(ends)

    def beta_rows(block):
        sides = load(False, block, 0)
        ends = load(False, block, 1)
        other = turn(sides)
        near_far = jnp.where(across == 0, other, sides)
        far_near = jnp.where(across == 0, sides, other)
        flipped = turn(ends)
        tiles = (
            jnp.where(left, 0.0, far_near),
            jnp.where(left & (third == 0), flipped, 0.0),
            jnp.where(
                third == 0,
                jnp.where(left, 0.0, near_far),
                jnp.where(left, far_near, ends),
            ),
        )
        return tiles, ends

    tiles_a, meet_a = alpha_rows(3)
    tiles_b, meet_b = beta_rows(2)
    system = (meet_a + meet_b)[:, :FACE]
    right = jnp.concatenate([x + y for x, y in zip(tiles_a, tiles_b)], axis=1)
    spots = (
        (alpha_rows, near, 0),
        (beta_rows, near, 1),
        (alpha_rows, 1 - near, 3),
        (alpha_rows, 2, jnp.where(third == 0, 4, 2)),
        (beta_rows, 1 - near, jnp.where(third == 0, 5, 4)),
        (beta_rows, 3, jnp.where(third == 0, 2, 5)),
    )
    for rows, block, place_to in spots:
        tiles, meet = rows(block)
        spot = pl.ds(pl.multiple_of(place_to * FACE, FACE), FACE)
        for i in range(3):
            direct[spot, 128 * i : 128 * i + 128] = tiles[i]
        coupling[spot, :] = meet
    inverse = spd_inverse(system)
    solved = split(product(split(inverse), split(right)))
    merged = direct[...] - product(split(coupling[:, :FACE]), solved)
    out[...] = merged
    message[0:128, :] = merged[0:128, 0:128]
    message[128:256, :] = merged[0:128, 128:256]
    message[256:384, :] = merged[0:128, 256:384]
    message[384:448, :] = merged[128:192, 128:256]
    message[448:512, :] = merged[128:192, 256:384]


def second_kernel(place, own, theirs, face_rows, outer):
    across, lead = place[0], place[2]
    is_alpha = across == 0
    near = slice(0, 128)

    def assemble(alpha, beta):
        rows = (alpha or beta)[0].shape[0]
        left = halves((rows, 128))
        blank = jnp.zeros((rows, 128), F32)
        if alpha is None:
            return (
                jnp.where(left, 0.0, turn(beta[0])),
                blank,
                jnp.where(left, 0.0, beta[0]),
                beta[1],
            )
        turned = turn(alpha[1])
        middle = jnp.where(left, turn(alpha[0]), turned)
        if beta is None:
            return jnp.where(left, alpha[0], 0.0), middle, jnp.where(left, turned, 0.0), blank
        return (
            jnp.where(left, alpha[0], turn(beta[0])),
            middle,
            jnp.where(left, turned, beta[0]),
            beta[1],
        )

    def both(mine, other):
        return jnp.where(is_alpha, mine, other), jnp.where(is_alpha, other, mine)

    system = own[near, 0:128] + theirs[near, :]
    own_near = own[near, 128:256], own[near, 256:384]
    their_near = theirs[128:256, :], theirs[256:384, :]
    one = both(own_near[0], their_near[0])
    two = both(own_near[1], their_near[1])
    right = jnp.concatenate(assemble((one[0], two[0]), (one[1], two[1])), axis=1)
    face = both(own[128:192, 128:256], theirs[384:448, :])
    back = both(own[128:192, 256:384], theirs[448:512, :])
    start = pl.multiple_of(3 * FACE + lead * 96, 32)
    mine = own[pl.ds(start, 96), 128:256], own[pl.ds(start, 96), 256:384]
    as_alpha = assemble(mine, None)
    as_beta = assemble(None, mine)
    direct_mine = [jnp.where(is_alpha, x, y) for x, y in zip(as_alpha, as_beta)]
    direct = jnp.concatenate(
        [
            jnp.concatenate(assemble((face[0], back[0]), None), axis=1),
            jnp.concatenate(assemble(None, (face[1], back[1])), axis=1),
            jnp.concatenate(direct_mine, axis=1),
        ],
        axis=0,
    )
    link_mine = own[128:192, 0:128]
    link_their = jnp.transpose(theirs[128:256, :])[0:FACE]
    links = both(link_mine, link_their)
    coupling = jnp.concatenate([links[0], links[1], own[pl.ds(start, 96), 0:128]], axis=0)
    right = split(right)
    coupling = split(coupling)
    inverse = spd_inverse(system)
    solved = split(product(coupling, split(inverse)))
    merged = direct - product(solved, right)
    face_rows[...] = merged[0:128]
    outer[...] = merged[128:224]


def third_kernel(place, own, theirs, outer, out):
    third = place[1]
    system = own[:, 0:128] + theirs[:, 0:128]
    right = split(jnp.concatenate([own[:, 128:], theirs[:, 128:]], axis=1))
    coupling = split(outer[:, 0:128])
    inverse = spd_inverse(system)
    solved = split(product(coupling, split(inverse)))
    update = product(solved, right)
    half = 6 * FACE
    mine = pl.multiple_of(third * half, 128)
    other = pl.multiple_of((1 - third) * half, 128)
    out[:, pl.ds(mine, half)] = outer[:, 128:] - update[:, :half]
    out[:, pl.ds(other, half)] = -update[:, half:]


def shapes(*sizes):
    return [jax.ShapeDtypeStruct(size, F32) for size in sizes]


def body(leaf_maps, leaf_operator, region_eps, wave_sq, region_labels, build_flags):
    smem = pl.BlockSpec(memory_space=pltpu.SMEM)
    vmem = pl.BlockSpec(memory_space=pltpu.VMEM)
    params = pltpu.CompilerParams(vmem_limit_bytes=32 * 1024 * 1024)
    call = functools.partial(pl.pallas_call, compiler_params=params)
    across = lax.axis_index("bx") % 2
    upward = lax.axis_index("by")
    place = jnp.stack([across, upward // 2 % 2, upward % 2]).astype(jnp.int32)
    (leaf_map,) = call(
        build_kernel,
        out_shape=shapes((LEAF, LEAF)),
        in_specs=[smem, smem, smem, vmem, vmem, vmem],
        out_specs=[vmem],
        name="leaf_build",
    )(region_labels, build_flags, wave_sq, leaf_maps[0, 0], leaf_operator, region_eps)
    theirs = swapped(leaf_map, "by", 0)
    first, message = call(
        first_kernel,
        out_shape=shapes((6 * FACE, 6 * FACE), (8 * FACE, 128)),
        in_specs=[smem, vmem, vmem],
        out_specs=[vmem, vmem],
        scratch_shapes=[pltpu.VMEM((6 * FACE, 6 * FACE), F32), pltpu.VMEM((6 * FACE, 128), F32)],
        name="first_merge",
    )(place, leaf_map, theirs)
    theirs = swapped(message, "bx", 0)
    face_rows, outer = call(
        second_kernel,
        out_shape=shapes((128, 8 * FACE), (96, 8 * FACE)),
        in_specs=[smem, vmem, vmem],
        out_specs=[vmem, vmem],
        name="second_merge",
    )(place, first, theirs)
    theirs = swapped(face_rows, "by", 1)
    (result,) = call(
        third_kernel,
        out_shape=shapes((96, 12 * FACE)),
        in_specs=[smem, vmem, vmem, vmem],
        out_specs=[vmem],
        name="third_merge",
    )(place, face_rows, theirs, outer)
    return result.reshape((1, 1, 96, 12 * FACE))


def solution(mesh):
    placed = (
        P(("freq", "bx"), "by", None, None),
        P(),
        P(),
        P("freq"),
        P("bx", "by"),
        P("bx", "by"),
    )
    return jax.shard_map(
        body,
        mesh=mesh,
        in_specs=placed,
        out_specs=P(("freq", "bx"), "by", None, None),
        check_vma=False,
    )
```

```python
import jax
import jax.numpy as jnp
from jax import lax
from jax.experimental import pallas as pl
from jax.experimental.pallas import tpu as pltpu
from jax.sharding import PartitionSpec as P

FACE = 64
LEAF = 4 * FACE
F32 = jnp.float32
BF16 = jnp.bfloat16


def swapped(shard, axis, stride):
    return lax.ppermute(shard, axis, [(i, i ^ 1 << stride) for i in range(lax.axis_size(axis))])


def split(x):
    high = x.astype(BF16)
    return high, (x - high.astype(F32)).astype(BF16)


def dot(a, b):
    return jnp.dot(a, b, preferred_element_type=F32)


def product(a, b):
    (a_high, a_low), (b_high, b_low) = a, b
    depth = a_high.shape[1]
    if depth % 128 and depth != FACE:
        return dot(a_high, b_high) + (dot(a_high, b_low) + dot(a_low, b_high))
    twice = dot(
        jnp.concatenate([a_high, a_low], axis=1), jnp.concatenate([b_high, b_high], axis=0)
    )
    return twice + dot(a_high, b_low)


def spd_inverse(matrix):
    size = matrix.shape[0]
    shape = (8, size)
    count = size // 8
    tiles = [matrix[8 * g : 8 * g + 8] for g in range(count)]
    lane = lax.broadcasted_iota(jnp.int32, shape, 1)
    sub = lax.broadcasted_iota(jnp.int32, shape, 0)

    def column(tile, c):
        return jnp.broadcast_to(tile[:, c : c + 1], shape)

    def row(tile, r):
        return jnp.broadcast_to(tile[r : r + 1, :], shape)

    for k in range(count):
        first = 8 * k
        inside = (lane >= first) & (lane < first + 8)
        pivot = tiles[k]
        columns = [column(pivot, first + j) for j in range(8)]
        element = {(j, i): row(columns[i], j) for i in range(8) for j in range(i + 1)}
        cleared = jnp.where(inside, (lane - first == sub).astype(F32), pivot)
        rows = [row(cleared, i) for i in range(8)]
        inverse = [None] * 8
        lower = {}
        ahead = k + 1 < count
        if ahead:
            after = jnp.where(inside, 0.0, tiles[k + 1])
            strip = [column(tiles[k + 1], first + j) for j in range(8)]
        for p in range(8):
            inverse[p] = pl.reciprocal(element[p, p], approx=True)
            for i in range(p + 1, 8):
                lower[i, p] = element[p, i] * inverse[p]
            for i in range(p + 1, 8):
                for j in range(i, 8):
                    element[i, j] = element[i, j] - lower[i, p] * element[p, j]
                rows[i] = rows[i] - lower[i, p] * rows[p]
            if ahead:
                scaled = strip[p] * inverse[p]
                for j in range(p + 1, 8):
                    strip[j] = strip[j] - scaled * element[p, j]
                after = after - scaled * rows[p]
        for p in reversed(range(8)):
            value = rows[p] * inverse[p]
            for i in reversed(range(p + 1, 8)):
                value = value - lower[i, p] * rows[i]
            rows[p] = value
        for g in range(count):
            if g == k:
                new = rows[0]
                for i in range(1, 8):
                    new = jnp.where(sub == i, rows[i], new)
            elif g == k + 1:
                new = after
            else:
                new = jnp.where(inside, 0.0, tiles[g])
                for j in reversed(range(8)):
                    new = new - column(tiles[g], first + j) * rows[j]
            tiles[g] = new
    return jnp.concatenate(tiles, axis=0)


def build_kernel(
    label_at, flag_at, wave_at, given, operator, table_at, out, scalars, wave, table, one, two, edge, sems
):
    size = operator.shape[0]
    middle = LEAF + 128
    copies = [
        pltpu.make_async_copy(source, target, sems.at[i])
        for i, (source, target) in enumerate(
            (
                (flag_at, scalars.at[pl.ds(0, 1)]),
                (label_at, scalars.at[pl.ds(1, 1)]),
                (wave_at, wave),
                (table_at, table),
                (operator.at[pl.ds(LEAF, 128)], one),
                (operator.at[pl.ds(middle, size - middle)], two),
                (operator.at[pl.ds(0, LEAF)], edge),
                (given, out),
            )
        )
    ]
    for copy in copies:
        copy.start()
    for copy in copies:
        copy.wait()

    @pl.when(scalars[0, 0] > 0)
    def _():
        shift = wave[0] * table[pl.ds(scalars[1, 0], 1), :]
        border, near, far = slice(0, LEAF), slice(LEAF, middle), slice(middle, size)

        def shifted(ref, span):
            block = ref[:, span]
            ids = lax.broadcasted_iota(jnp.int32, block.shape, 0)
            diagonal = ids == lax.broadcasted_iota(jnp.int32, block.shape, 1)
            return block - jnp.where(diagonal, shift[:, span], 0.0)

        right = split(one[:, border]), split(one[:, far])
        left = split(two[:, near])
        inverse = split(spd_inverse(shifted(one, near)))
        solved_far = split(product(inverse, right[1]))
        inner = shifted(two, far) - product(left, solved_far)
        solved = split(product(inverse, right[0]))
        coupled = split(two[:, border] - product(left, solved))
        left = split(edge[:, near])
        merged = shifted(edge, border) - product(left, solved)
        across = split(edge[:, far] - product(left, solved_far))
        inverse = split(spd_inverse(inner))
        solved = split(product(inverse, coupled))
        out[...] = merged - product(across, solved)


def halves(shape):
    return lax.broadcasted_iota(jnp.int32, shape, 1) < FACE


def turn(tile):
    return pltpu.roll(tile, FACE, 1)


def leaf_rows(place, mine, theirs):
    across, third, lead = place[0], place[1], place[2]
    is_alpha = lead == 0
    left = halves((FACE, 128))

    def load(alpha, block, tile):
        spot = pl.ds(pl.multiple_of(block * FACE, FACE), FACE)
        span = slice(128 * tile, 128 * tile + 128)
        own = is_alpha if alpha else jnp.logical_not(is_alpha)
        return jnp.where(own, mine[spot, span], theirs[spot, span])

    def alpha_rows(block):
        sides = load(True, block, 0)
        ends = load(True, block, 1)
        sides = jnp.where(across == 0, turn(sides), sides)
        tiles = (
            jnp.where(left, sides, 0.0),
            jnp.where(left, jnp.where(third == 0, 0.0, ends), sides),
            jnp.where(left & (third == 0), ends, 0.0),
        )
        return jnp.concatenate(tiles, axis=1), turn(ends)

    def beta_rows(block):
        sides = load(False, block, 0)
        ends = load(False, block, 1)
        other = turn(sides)
        near_far = jnp.where(across == 0, other, sides)
        far_near = jnp.where(across == 0, sides, other)
        flipped = turn(ends)
        tiles = (
            jnp.where(left, 0.0, far_near),
            jnp.where(left & (third == 0), flipped, 0.0),
            jnp.where(
                third == 0,
                jnp.where(left, 0.0, near_far),
                jnp.where(left, far_near, ends),
            ),
        )
        return jnp.concatenate(tiles, axis=1), ends

    return alpha_rows, beta_rows


def either(flag, one, other):
    return [jnp.where(flag, x, y) for x, y in zip(one, other)]


def first_kernel(place, mine, theirs, system_out, near_out, solved_high, solved_low):
    alpha_rows, beta_rows = leaf_rows(place, mine, theirs)
    near = jnp.where(place[0] == 0, 1, 0)
    tiles_a, meet_a = alpha_rows(3)
    tiles_b, meet_b = beta_rows(2)
    system = (meet_a + meet_b)[:, :FACE]
    right = split(tiles_a + tiles_b)
    tiles_a, meet_a = alpha_rows(near)
    tiles_b, meet_b = beta_rows(near)
    direct = jnp.concatenate([tiles_a, tiles_b], axis=0)
    coupling = split(jnp.concatenate([meet_a, meet_b], axis=0)[:, :FACE])
    inverse = split(spd_inverse(system))
    solved = split(product(inverse, right))
    merged = direct - product(coupling, solved)
    system_out[...] = merged[:, 0:128]
    near_out[0:128, :] = merged[:, 128:256]
    near_out[128:256, :] = merged[:, 256:384]
    solved_high[...], solved_low[...] = solved


def face_kernel(place, mine, theirs, near_rows, solved_high, solved_low, message, link):
    alpha_rows, beta_rows = leaf_rows(place, mine, theirs)
    direct, coupling = either(place[1] == 0, beta_rows(3), alpha_rows(2))
    solved = solved_high[...], solved_low[...]
    merged = direct - product(split(coupling[:, :FACE]), solved)
    message[0:256, :] = near_rows[...]
    message[256:320, :] = merged[:, 128:256]
    message[320:384, :] = merged[:, 256:384]
    link[...] = merged[:, 0:128]


def second_kernel(
    place, own, received, mine, theirs, solved_high, solved_low, inverse_high, inverse_low, outer, direct, coupling
):
    alpha_rows, beta_rows = leaf_rows(place, mine, theirs)
    third, lead = place[1], place[2]
    far = jnp.where(place[0] == 0, 0, 1)
    direct[0:64, :], coupling[0:64, :] = alpha_rows(far)
    at_two = alpha_rows(2)
    at_far = beta_rows(far)
    at_three = beta_rows(3)
    direct[64:128, :], coupling[64:128, :] = either(third == 0, at_two, at_far)
    direct[128:192, :], coupling[128:192, :] = either(third == 0, at_far, at_three)
    spot = pl.ds(pl.multiple_of(lead * 96, 32), 96)
    solved = solved_high[...], solved_low[...]
    outer[...] = direct[spot, :] - product(split(coupling[spot, :][:, :FACE]), solved)
    inverse_high[...], inverse_low[...] = split(spd_inverse(own[...] + received[...]))


def assemble(alpha, beta):
    rows = (alpha or beta)[0].shape[0]
    left = halves((rows, 128))
    blank = jnp.zeros((rows, 128), F32)
    if alpha is None:
        tiles = (
            jnp.where(left, 0.0, turn(beta[0])),
            blank,
            jnp.where(left, 0.0, beta[0]),
            beta[1],
        )
        return jnp.concatenate(tiles, axis=1)
    turned = turn(alpha[1])
    middle = jnp.where(left, turn(alpha[0]), turned)
    if beta is None:
        tiles = jnp.where(left, alpha[0], 0.0), middle, jnp.where(left, turned, 0.0), blank
        return jnp.concatenate(tiles, axis=1)
    tiles = (
        jnp.where(left, alpha[0], turn(beta[0])),
        middle,
        jnp.where(left, turned, beta[0]),
        beta[1],
    )
    return jnp.concatenate(tiles, axis=1)


def exchange_kernel(
    place, own, received, link, inverse_high, inverse_low, system_out, rest_out, right_high, right_low
):
    is_alpha = place[0] == 0

    def both(span):
        mine, other = own[span, :], received[span, :]
        return jnp.where(is_alpha, mine, other), jnp.where(is_alpha, other, mine)

    one, two = both(slice(0, 128)), both(slice(128, 256))
    right = split(assemble((one[0], two[0]), (one[1], two[1])))
    face, back = both(slice(256, 320)), both(slice(320, 384))
    direct = jnp.concatenate(
        [assemble((face[0], back[0]), None), assemble(None, (face[1], back[1]))], axis=0
    )
    mine = link[...]
    other = jnp.transpose(received[0:128, :])[0:FACE]
    coupling = jnp.concatenate(
        [jnp.where(is_alpha, mine, other), jnp.where(is_alpha, other, mine)], axis=0
    )
    solved = split(product(split(coupling), (inverse_high[...], inverse_low[...])))
    merged = direct - product(solved, right)
    system_out[...] = merged[:, 0:128]
    rest_out[...] = merged[:, 128:512]
    right_high[...], right_low[...] = right


def third_kernel(
    place, own, received, rest, outer, inverse_high, inverse_low, right_high, right_low, half, solved_high, solved_low
):
    mine = outer[:, 128:256], outer[:, 256:384]
    direct = jnp.where(place[0] == 0, assemble(mine, None), assemble(None, mine))
    solved = split(product(split(outer[:, 0:128]), (inverse_high[...], inverse_low[...])))
    merged = direct - product(solved, (right_high[...], right_low[...]))
    coupling = split(merged[:, 0:128])
    right = split(rest[...])
    inverse = split(spd_inverse(own[...] + received[...]))
    solved = split(product(coupling, inverse))
    half[...] = merged[:, 128:512] - product(solved, right)
    solved_high[...], solved_low[...] = solved


def last_kernel(place, half, received, solved_high, solved_low, out):
    third = place[1]
    width = 6 * FACE
    mine = pl.multiple_of(third * width, 128)
    other = pl.multiple_of((1 - third) * width, 128)
    out[:, pl.ds(mine, width)] = half[...]
    solved = solved_high[...], solved_low[...]
    out[:, pl.ds(other, width)] = -product(solved, split(received[...]))


def shapes(*sizes):
    return [jax.ShapeDtypeStruct(size, F32) for size in sizes]


def pair(*size):
    return [jax.ShapeDtypeStruct(size, BF16)] * 2


def run(kernel, out_shape, *operands, scalars=1, **options):
    smem = pl.BlockSpec(memory_space=pltpu.SMEM)
    vmem = pl.BlockSpec(memory_space=pltpu.VMEM)
    return pl.pallas_call(
        kernel,
        out_shape=out_shape,
        in_specs=[smem] * scalars + [vmem] * (len(operands) - scalars),
        out_specs=[vmem] * len(out_shape),
        compiler_params=pltpu.CompilerParams(vmem_limit_bytes=32 * 1024 * 1024),
        **options,
    )(*operands)


def body(leaf_maps, leaf_operator, region_eps, wave_sq, region_labels, build_flags):
    across = lax.axis_index("bx") % 2
    upward = lax.axis_index("by")
    place = jnp.stack([across, upward // 2 % 2, upward % 2]).astype(jnp.int32)
    size = leaf_operator.shape[0]
    mine = pl.pallas_call(
        build_kernel,
        out_shape=jax.ShapeDtypeStruct((LEAF, LEAF), F32),
        in_specs=[pl.BlockSpec(memory_space=pl.ANY)] * 6,
        out_specs=pl.BlockSpec(memory_space=pltpu.VMEM),
        scratch_shapes=[
            pltpu.SMEM((2, 1), jnp.int32),
            pltpu.SMEM((1,), F32),
            pltpu.VMEM(region_eps.shape, F32),
            pltpu.VMEM((128, size), F32),
            pltpu.VMEM((size - LEAF - 128, size), F32),
            pltpu.VMEM((LEAF, size), F32),
            pltpu.SemaphoreType.DMA((8,)),
        ],
        compiler_params=pltpu.CompilerParams(vmem_limit_bytes=32 * 1024 * 1024),
        name="leaf_build",
    )(region_labels, build_flags, wave_sq, leaf_maps[0, 0], leaf_operator, region_eps)
    theirs = swapped(mine, "by", 0)
    system, near_rows, *solved = run(
        first_kernel,
        shapes((128, 128), (256, 128)) + pair(FACE, 6 * FACE),
        place,
        mine,
        theirs,
        name="first_merge",
    )
    received = swapped(system, "bx", 0)
    message, link = run(
        face_kernel,
        shapes((384, 128), (FACE, 128)),
        place,
        mine,
        theirs,
        near_rows,
        *solved,
        name="first_faces",
    )
    received_rest = swapped(message, "bx", 0)
    *inverse, outer = run(
        second_kernel,
        pair(128, 128) + shapes((96, 6 * FACE)),
        place,
        system,
        received,
        mine,
        theirs,
        *solved,
        scratch_shapes=[pltpu.VMEM((192, 6 * FACE), F32), pltpu.VMEM((192, 128), F32)],
        name="second_inverse",
    )
    system, rest, *right = run(
        exchange_kernel,
        shapes((128, 128), (128, 6 * FACE)) + pair(128, 8 * FACE),
        place,
        message,
        received_rest,
        link,
        *inverse,
        name="second_merge",
    )
    received = swapped(system, "by", 1)
    received_rest = swapped(rest, "by", 1)
    half, *solved = run(
        third_kernel,
        shapes((96, 6 * FACE)) + pair(96, 128),
        place,
        system,
        received,
        rest,
        outer,
        *inverse,
        *right,
        name="third_inverse",
    )
    (result,) = run(
        last_kernel, shapes((96, 12 * FACE)), place, half, received_rest, *solved, name="third_merge"
    )
    return result.reshape((1, 1, 96, 12 * FACE))


def solution(mesh):
    placed = (
        P(("freq", "bx"), "by", None, None),
        P(),
        P(),
        P("freq"),
        P("bx", "by"),
        P("bx", "by"),
    )
    return jax.shard_map(
        body,
        mesh=mesh,
        in_specs=placed,
        out_specs=P(("freq", "bx"), "by", None, None),
        check_vma=False,
    )
```

```python
import jax
import jax.numpy as jnp
from jax import lax
from jax.experimental import pallas as pl
from jax.experimental.pallas import tpu as pltpu
from jax.sharding import PartitionSpec as P

FACE = 64
LEAF = 4 * FACE
CUT = 288
F32 = jnp.float32
BF16 = jnp.bfloat16


def swapped(shard, axis, stride):
    return lax.ppermute(shard, axis, [(i, i ^ 1 << stride) for i in range(lax.axis_size(axis))])


def split(x):
    high = x.astype(BF16)
    return high, (x - high.astype(F32)).astype(BF16)


def thirds(x):
    high = x.astype(BF16).astype(F32)
    rest = x - high
    middle = rest.astype(BF16).astype(F32)
    return high, middle, (rest - middle).astype(BF16).astype(F32)


def dot(a, b):
    return jnp.dot(a, b, preferred_element_type=F32)


def product(a, b):
    (a_high, a_low), (b_high, b_low) = a, b
    depth = a_high.shape[1]
    if depth % 128 and depth != FACE:
        return dot(a_high, b_high) + (dot(a_high, b_low) + dot(a_low, b_high))
    twice = dot(
        jnp.concatenate([a_high, a_low], axis=1), jnp.concatenate([b_high, b_high], axis=0)
    )
    return twice + dot(a_high, b_low)


def spd_inverse(matrix, panel=4, look=2):
    size = matrix.shape[0]
    shape = (8, size)
    count = size // 8
    tiles = [matrix[8 * g : 8 * g + 8] for g in range(count)]
    lane = lax.broadcasted_iota(jnp.int32, shape, 1)
    sub = lax.broadcasted_iota(jnp.int32, shape, 0)

    def column(tile, c):
        return jnp.broadcast_to(tile[:, c : c + 1], shape)

    def row(tile, r):
        return jnp.broadcast_to(tile[r : r + 1, :], shape)

    def inside(start, stop):
        return (lane >= start) & (lane < stop)

    pivot = [column(tiles[0], j) for j in range(8)]
    for start in range(0, count, panel):
        stop = min(start + panel, count)
        last = min(stop + look, count)
        outside = [*range(last, count), *range(start)]
        if outside:
            strip = jnp.concatenate([tiles[g] for g in outside], axis=0)[:, 8 * start : 8 * stop]
            high, middle, low = thirds(strip)
            left = jnp.concatenate([high, high, middle, high, low, middle], axis=1).astype(BF16)
        for k in range(start, stop):
            first = 8 * k
            block = inside(first, first + 8)
            rows = jnp.where(block, (lane - first == sub).astype(F32), tiles[k])
            ahead = k + 1 < count
            if ahead:
                after = jnp.where(block, 0.0, tiles[k + 1])
                side = [column(tiles[k + 1], first + j) for j in range(8)]
                coming = [column(tiles[k + 1], first + 8 + j) for j in range(8)]
            scale = None
            for p in range(8):
                inverse = pl.reciprocal(row(pivot[p], p), approx=True)
                factor = jnp.where(sub == p, 0.0, pivot[p]) * inverse
                picked = row(rows, p)
                if ahead:
                    edge = side[p]
                    factor_ahead = edge * inverse
                    after = after - factor_ahead * picked
                    for j in range(8):
                        coming[j] = coming[j] - factor_ahead * row(edge, j)
                for j in range(p + 1, 8):
                    element = row(pivot[j], p)
                    pivot[j] = pivot[j] - factor * element
                    if ahead:
                        side[j] = side[j] - factor_ahead * element
                rows = rows - factor * picked
                scale = inverse if scale is None else jnp.where(sub == p, inverse, scale)
            rows = rows * scale
            picked = [row(rows, j) for j in range(8)]
            for g in range(start, last):
                if g == k:
                    tiles[g] = rows
                elif g == k + 1:
                    tiles[g] = after
                else:
                    new = jnp.where(block, 0.0, tiles[g])
                    for j in range(8):
                        new = new - column(tiles[g], first + j) * picked[j]
                    tiles[g] = new
            if ahead:
                pivot = coming
        if outside:
            right = jnp.concatenate(tiles[start:stop], axis=0)
            high, middle, low = thirds(right)
            right = jnp.concatenate([high, middle, high, low, high, middle], axis=0).astype(BF16)
            update = dot(left, right)
            block = inside(8 * start, 8 * stop)
            for i, g in enumerate(outside):
                tiles[g] = jnp.where(block, 0.0, tiles[g]) - update[8 * i : 8 * i + 8]
    return jnp.concatenate(tiles, axis=0)


def build_kernel(facts, given, operator, table_at, out, table, one, two, edge, sems):
    size = operator.shape[0]
    middle = LEAF + 128
    copies = [
        pltpu.make_async_copy(source, target, sems.at[i])
        for i, (source, target) in enumerate(
            (
                (operator.at[pl.ds(LEAF, 128)], one),
                (table_at, table),
                (operator.at[pl.ds(middle, size - middle)], two),
                (operator.at[pl.ds(0, LEAF)], edge),
                (given, out),
            )
        )
    ]
    for copy in copies:
        copy.start()
    flag = jnp.max(facts[0:1, :])
    for copy in copies:
        copy.wait()

    @pl.when(flag > 0.0)
    def _():
        labels = lax.broadcasted_iota(jnp.int32, table.shape, 0).astype(F32)
        picked = jnp.where(labels == facts[1:2, 0:1], table[...], 0.0)
        shift = facts[2:3, 0:1] * jnp.sum(picked, axis=0, keepdims=True)
        border, near, far = slice(0, LEAF), slice(LEAF, middle), slice(middle, size)

        def shifted(ref, span):
            block = ref[:, span]
            ids = lax.broadcasted_iota(jnp.int32, block.shape, 0)
            diagonal = ids == lax.broadcasted_iota(jnp.int32, block.shape, 1)
            return block - jnp.where(diagonal, shift[:, span], 0.0)

        right = split(one[:, border]), split(one[:, far])
        left = split(two[:, near])
        inverse = split(spd_inverse(shifted(one, near)))
        solved_far = split(product(inverse, right[1]))
        inner = shifted(two, far) - product(left, solved_far)
        solved = split(product(inverse, right[0]))
        coupled = split(two[:, border] - product(left, solved))
        left = split(edge[:, near])
        merged = shifted(edge, border) - product(left, solved)
        across = split(edge[:, far] - product(left, solved_far))
        inverse = split(spd_inverse(inner))
        solved = split(product(inverse, coupled))
        out[...] = merged - product(across, solved)


def halves(shape):
    return lax.broadcasted_iota(jnp.int32, shape, 1) < FACE


def turn(tile):
    return pltpu.roll(tile, FACE, 1)


def leaf_rows(place, mine, theirs):
    across, third, lead = place[0], place[1], place[2]
    is_alpha = lead == 0
    left = halves((FACE, 128))

    def load(alpha, block, tile):
        spot = pl.ds(pl.multiple_of(block * FACE, FACE), FACE)
        span = slice(128 * tile, 128 * tile + 128)
        own = is_alpha if alpha else jnp.logical_not(is_alpha)
        return jnp.where(own, mine[spot, span], theirs[spot, span])

    def alpha_rows(block):
        sides = load(True, block, 0)
        ends = load(True, block, 1)
        sides = jnp.where(across == 0, turn(sides), sides)
        tiles = (
            jnp.where(left, sides, 0.0),
            jnp.where(left, jnp.where(third == 0, 0.0, ends), sides),
            jnp.where(left & (third == 0), ends, 0.0),
        )
        return jnp.concatenate(tiles, axis=1), turn(ends)

    def beta_rows(block):
        sides = load(False, block, 0)
        ends = load(False, block, 1)
        other = turn(sides)
        near_far = jnp.where(across == 0, other, sides)
        far_near = jnp.where(across == 0, sides, other)
        flipped = turn(ends)
        tiles = (
            jnp.where(left, 0.0, far_near),
            jnp.where(left & (third == 0), flipped, 0.0),
            jnp.where(
                third == 0,
                jnp.where(left, 0.0, near_far),
                jnp.where(left, far_near, ends),
            ),
        )
        return jnp.concatenate(tiles, axis=1), ends

    return alpha_rows, beta_rows


def either(flag, one, other):
    return [jnp.where(flag, x, y) for x, y in zip(one, other)]


def third_tile(one, two):
    return jnp.concatenate([one[256:CUT, :], two[0 : 384 - CUT, :]], axis=0)


def first_kernel(place, mine, theirs, message_one, near_rest, solved_high, solved_low):
    alpha_rows, beta_rows = leaf_rows(place, mine, theirs)
    near = jnp.where(place[0] == 0, 1, 0)
    tiles_a, meet_a = alpha_rows(3)
    tiles_b, meet_b = beta_rows(2)
    system = (meet_a + meet_b)[:, :FACE]
    right = split(tiles_a + tiles_b)
    tiles_a, meet_a = alpha_rows(near)
    tiles_b, meet_b = beta_rows(near)
    direct = jnp.concatenate([tiles_a, tiles_b], axis=0)
    coupling = split(jnp.concatenate([meet_a, meet_b], axis=0)[:, :FACE])
    inverse = split(spd_inverse(system, panel=8))
    solved = split(product(inverse, right))
    merged = direct - product(coupling, solved)
    message_one[0:128, :] = merged[:, 0:128]
    message_one[128:256, :] = merged[:, 128:256]
    message_one[256:CUT, :] = merged[0 : CUT - 256, 256:384]
    near_rest[...] = merged[CUT - 256 :, 256:384]
    solved_high[...], solved_low[...] = solved


def face_kernel(place, mine, theirs, near_rest, solved_high, solved_low, message_two, link):
    alpha_rows, beta_rows = leaf_rows(place, mine, theirs)
    direct, coupling = either(place[1] == 0, beta_rows(3), alpha_rows(2))
    solved = solved_high[...], solved_low[...]
    merged = direct - product(split(coupling[:, :FACE]), solved)
    message_two[0 : 384 - CUT, :] = near_rest[...]
    message_two[384 - CUT : 448 - CUT, :] = merged[:, 128:256]
    message_two[448 - CUT :, :] = merged[:, 256:384]
    link[...] = merged[:, 0:128]


def second_kernel(
    place, own, received, mine, theirs, solved_high, solved_low, inverse_high, inverse_low, outer, direct, coupling
):
    alpha_rows, beta_rows = leaf_rows(place, mine, theirs)
    third, lead = place[1], place[2]
    far = jnp.where(place[0] == 0, 0, 1)
    direct[0:64, :], coupling[0:64, :] = alpha_rows(far)
    at_two = alpha_rows(2)
    at_far = beta_rows(far)
    at_three = beta_rows(3)
    direct[64:128, :], coupling[64:128, :] = either(third == 0, at_two, at_far)
    direct[128:192, :], coupling[128:192, :] = either(third == 0, at_far, at_three)
    spot = pl.ds(pl.multiple_of(lead * 96, 32), 96)
    solved = solved_high[...], solved_low[...]
    outer[...] = direct[spot, :] - product(split(coupling[spot, :][:, :FACE]), solved)
    inverse_high[...], inverse_low[...] = split(spd_inverse(own[0:128, :] + received[0:128, :]))


def assemble(alpha, beta):
    rows = (alpha or beta)[0].shape[0]
    left = halves((rows, 128))
    blank = jnp.zeros((rows, 128), F32)
    if alpha is None:
        tiles = (
            jnp.where(left, 0.0, turn(beta[0])),
            blank,
            jnp.where(left, 0.0, beta[0]),
            beta[1],
        )
        return jnp.concatenate(tiles, axis=1)
    turned = turn(alpha[1])
    middle = jnp.where(left, turn(alpha[0]), turned)
    if beta is None:
        tiles = jnp.where(left, alpha[0], 0.0), middle, jnp.where(left, turned, 0.0), blank
        return jnp.concatenate(tiles, axis=1)
    tiles = (
        jnp.where(left, alpha[0], turn(beta[0])),
        middle,
        jnp.where(left, turned, beta[0]),
        beta[1],
    )
    return jnp.concatenate(tiles, axis=1)


def exchange_kernel(
    place,
    own_one,
    own_two,
    received_one,
    received_two,
    link,
    inverse_high,
    inverse_low,
    message_one,
    message_two,
    right_high,
    right_low,
):
    is_alpha = place[0] == 0

    def both(mine, other):
        return jnp.where(is_alpha, mine, other), jnp.where(is_alpha, other, mine)

    one = both(own_one[128:256, :], received_one[128:256, :])
    two = both(third_tile(own_one, own_two), third_tile(received_one, received_two))
    right = split(assemble((one[0], two[0]), (one[1], two[1])))
    span = slice(384 - CUT, 448 - CUT)
    face = both(own_two[span, :], received_two[span, :])
    span = slice(448 - CUT, 512 - CUT)
    back = both(own_two[span, :], received_two[span, :])
    direct = jnp.concatenate(
        [assemble((face[0], back[0]), None), assemble(None, (face[1], back[1]))], axis=0
    )
    mine = link[...]
    other = jnp.transpose(received_one[128:256, :])[0:FACE]
    coupling = jnp.concatenate(
        [jnp.where(is_alpha, mine, other), jnp.where(is_alpha, other, mine)], axis=0
    )
    solved = split(product(split(coupling), (inverse_high[...], inverse_low[...])))
    merged = direct - product(solved, right)
    for i in range(2):
        message_one[128 * i : 128 * i + 128, :] = merged[:, 128 * i : 128 * i + 128]
    message_one[256:CUT, :] = merged[0 : CUT - 256, 256:384]
    message_two[0 : 384 - CUT, :] = merged[CUT - 256 :, 256:384]
    message_two[384 - CUT :, :] = merged[:, 384:512]
    right_high[...], right_low[...] = right


def rest_columns(one, two):
    return jnp.concatenate(
        [one[128:256, :], third_tile(one, two), two[384 - CUT :, :]], axis=1
    )


def third_kernel(
    place,
    own_one,
    own_two,
    received,
    outer,
    inverse_high,
    inverse_low,
    right_high,
    right_low,
    half,
    solved_high,
    solved_low,
):
    mine = outer[:, 128:256], outer[:, 256:384]
    direct = jnp.where(place[0] == 0, assemble(mine, None), assemble(None, mine))
    solved = split(product(split(outer[:, 0:128]), (inverse_high[...], inverse_low[...])))
    merged = direct - product(solved, (right_high[...], right_low[...]))
    coupling = split(merged[:, 0:128])
    right = split(rest_columns(own_one, own_two))
    inverse = split(spd_inverse(own_one[0:128, :] + received[0:128, :]))
    solved = split(product(coupling, inverse))
    half[...] = merged[:, 128:512] - product(solved, right)
    solved_high[...], solved_low[...] = solved


def last_kernel(place, half, received_one, received_two, solved_high, solved_low, out):
    third = place[1]
    width = 6 * FACE
    mine = pl.multiple_of(third * width, 128)
    other = pl.multiple_of((1 - third) * width, 128)
    out[:, pl.ds(mine, width)] = half[...]
    solved = solved_high[...], solved_low[...]
    out[:, pl.ds(other, width)] = -product(solved, split(rest_columns(received_one, received_two)))


def shapes(*sizes):
    return [jax.ShapeDtypeStruct(size, F32) for size in sizes]


def pair(*size):
    return [jax.ShapeDtypeStruct(size, BF16)] * 2


def run(kernel, out_shape, *operands, scalars=1, **options):
    smem = pl.BlockSpec(memory_space=pltpu.SMEM)
    vmem = pl.BlockSpec(memory_space=pltpu.VMEM)
    return pl.pallas_call(
        kernel,
        out_shape=out_shape,
        in_specs=[smem] * scalars + [vmem] * (len(operands) - scalars),
        out_specs=[vmem] * len(out_shape),
        compiler_params=pltpu.CompilerParams(vmem_limit_bytes=32 * 1024 * 1024),
        **options,
    )(*operands)


def body(leaf_maps, leaf_operator, region_eps, wave_sq, region_labels, build_flags):
    across = lax.axis_index("bx") % 2
    upward = lax.axis_index("by")
    place = jnp.stack([across, upward // 2 % 2, upward % 2]).astype(jnp.int32)
    size = leaf_operator.shape[0]
    facts = sum(
        lax.pad(x.reshape((1, 1)).astype(F32), jnp.float32(0), ((i, 7 - i, 0), (0, 127, 0)))
        for i, x in enumerate((build_flags, region_labels, wave_sq))
    )
    mine = pl.pallas_call(
        build_kernel,
        out_shape=jax.ShapeDtypeStruct((LEAF, LEAF), F32),
        in_specs=[pl.BlockSpec(memory_space=pltpu.VMEM)]
        + [pl.BlockSpec(memory_space=pltpu.HBM)] * 3,
        out_specs=pl.BlockSpec(memory_space=pltpu.VMEM),
        scratch_shapes=[
            pltpu.VMEM(region_eps.shape, F32),
            pltpu.VMEM((128, size), F32),
            pltpu.VMEM((size - LEAF - 128, size), F32),
            pltpu.VMEM((LEAF, size), F32),
            pltpu.SemaphoreType.DMA((5,)),
        ],
        compiler_params=pltpu.CompilerParams(vmem_limit_bytes=32 * 1024 * 1024),
        name="leaf_build",
    )(
        facts,
        *(
            pltpu.with_memory_space_constraint(x, pltpu.HBM)
            for x in (leaf_maps[0, 0], leaf_operator, region_eps)
        ),
    )
    theirs = swapped(mine, "by", 0)
    one, near_rest, *solved = run(
        first_kernel,
        shapes((CUT, 128), (384 - CUT, 128)) + pair(FACE, 6 * FACE),
        place,
        mine,
        theirs,
        name="first_merge",
    )
    received_one = swapped(one, "bx", 0)
    two, link = run(
        face_kernel,
        shapes((512 - CUT, 128), (FACE, 128)),
        place,
        mine,
        theirs,
        near_rest,
        *solved,
        name="first_faces",
    )
    received_two = swapped(two, "bx", 0)
    *inverse, outer = run(
        second_kernel,
        pair(128, 128) + shapes((96, 6 * FACE)),
        place,
        one,
        received_one,
        mine,
        theirs,
        *solved,
        scratch_shapes=[pltpu.VMEM((192, 6 * FACE), F32), pltpu.VMEM((192, 128), F32)],
        name="second_inverse",
    )
    one, two, *right = run(
        exchange_kernel,
        shapes((CUT, 128), (512 - CUT, 128)) + pair(128, 8 * FACE),
        place,
        one,
        two,
        received_one,
        received_two,
        link,
        *inverse,
        name="second_merge",
    )
    received_one = swapped(one, "by", 1)
    received_two = swapped(two, "by", 1)
    half, *solved = run(
        third_kernel,
        shapes((96, 6 * FACE)) + pair(96, 128),
        place,
        one,
        two,
        received_one,
        outer,
        *inverse,
        *right,
        name="third_inverse",
    )
    (result,) = run(
        last_kernel,
        shapes((96, 12 * FACE)),
        place,
        half,
        received_one,
        received_two,
        *solved,
        name="third_merge",
    )
    return result.reshape((1, 1, 96, 12 * FACE))


def solution(mesh):
    placed = (
        P(("freq", "bx"), "by", None, None),
        P(),
        P(),
        P("freq"),
        P("bx", "by"),
        P("bx", "by"),
    )
    return jax.shard_map(
        body,
        mesh=mesh,
        in_specs=placed,
        out_specs=P(("freq", "bx"), "by", None, None),
        check_vma=False,
    )
```

```python
import jax
import jax.numpy as jnp
from jax import lax
from jax.experimental import pallas as pl
from jax.experimental.pallas import tpu as pltpu
from jax.sharding import PartitionSpec as P

FACE = 64
LEAF = 4 * FACE
CUT = 128
F32 = jnp.float32
BF16 = jnp.bfloat16


LONG = pl.CostEstimate(flops=10**10, bytes_accessed=10**8, transcendentals=10**6)


def swapped(shard, axis, stride):
    return lax.ppermute(shard, axis, [(i, i ^ 1 << stride) for i in range(lax.axis_size(axis))])


def split(x):
    high = x.astype(BF16)
    return high, (x - high.astype(F32)).astype(BF16)


def thirds(x):
    high = x.astype(BF16).astype(F32)
    rest = x - high
    middle = rest.astype(BF16).astype(F32)
    return high, middle, (rest - middle).astype(BF16).astype(F32)


def dot(a, b):
    return jnp.dot(a, b, preferred_element_type=F32)


def product(a, b):
    (a_high, a_low), (b_high, b_low) = a, b
    depth = a_high.shape[1]
    if depth % 128 and depth != FACE:
        return dot(a_high, b_high) + (dot(a_high, b_low) + dot(a_low, b_high))
    twice = dot(
        jnp.concatenate([a_high, a_low], axis=1), jnp.concatenate([b_high, b_high], axis=0)
    )
    return twice + dot(a_high, b_low)


def spd_inverse(matrix, panel=4, look=2):
    size = matrix.shape[0]
    shape = (8, size)
    count = size // 8
    tiles = [matrix[8 * g : 8 * g + 8] for g in range(count)]
    lane = lax.broadcasted_iota(jnp.int32, shape, 1)
    sub = lax.broadcasted_iota(jnp.int32, shape, 0)

    def column(tile, c):
        return jnp.broadcast_to(tile[:, c : c + 1], shape)

    def row(tile, r):
        return jnp.broadcast_to(tile[r : r + 1, :], shape)

    def inside(start, stop):
        return (lane >= start) & (lane < stop)

    def bounds(columns):
        return [pl.reciprocal(row(columns[j], j), approx=True) for j in range(8)]

    even = sub % 2 == 0
    pivot = [column(tiles[0], j) for j in range(8)]
    bound = bounds(pivot)
    for start in range(0, count, panel):
        stop = min(start + panel, count)
        last = min(stop + look, count)
        outside = [*range(last, count), *range(start)]
        if outside:
            strip = jnp.concatenate([tiles[g] for g in outside], axis=0)[:, 8 * start : 8 * stop]
            high, middle, low = thirds(strip)
            left = jnp.concatenate([high, high, middle, high, low, middle], axis=1).astype(BF16)
        for k in range(start, stop):
            first = 8 * k
            block = inside(first, first + 8)
            rows = jnp.where(block, (lane - first == sub).astype(F32), tiles[k])
            ahead = k + 1 < count
            if ahead:
                after = jnp.where(block, 0.0, tiles[k + 1])
                side = [column(tiles[k + 1], first + j) for j in range(8)]
                coming = [column(tiles[k + 1], first + 8 + j) for j in range(8)]
                bound_ahead = bounds(coming)
            scale, cross = jnp.zeros(shape, F32), jnp.zeros(shape, F32)
            for p in range(0, 8, 2):
                q = p + 1
                one, two = pivot[p] * bound[p], pivot[q] * bound[q]
                a, b_one, b_two, c = row(one, p), row(one, q), row(two, p), row(two, q)
                inverse = pl.reciprocal(a * c - b_one * b_two, approx=True)
                pair = (sub == p) | (sub == q)
                factor_p = jnp.where(pair, 0.0, one * c - two * b_one) * inverse
                factor_q = jnp.where(pair, 0.0, two * a - one * b_two) * inverse
                row_p, row_q = row(rows, p), row(rows, q)
                if ahead:
                    edge_p, edge_q = side[p], side[q]
                    one, two = edge_p * bound[p], edge_q * bound[q]
                    ahead_p = (one * c - two * b_one) * inverse
                    ahead_q = (two * a - one * b_two) * inverse
                    for j in range(8):
                        coming[j] = coming[j] - (ahead_p * row(edge_p, j) + ahead_q * row(edge_q, j))
                    after = after - (ahead_p * row_p + ahead_q * row_q)
                for j in range(p + 2, 8):
                    at_p, at_q = row(pivot[j], p), row(pivot[j], q)
                    pivot[j] = pivot[j] - (factor_p * at_p + factor_q * at_q)
                    if ahead:
                        side[j] = side[j] - (ahead_p * at_p + ahead_q * at_q)
                rows = rows - (factor_p * row_p + factor_q * row_q)
                inverse_p, inverse_q = inverse * bound[p], inverse * bound[q]
                scale = jnp.where(sub == p, c * inverse_p, jnp.where(sub == q, a * inverse_q, scale))
                cross = jnp.where(pair, b_one * inverse_q, cross)
            other = jnp.where(even, pltpu.roll(rows, 7, 0), pltpu.roll(rows, 1, 0))
            rows = rows * scale - other * cross
            picked = [row(rows, j) for j in range(8)]
            for g in range(start, last):
                if g == k:
                    tiles[g] = rows
                elif g == k + 1:
                    tiles[g] = after
                else:
                    new = jnp.where(block, 0.0, tiles[g])
                    for j in range(8):
                        new = new - column(tiles[g], first + j) * picked[j]
                    tiles[g] = new
            if ahead:
                pivot, bound = coming, bound_ahead
        if outside:
            right = jnp.concatenate(tiles[start:stop], axis=0)
            high, middle, low = thirds(right)
            right = jnp.concatenate([high, middle, high, low, high, middle], axis=0).astype(BF16)
            update = dot(left, right)
            block = inside(8 * start, 8 * stop)
            for i, g in enumerate(outside):
                tiles[g] = jnp.where(block, 0.0, tiles[g]) - update[8 * i : 8 * i + 8]
    return jnp.concatenate(tiles, axis=0)


def build_kernel(facts, given, operator, table_at, out, table, one, two, edge, sems):
    size = operator.shape[0]
    middle = LEAF + 128
    copies = [
        pltpu.make_async_copy(source, target, sems.at[i])
        for i, (source, target) in enumerate(
            (
                (operator.at[pl.ds(LEAF, 128)], one),
                (table_at, table),
                (operator.at[pl.ds(middle, size - middle)], two),
                (operator.at[pl.ds(0, LEAF)], edge),
                (given, out),
            )
        )
    ]
    for copy in copies:
        copy.start()
    flag = jnp.max(facts[0:1, :])
    for copy in copies[:2]:
        copy.wait()

    @pl.when(flag <= 0.0)
    def _():
        for copy in copies[2:]:
            copy.wait()

    @pl.when(flag > 0.0)
    def _():
        labels = lax.broadcasted_iota(jnp.int32, table.shape, 0).astype(F32)
        picked = jnp.where(labels == facts[1:2, 0:1], table[...], 0.0)
        shift = facts[2:3, 0:1] * jnp.sum(picked, axis=0, keepdims=True)
        border, near, far = slice(0, LEAF), slice(LEAF, middle), slice(middle, size)

        def shifted(ref, span):
            block = ref[:, span]
            ids = lax.broadcasted_iota(jnp.int32, block.shape, 0)
            diagonal = ids == lax.broadcasted_iota(jnp.int32, block.shape, 1)
            return block - jnp.where(diagonal, shift[:, span], 0.0)

        right = split(one[:, border]), split(one[:, far])
        inverse = split(spd_inverse(shifted(one, near)))
        for copy in copies[2:]:
            copy.wait()
        left = split(two[:, near])
        solved_far = split(product(inverse, right[1]))
        inner = shifted(two, far) - product(left, solved_far)
        solved = split(product(inverse, right[0]))
        coupled = split(two[:, border] - product(left, solved))
        left = split(edge[:, near])
        merged = shifted(edge, border) - product(left, solved)
        across = split(edge[:, far] - product(left, solved_far))
        inverse = split(spd_inverse(inner))
        solved = split(product(inverse, coupled))
        out[...] = merged - product(across, solved)


def halves(shape):
    return lax.broadcasted_iota(jnp.int32, shape, 1) < FACE


def turn(tile):
    return pltpu.roll(tile, FACE, 1)


def leaf_rows(place, mine, theirs):
    across, third, lead = place[0], place[1], place[2]
    is_alpha = lead == 0
    left = halves((FACE, 128))

    def load(alpha, block, tile):
        spot = pl.ds(pl.multiple_of(block * FACE, FACE), FACE)
        span = slice(128 * tile, 128 * tile + 128)
        own = is_alpha if alpha else jnp.logical_not(is_alpha)
        return jnp.where(own, mine[spot, span], theirs[spot, span])

    def alpha_rows(block):
        sides = load(True, block, 0)
        ends = load(True, block, 1)
        sides = jnp.where(across == 0, turn(sides), sides)
        tiles = (
            jnp.where(left, sides, 0.0),
            jnp.where(left, jnp.where(third == 0, 0.0, ends), sides),
            jnp.where(left & (third == 0), ends, 0.0),
        )
        return jnp.concatenate(tiles, axis=1), turn(ends)

    def beta_rows(block):
        sides = load(False, block, 0)
        ends = load(False, block, 1)
        other = turn(sides)
        near_far = jnp.where(across == 0, other, sides)
        far_near = jnp.where(across == 0, sides, other)
        flipped = turn(ends)
        tiles = (
            jnp.where(left, 0.0, far_near),
            jnp.where(left & (third == 0), flipped, 0.0),
            jnp.where(
                third == 0,
                jnp.where(left, 0.0, near_far),
                jnp.where(left, far_near, ends),
            ),
        )
        return jnp.concatenate(tiles, axis=1), ends

    return alpha_rows, beta_rows


def either(flag, one, other):
    return [jnp.where(flag, x, y) for x, y in zip(one, other)]


def stacked(one, two, start, stop):
    parts = []
    if start < CUT:
        parts.append(one[start : min(stop, CUT), :])
    if stop > CUT:
        parts.append(two[max(start, CUT) - CUT : stop - CUT, :])
    return jnp.concatenate(parts, axis=0)


def stack(one, two, start, value):
    stop = start + value.shape[0]
    if start < CUT:
        one[start : min(stop, CUT), :] = value[: CUT - start]
    if stop > CUT:
        two[max(start, CUT) - CUT : stop - CUT, :] = value[max(CUT - start, 0) :]


def first_kernel(place, mine, theirs, message_one, near_rest, solved_high, solved_low):
    alpha_rows, beta_rows = leaf_rows(place, mine, theirs)
    near = jnp.where(place[0] == 0, 1, 0)
    tiles_a, meet_a = alpha_rows(3)
    tiles_b, meet_b = beta_rows(2)
    system = (meet_a + meet_b)[:, :FACE]
    right = split(tiles_a + tiles_b)
    tiles_a, meet_a = alpha_rows(near)
    tiles_b, meet_b = beta_rows(near)
    direct = jnp.concatenate([tiles_a, tiles_b], axis=0)
    coupling = split(jnp.concatenate([meet_a, meet_b], axis=0)[:, :FACE])
    inverse = split(spd_inverse(system, panel=8))
    solved = split(product(inverse, right))
    merged = direct - product(coupling, solved)
    for i in range(3):
        stack(message_one, near_rest, 128 * i, merged[:, 128 * i : 128 * i + 128])
    solved_high[...], solved_low[...] = solved


def face_kernel(place, mine, theirs, near_rest, solved_high, solved_low, message_two, link):
    alpha_rows, beta_rows = leaf_rows(place, mine, theirs)
    direct, coupling = either(place[1] == 0, beta_rows(3), alpha_rows(2))
    solved = solved_high[...], solved_low[...]
    merged = direct - product(split(coupling[:, :FACE]), solved)
    message_two[0 : 384 - CUT, :] = near_rest[...]
    message_two[384 - CUT : 448 - CUT, :] = merged[:, 128:256]
    message_two[448 - CUT :, :] = merged[:, 256:384]
    link[...] = merged[:, 0:128]


def second_kernel(
    place, own, received, mine, theirs, solved_high, solved_low, inverse_high, inverse_low, outer, direct, coupling
):
    alpha_rows, beta_rows = leaf_rows(place, mine, theirs)
    third, lead = place[1], place[2]
    far = jnp.where(place[0] == 0, 0, 1)
    direct[0:64, :], coupling[0:64, :] = alpha_rows(far)
    at_two = alpha_rows(2)
    at_far = beta_rows(far)
    at_three = beta_rows(3)
    direct[64:128, :], coupling[64:128, :] = either(third == 0, at_two, at_far)
    direct[128:192, :], coupling[128:192, :] = either(third == 0, at_far, at_three)
    spot = pl.ds(pl.multiple_of(lead * 96, 32), 96)
    solved = solved_high[...], solved_low[...]
    outer[...] = direct[spot, :] - product(split(coupling[spot, :][:, :FACE]), solved)
    inverse_high[...], inverse_low[...] = split(spd_inverse(own[0:128, :] + received[0:128, :]))


def assemble(alpha, beta):
    rows = (alpha or beta)[0].shape[0]
    left = halves((rows, 128))
    blank = jnp.zeros((rows, 128), F32)
    if alpha is None:
        tiles = (
            jnp.where(left, 0.0, turn(beta[0])),
            blank,
            jnp.where(left, 0.0, beta[0]),
            beta[1],
        )
        return jnp.concatenate(tiles, axis=1)
    turned = turn(alpha[1])
    middle = jnp.where(left, turn(alpha[0]), turned)
    if beta is None:
        tiles = jnp.where(left, alpha[0], 0.0), middle, jnp.where(left, turned, 0.0), blank
        return jnp.concatenate(tiles, axis=1)
    tiles = (
        jnp.where(left, alpha[0], turn(beta[0])),
        middle,
        jnp.where(left, turned, beta[0]),
        beta[1],
    )
    return jnp.concatenate(tiles, axis=1)


def exchange_kernel(
    place,
    own_one,
    own_two,
    received_one,
    received_two,
    link,
    inverse_high,
    inverse_low,
    message_one,
    message_two,
    right_high,
    right_low,
):
    is_alpha = place[0] == 0

    def both(mine, other):
        return jnp.where(is_alpha, mine, other), jnp.where(is_alpha, other, mine)

    def part(start, stop):
        return both(stacked(own_one, own_two, start, stop), stacked(received_one, received_two, start, stop))

    one, two = part(128, 256), part(256, 384)
    right = split(assemble((one[0], two[0]), (one[1], two[1])))
    face, back = part(384, 448), part(448, 512)
    direct = jnp.concatenate(
        [assemble((face[0], back[0]), None), assemble(None, (face[1], back[1]))], axis=0
    )
    mine = link[...]
    other = jnp.transpose(stacked(received_one, received_two, 128, 256))[0:FACE]
    coupling = jnp.concatenate(
        [jnp.where(is_alpha, mine, other), jnp.where(is_alpha, other, mine)], axis=0
    )
    solved = split(product(split(coupling), (inverse_high[...], inverse_low[...])))
    merged = direct - product(solved, right)
    for i in range(4):
        stack(message_one, message_two, 128 * i, merged[:, 128 * i : 128 * i + 128])
    right_high[...], right_low[...] = right


def rest_columns(one, two):
    return jnp.concatenate(
        [stacked(one, two, 128 * i, 128 * i + 128) for i in range(1, 4)], axis=1
    )


def third_kernel(
    place,
    own_one,
    own_two,
    received,
    outer,
    inverse_high,
    inverse_low,
    right_high,
    right_low,
    half,
    solved_high,
    solved_low,
):
    mine = outer[:, 128:256], outer[:, 256:384]
    direct = jnp.where(place[0] == 0, assemble(mine, None), assemble(None, mine))
    solved = split(product(split(outer[:, 0:128]), (inverse_high[...], inverse_low[...])))
    merged = direct - product(solved, (right_high[...], right_low[...]))
    coupling = split(merged[:, 0:128])
    right = split(rest_columns(own_one, own_two))
    inverse = split(spd_inverse(own_one[0:128, :] + received[0:128, :]))
    solved = split(product(coupling, inverse))
    half[...] = merged[:, 128:512] - product(solved, right)
    solved_high[...], solved_low[...] = solved


def last_kernel(place, half, received_one, received_two, solved_high, solved_low, out):
    third = place[1]
    width = 6 * FACE
    mine = pl.multiple_of(third * width, 128)
    other = pl.multiple_of((1 - third) * width, 128)
    out[:, pl.ds(mine, width)] = half[...]
    solved = solved_high[...], solved_low[...]
    out[:, pl.ds(other, width)] = -product(solved, split(rest_columns(received_one, received_two)))


def shapes(*sizes):
    return [jax.ShapeDtypeStruct(size, F32) for size in sizes]


def pair(*size):
    return [jax.ShapeDtypeStruct(size, BF16)] * 2


def run(kernel, out_shape, *operands, scalars=1, **options):
    smem = pl.BlockSpec(memory_space=pltpu.SMEM)
    vmem = pl.BlockSpec(memory_space=pltpu.VMEM)
    return pl.pallas_call(
        kernel,
        out_shape=out_shape,
        in_specs=[smem] * scalars + [vmem] * (len(operands) - scalars),
        out_specs=[vmem] * len(out_shape),
        compiler_params=pltpu.CompilerParams(vmem_limit_bytes=32 * 1024 * 1024),
        **options,
    )(*operands)


def body(leaf_maps, leaf_operator, region_eps, wave_sq, region_labels, build_flags):
    across = lax.axis_index("bx") % 2
    upward = lax.axis_index("by")
    place = jnp.stack([across, upward // 2 % 2, upward % 2]).astype(jnp.int32)
    size = leaf_operator.shape[0]
    facts = sum(
        lax.pad(x.reshape((1, 1)).astype(F32), jnp.float32(0), ((i, 7 - i, 0), (0, 127, 0)))
        for i, x in enumerate((build_flags, region_labels, wave_sq))
    )
    mine = pl.pallas_call(
        build_kernel,
        out_shape=jax.ShapeDtypeStruct((LEAF, LEAF), F32),
        in_specs=[pl.BlockSpec(memory_space=pltpu.VMEM)]
        + [pl.BlockSpec(memory_space=pltpu.HBM)] * 3,
        out_specs=pl.BlockSpec(memory_space=pltpu.VMEM),
        scratch_shapes=[
            pltpu.VMEM(region_eps.shape, F32),
            pltpu.VMEM((128, size), F32),
            pltpu.VMEM((size - LEAF - 128, size), F32),
            pltpu.VMEM((LEAF, size), F32),
            pltpu.SemaphoreType.DMA((5,)),
        ],
        compiler_params=pltpu.CompilerParams(vmem_limit_bytes=32 * 1024 * 1024),
        name="leaf_build",
    )(
        facts,
        *(
            pltpu.with_memory_space_constraint(x, pltpu.HBM)
            for x in (leaf_maps[0, 0], leaf_operator, region_eps)
        ),
    )
    theirs = swapped(mine, "by", 0)
    one, near_rest, *solved = run(
        first_kernel,
        shapes((CUT, 128), (384 - CUT, 128)) + pair(FACE, 6 * FACE),
        place,
        mine,
        theirs,
        name="first_merge",
    )
    received_one = swapped(one, "bx", 0)
    two, link = run(
        face_kernel,
        shapes((512 - CUT, 128), (FACE, 128)),
        place,
        mine,
        theirs,
        near_rest,
        *solved,
        name="first_faces",
    )
    received_two = swapped(two, "bx", 0)
    *inverse, outer = run(
        second_kernel,
        pair(128, 128) + shapes((96, 6 * FACE)),
        place,
        one,
        received_one,
        mine,
        theirs,
        *solved,
        scratch_shapes=[pltpu.VMEM((192, 6 * FACE), F32), pltpu.VMEM((192, 128), F32)],
        cost_estimate=LONG,
        name="second_inverse",
    )
    one, two, *right = run(
        exchange_kernel,
        shapes((CUT, 128), (512 - CUT, 128)) + pair(128, 8 * FACE),
        place,
        one,
        two,
        received_one,
        received_two,
        link,
        *inverse,
        name="second_merge",
    )
    received_one = swapped(one, "by", 1)
    received_two = swapped(two, "by", 1)
    half, *solved = run(
        third_kernel,
        shapes((96, 6 * FACE)) + pair(96, 128),
        place,
        one,
        two,
        received_one,
        outer,
        *inverse,
        *right,
        cost_estimate=LONG,
        name="third_inverse",
    )
    (result,) = run(
        last_kernel,
        shapes((96, 12 * FACE)),
        place,
        half,
        received_one,
        received_two,
        *solved,
        name="third_merge",
    )
    return result.reshape((1, 1, 96, 12 * FACE))


def solution(mesh):
    placed = (
        P(("freq", "bx"), "by", None, None),
        P(),
        P(),
        P("freq"),
        P("bx", "by"),
        P("bx", "by"),
    )
    return jax.shard_map(
        body,
        mesh=mesh,
        in_specs=placed,
        out_specs=P(("freq", "bx"), "by", None, None),
        check_vma=False,
    )
```

```python
import jax
import jax.numpy as jnp
from jax import lax
from jax.experimental import pallas as pl
from jax.experimental.pallas import tpu as pltpu
from jax.sharding import PartitionSpec as P

FACE = 64
LEAF = 4 * FACE
CUT = 128
F32 = jnp.float32
BF16 = jnp.bfloat16


LONG = pl.CostEstimate(flops=10**10, bytes_accessed=10**8, transcendentals=10**6)


def swapped(shard, axis, stride):
    return lax.ppermute(shard, axis, [(i, i ^ 1 << stride) for i in range(lax.axis_size(axis))])


def split(x):
    high = x.astype(BF16)
    return high, (x - high.astype(F32)).astype(BF16)


def thirds(x):
    high = x.astype(BF16).astype(F32)
    rest = x - high
    middle = rest.astype(BF16).astype(F32)
    return high, middle, (rest - middle).astype(BF16).astype(F32)


def dot(a, b):
    return jnp.dot(a, b, preferred_element_type=F32)


def product(a, b):
    (a_high, a_low), (b_high, b_low) = a, b
    depth = a_high.shape[1]
    if depth % 128 and depth != FACE:
        return dot(a_high, b_high) + (dot(a_high, b_low) + dot(a_low, b_high))
    twice = dot(
        jnp.concatenate([a_high, a_low], axis=1), jnp.concatenate([b_high, b_high], axis=0)
    )
    return twice + dot(a_high, b_low)


def spd_inverse(matrix, panel=4, look=2, half=4):
    size = matrix.shape[0]
    shape = (8, size)
    count = size // 8
    tiles = [matrix[8 * g : 8 * g + 8] for g in range(count)]
    lane = lax.broadcasted_iota(jnp.int32, shape, 1)
    sub = lax.broadcasted_iota(jnp.int32, shape, 0)

    def column(tile, c):
        return jnp.broadcast_to(tile[:, c : c + 1], shape)

    def row(tile, r):
        return jnp.broadcast_to(tile[r : r + 1, :], shape)

    def inside(start, stop):
        return (lane >= start) & (lane < stop)

    pivot = [column(tiles[0], j) for j in range(8)]
    for start in range(0, count, panel):
        stop = min(start + panel, count)
        last = min(stop + look, count)
        outside = [*range(last, count), *range(start)]
        if outside:
            strip = jnp.concatenate([tiles[g] for g in outside], axis=0)[:, 8 * start : 8 * stop]
            high, middle, low = thirds(strip)
            left = jnp.concatenate([high, high, middle, high, low, middle], axis=1).astype(BF16)
        for k in range(start, stop):
            first = 8 * k
            block = inside(first, first + 8)
            rows = jnp.where(block, (lane - first == sub).astype(F32), tiles[k])
            ahead = k + 1 < count
            if ahead:
                after = jnp.where(block, 0.0, tiles[k + 1])
                side = [column(tiles[k + 1], first + j) for j in range(8)]
            scale = None
            for p in range(8):
                inverse = pl.reciprocal(row(pivot[p], p), approx=True)
                factor = jnp.where(sub == p, 0.0, pivot[p]) * inverse
                picked = row(rows, p)
                if ahead:
                    edge = side[p]
                    factor_ahead = edge * inverse
                    if p == half:
                        coming = [column(after, first + 8 + j) for j in range(8)]
                    if p >= half:
                        for j in range(8):
                            coming[j] = coming[j] - factor_ahead * row(edge, j)
                    after = after - factor_ahead * picked
                for j in range(p + 1, 8):
                    element = row(pivot[j], p)
                    pivot[j] = pivot[j] - factor * element
                    if ahead:
                        side[j] = side[j] - factor_ahead * element
                rows = rows - factor * picked
                scale = inverse if scale is None else jnp.where(sub == p, inverse, scale)
            rows = rows * scale
            picked = [row(rows, j) for j in range(8)]
            for g in range(start, last):
                if g == k:
                    tiles[g] = rows
                elif g == k + 1:
                    tiles[g] = after
                else:
                    new = jnp.where(block, 0.0, tiles[g])
                    for j in range(8):
                        new = new - column(tiles[g], first + j) * picked[j]
                    tiles[g] = new
            if ahead:
                pivot = coming
        if outside:
            right = jnp.concatenate(tiles[start:stop], axis=0)
            high, middle, low = thirds(right)
            right = jnp.concatenate([high, middle, high, low, high, middle], axis=0).astype(BF16)
            update = dot(left, right)
            block = inside(8 * start, 8 * stop)
            for i, g in enumerate(outside):
                tiles[g] = jnp.where(block, 0.0, tiles[g]) - update[8 * i : 8 * i + 8]
    return jnp.concatenate(tiles, axis=0)


def build_kernel(facts, given, operator, table_at, out, table, one, two, edge, sems):
    size = operator.shape[0]
    middle = LEAF + 128
    copies = [
        pltpu.make_async_copy(source, target, sems.at[i])
        for i, (source, target) in enumerate(
            (
                (operator.at[pl.ds(LEAF, 128)], one),
                (table_at, table),
                (operator.at[pl.ds(middle, size - middle)], two),
                (operator.at[pl.ds(0, LEAF)], edge),
                (given, out),
            )
        )
    ]
    for copy in copies:
        copy.start()
    flag = jnp.max(facts[0:1, :])
    for copy in copies[:2]:
        copy.wait()

    @pl.when(flag <= 0.0)
    def _():
        for copy in copies[2:]:
            copy.wait()

    @pl.when(flag > 0.0)
    def _():
        labels = lax.broadcasted_iota(jnp.int32, table.shape, 0).astype(F32)
        picked = jnp.where(labels == facts[1:2, 0:1], table[...], 0.0)
        shift = facts[2:3, 0:1] * jnp.sum(picked, axis=0, keepdims=True)
        border, near, far = slice(0, LEAF), slice(LEAF, middle), slice(middle, size)

        def shifted(ref, span):
            block = ref[:, span]
            ids = lax.broadcasted_iota(jnp.int32, block.shape, 0)
            diagonal = ids == lax.broadcasted_iota(jnp.int32, block.shape, 1)
            return block - jnp.where(diagonal, shift[:, span], 0.0)

        right = split(one[:, border]), split(one[:, far])
        inverse = split(spd_inverse(shifted(one, near)))
        for copy in copies[2:]:
            copy.wait()
        left = split(two[:, near])
        solved_far = split(product(inverse, right[1]))
        inner = shifted(two, far) - product(left, solved_far)
        solved = split(product(inverse, right[0]))
        coupled = split(two[:, border] - product(left, solved))
        left = split(edge[:, near])
        merged = shifted(edge, border) - product(left, solved)
        across = split(edge[:, far] - product(left, solved_far))
        inverse = split(spd_inverse(inner))
        solved = split(product(inverse, coupled))
        out[...] = merged - product(across, solved)


def halves(shape):
    return lax.broadcasted_iota(jnp.int32, shape, 1) < FACE


def turn(tile):
    return pltpu.roll(tile, FACE, 1)


def leaf_rows(place, mine, theirs):
    across, third, lead = place[0], place[1], place[2]
    is_alpha = lead == 0
    left = halves((FACE, 128))

    def load(alpha, block, tile):
        spot = pl.ds(pl.multiple_of(block * FACE, FACE), FACE)
        span = slice(128 * tile, 128 * tile + 128)
        own = is_alpha if alpha else jnp.logical_not(is_alpha)
        return jnp.where(own, mine[spot, span], theirs[spot, span])

    def alpha_rows(block):
        sides = load(True, block, 0)
        ends = load(True, block, 1)
        sides = jnp.where(across == 0, turn(sides), sides)
        tiles = (
            jnp.where(left, sides, 0.0),
            jnp.where(left, jnp.where(third == 0, 0.0, ends), sides),
            jnp.where(left & (third == 0), ends, 0.0),
        )
        return jnp.concatenate(tiles, axis=1), turn(ends)

    def beta_rows(block):
        sides = load(False, block, 0)
        ends = load(False, block, 1)
        other = turn(sides)
        near_far = jnp.where(across == 0, other, sides)
        far_near = jnp.where(across == 0, sides, other)
        flipped = turn(ends)
        tiles = (
            jnp.where(left, 0.0, far_near),
            jnp.where(left & (third == 0), flipped, 0.0),
            jnp.where(
                third == 0,
                jnp.where(left, 0.0, near_far),
                jnp.where(left, far_near, ends),
            ),
        )
        return jnp.concatenate(tiles, axis=1), ends

    return alpha_rows, beta_rows


def either(flag, one, other):
    return [jnp.where(flag, x, y) for x, y in zip(one, other)]


def stacked(one, two, start, stop):
    parts = []
    if start < CUT:
        parts.append(one[start : min(stop, CUT), :])
    if stop > CUT:
        parts.append(two[max(start, CUT) - CUT : stop - CUT, :])
    return jnp.concatenate(parts, axis=0)


def stack(one, two, start, value):
    stop = start + value.shape[0]
    if start < CUT:
        one[start : min(stop, CUT), :] = value[: CUT - start]
    if stop > CUT:
        two[max(start, CUT) - CUT : stop - CUT, :] = value[max(CUT - start, 0) :]


def first_kernel(place, mine, theirs, message_one, near_rest, solved_high, solved_low):
    alpha_rows, beta_rows = leaf_rows(place, mine, theirs)
    near = jnp.where(place[0] == 0, 1, 0)
    tiles_a, meet_a = alpha_rows(3)
    tiles_b, meet_b = beta_rows(2)
    system = (meet_a + meet_b)[:, :FACE]
    right = split(tiles_a + tiles_b)
    tiles_a, meet_a = alpha_rows(near)
    tiles_b, meet_b = beta_rows(near)
    direct = jnp.concatenate([tiles_a, tiles_b], axis=0)
    coupling = split(jnp.concatenate([meet_a, meet_b], axis=0)[:, :FACE])
    inverse = split(spd_inverse(system, panel=8))
    solved = split(product(inverse, right))
    merged = direct - product(coupling, solved)
    for i in range(3):
        stack(message_one, near_rest, 128 * i, merged[:, 128 * i : 128 * i + 128])
    solved_high[...], solved_low[...] = solved


def face_kernel(place, mine, theirs, near_rest, solved_high, solved_low, message_two, link):
    alpha_rows, beta_rows = leaf_rows(place, mine, theirs)
    direct, coupling = either(place[1] == 0, beta_rows(3), alpha_rows(2))
    solved = solved_high[...], solved_low[...]
    merged = direct - product(split(coupling[:, :FACE]), solved)
    message_two[0 : 384 - CUT, :] = near_rest[...]
    message_two[384 - CUT : 448 - CUT, :] = merged[:, 128:256]
    message_two[448 - CUT :, :] = merged[:, 256:384]
    link[...] = merged[:, 0:128]


def second_kernel(
    place, own, received, mine, theirs, solved_high, solved_low, inverse_high, inverse_low, outer, direct, coupling
):
    alpha_rows, beta_rows = leaf_rows(place, mine, theirs)
    third, lead = place[1], place[2]
    far = jnp.where(place[0] == 0, 0, 1)
    direct[0:64, :], coupling[0:64, :] = alpha_rows(far)
    at_two = alpha_rows(2)
    at_far = beta_rows(far)
    at_three = beta_rows(3)
    direct[64:128, :], coupling[64:128, :] = either(third == 0, at_two, at_far)
    direct[128:192, :], coupling[128:192, :] = either(third == 0, at_far, at_three)
    spot = pl.ds(pl.multiple_of(lead * 96, 32), 96)
    solved = solved_high[...], solved_low[...]
    outer[...] = direct[spot, :] - product(split(coupling[spot, :][:, :FACE]), solved)
    inverse_high[...], inverse_low[...] = split(spd_inverse(own[0:128, :] + received[0:128, :]))


def assemble(alpha, beta):
    rows = (alpha or beta)[0].shape[0]
    left = halves((rows, 128))
    blank = jnp.zeros((rows, 128), F32)
    if alpha is None:
        tiles = (
            jnp.where(left, 0.0, turn(beta[0])),
            blank,
            jnp.where(left, 0.0, beta[0]),
            beta[1],
        )
        return jnp.concatenate(tiles, axis=1)
    turned = turn(alpha[1])
    middle = jnp.where(left, turn(alpha[0]), turned)
    if beta is None:
        tiles = jnp.where(left, alpha[0], 0.0), middle, jnp.where(left, turned, 0.0), blank
        return jnp.concatenate(tiles, axis=1)
    tiles = (
        jnp.where(left, alpha[0], turn(beta[0])),
        middle,
        jnp.where(left, turned, beta[0]),
        beta[1],
    )
    return jnp.concatenate(tiles, axis=1)


def exchange_kernel(
    place,
    own_one,
    own_two,
    received_one,
    received_two,
    link,
    inverse_high,
    inverse_low,
    message_one,
    message_two,
    right_high,
    right_low,
):
    is_alpha = place[0] == 0

    def both(mine, other):
        return jnp.where(is_alpha, mine, other), jnp.where(is_alpha, other, mine)

    def part(start, stop):
        return both(stacked(own_one, own_two, start, stop), stacked(received_one, received_two, start, stop))

    one, two = part(128, 256), part(256, 384)
    right = split(assemble((one[0], two[0]), (one[1], two[1])))
    face, back = part(384, 448), part(448, 512)
    direct = jnp.concatenate(
        [assemble((face[0], back[0]), None), assemble(None, (face[1], back[1]))], axis=0
    )
    mine = link[...]
    other = jnp.transpose(stacked(received_one, received_two, 128, 256))[0:FACE]
    coupling = jnp.concatenate(
        [jnp.where(is_alpha, mine, other), jnp.where(is_alpha, other, mine)], axis=0
    )
    solved = split(product(split(coupling), (inverse_high[...], inverse_low[...])))
    merged = direct - product(solved, right)
    for i in range(4):
        stack(message_one, message_two, 128 * i, merged[:, 128 * i : 128 * i + 128])
    right_high[...], right_low[...] = right


def rest_columns(one, two):
    return jnp.concatenate(
        [stacked(one, two, 128 * i, 128 * i + 128) for i in range(1, 4)], axis=1
    )


def third_kernel(
    place,
    own_one,
    own_two,
    received,
    outer,
    inverse_high,
    inverse_low,
    right_high,
    right_low,
    half,
    solved_high,
    solved_low,
):
    mine = outer[:, 128:256], outer[:, 256:384]
    direct = jnp.where(place[0] == 0, assemble(mine, None), assemble(None, mine))
    solved = split(product(split(outer[:, 0:128]), (inverse_high[...], inverse_low[...])))
    merged = direct - product(solved, (right_high[...], right_low[...]))
    coupling = split(merged[:, 0:128])
    right = split(rest_columns(own_one, own_two))
    inverse = split(spd_inverse(own_one[0:128, :] + received[0:128, :]))
    solved = split(product(coupling, inverse))
    half[...] = merged[:, 128:512] - product(solved, right)
    solved_high[...], solved_low[...] = solved


def last_kernel(place, half, received_one, received_two, solved_high, solved_low, out):
    third = place[1]
    width = 6 * FACE
    mine = pl.multiple_of(third * width, 128)
    other = pl.multiple_of((1 - third) * width, 128)
    out[:, pl.ds(mine, width)] = half[...]
    solved = solved_high[...], solved_low[...]
    out[:, pl.ds(other, width)] = -product(solved, split(rest_columns(received_one, received_two)))


def shapes(*sizes):
    return [jax.ShapeDtypeStruct(size, F32) for size in sizes]


def pair(*size):
    return [jax.ShapeDtypeStruct(size, BF16)] * 2


def run(kernel, out_shape, *operands, scalars=1, **options):
    smem = pl.BlockSpec(memory_space=pltpu.SMEM)
    vmem = pl.BlockSpec(memory_space=pltpu.VMEM)
    return pl.pallas_call(
        kernel,
        out_shape=out_shape,
        in_specs=[smem] * scalars + [vmem] * (len(operands) - scalars),
        out_specs=[vmem] * len(out_shape),
        compiler_params=pltpu.CompilerParams(vmem_limit_bytes=32 * 1024 * 1024),
        **options,
    )(*operands)


def body(leaf_maps, leaf_operator, region_eps, wave_sq, region_labels, build_flags):
    across = lax.axis_index("bx") % 2
    upward = lax.axis_index("by")
    place = jnp.stack([across, upward // 2 % 2, upward % 2]).astype(jnp.int32)
    size = leaf_operator.shape[0]
    facts = sum(
        lax.pad(x.reshape((1, 1)).astype(F32), jnp.float32(0), ((i, 7 - i, 0), (0, 127, 0)))
        for i, x in enumerate((build_flags, region_labels, wave_sq))
    )
    mine = pl.pallas_call(
        build_kernel,
        out_shape=jax.ShapeDtypeStruct((LEAF, LEAF), F32),
        in_specs=[pl.BlockSpec(memory_space=pltpu.VMEM)]
        + [pl.BlockSpec(memory_space=pltpu.HBM)] * 3,
        out_specs=pl.BlockSpec(memory_space=pltpu.VMEM),
        scratch_shapes=[
            pltpu.VMEM(region_eps.shape, F32),
            pltpu.VMEM((128, size), F32),
            pltpu.VMEM((size - LEAF - 128, size), F32),
            pltpu.VMEM((LEAF, size), F32),
            pltpu.SemaphoreType.DMA((5,)),
        ],
        compiler_params=pltpu.CompilerParams(vmem_limit_bytes=32 * 1024 * 1024),
        name="leaf_build",
    )(
        facts,
        *(
            pltpu.with_memory_space_constraint(x, pltpu.HBM)
            for x in (leaf_maps[0, 0], leaf_operator, region_eps)
        ),
    )
    theirs = swapped(mine, "by", 0)
    one, near_rest, *solved = run(
        first_kernel,
        shapes((CUT, 128), (384 - CUT, 128)) + pair(FACE, 6 * FACE),
        place,
        mine,
        theirs,
        name="first_merge",
    )
    received_one = swapped(one, "bx", 0)
    two, link = run(
        face_kernel,
        shapes((512 - CUT, 128), (FACE, 128)),
        place,
        mine,
        theirs,
        near_rest,
        *solved,
        name="first_faces",
    )
    received_two = swapped(two, "bx", 0)
    *inverse, outer = run(
        second_kernel,
        pair(128, 128) + shapes((96, 6 * FACE)),
        place,
        one,
        received_one,
        mine,
        theirs,
        *solved,
        scratch_shapes=[pltpu.VMEM((192, 6 * FACE), F32), pltpu.VMEM((192, 128), F32)],
        cost_estimate=LONG,
        name="second_inverse",
    )
    one, two, *right = run(
        exchange_kernel,
        shapes((CUT, 128), (512 - CUT, 128)) + pair(128, 8 * FACE),
        place,
        one,
        two,
        received_one,
        received_two,
        link,
        *inverse,
        name="second_merge",
    )
    received_one = swapped(one, "by", 1)
    received_two = swapped(two, "by", 1)
    half, *solved = run(
        third_kernel,
        shapes((96, 6 * FACE)) + pair(96, 128),
        place,
        one,
        two,
        received_one,
        outer,
        *inverse,
        *right,
        cost_estimate=LONG,
        name="third_inverse",
    )
    (result,) = run(
        last_kernel,
        shapes((96, 12 * FACE)),
        place,
        half,
        received_one,
        received_two,
        *solved,
        name="third_merge",
    )
    return result.reshape((1, 1, 96, 12 * FACE))


def solution(mesh):
    placed = (
        P(("freq", "bx"), "by", None, None),
        P(),
        P(),
        P("freq"),
        P("bx", "by"),
        P("bx", "by"),
    )
    return jax.shard_map(
        body,
        mesh=mesh,
        in_specs=placed,
        out_specs=P(("freq", "bx"), "by", None, None),
        check_vma=False,
    )
```

```python
import jax
import jax.numpy as jnp
from jax import lax
from jax.experimental import pallas as pl
from jax.experimental.pallas import tpu as pltpu
from jax.sharding import PartitionSpec as P

FACE = 64
LEAF = 4 * FACE
CUT = 128
F32 = jnp.float32
BF16 = jnp.bfloat16


LONG = pl.CostEstimate(flops=10**10, bytes_accessed=10**8, transcendentals=10**6)


def swapped(shard, axis, stride):
    return lax.ppermute(shard, axis, [(i, i ^ 1 << stride) for i in range(lax.axis_size(axis))])


def gathered(shard, axis, stride):
    size = lax.axis_size(axis)
    groups = [[i, i | 1 << stride] for i in range(size) if not i >> stride & 1]
    return lax.all_gather(shard, axis, axis_index_groups=groups)


def split(x):
    high = x.astype(BF16)
    return high, (x - high.astype(F32)).astype(BF16)


def thirds(x):
    high = x.astype(BF16).astype(F32)
    rest = x - high
    middle = rest.astype(BF16).astype(F32)
    return high, middle, (rest - middle).astype(BF16).astype(F32)


def dot(a, b):
    return jnp.dot(a, b, preferred_element_type=F32)


def product(a, b):
    (a_high, a_low), (b_high, b_low) = a, b
    depth = a_high.shape[1]
    if depth % 128 and depth != FACE:
        return dot(a_high, b_high) + (dot(a_high, b_low) + dot(a_low, b_high))
    twice = dot(
        jnp.concatenate([a_high, a_low], axis=1), jnp.concatenate([b_high, b_high], axis=0)
    )
    return twice + dot(a_high, b_low)


def spd_inverse(matrix, panel=4, look=2, half=4):
    size = matrix.shape[0]
    shape = (8, size)
    count = size // 8
    tiles = [matrix[8 * g : 8 * g + 8] for g in range(count)]
    lane = lax.broadcasted_iota(jnp.int32, shape, 1)
    sub = lax.broadcasted_iota(jnp.int32, shape, 0)

    def column(tile, c):
        return jnp.broadcast_to(tile[:, c : c + 1], shape)

    def row(tile, r):
        return jnp.broadcast_to(tile[r : r + 1, :], shape)

    def inside(start, stop):
        return (lane >= start) & (lane < stop)

    pivot = [column(tiles[0], j) for j in range(8)]
    for start in range(0, count, panel):
        stop = min(start + panel, count)
        last = min(stop + look, count)
        outside = [*range(last, count), *range(start)]
        if outside:
            strip = jnp.concatenate([tiles[g] for g in outside], axis=0)[:, 8 * start : 8 * stop]
            high, middle, low = thirds(strip)
            left = jnp.concatenate([high, high, middle, high, low, middle], axis=1).astype(BF16)
        for k in range(start, stop):
            first = 8 * k
            block = inside(first, first + 8)
            rows = jnp.where(block, (lane - first == sub).astype(F32), tiles[k])
            ahead = k + 1 < count
            if ahead:
                after = jnp.where(block, 0.0, tiles[k + 1])
                side = [column(tiles[k + 1], first + j) for j in range(8)]
            scale = None
            for p in range(8):
                inverse = pl.reciprocal(row(pivot[p], p), approx=True)
                factor = jnp.where(sub == p, 0.0, pivot[p]) * inverse
                picked = row(rows, p)
                if ahead:
                    edge = side[p]
                    factor_ahead = edge * inverse
                    if p == half:
                        coming = [column(after, first + 8 + j) for j in range(8)]
                    if p >= half:
                        for j in range(8):
                            coming[j] = coming[j] - factor_ahead * row(edge, j)
                    after = after - factor_ahead * picked
                for j in range(p + 1, 8):
                    element = row(pivot[j], p)
                    pivot[j] = pivot[j] - factor * element
                    if ahead:
                        side[j] = side[j] - factor_ahead * element
                rows = rows - factor * picked
                scale = inverse if scale is None else jnp.where(sub == p, inverse, scale)
            rows = rows * scale
            picked = [row(rows, j) for j in range(8)]
            for g in range(start, last):
                if g == k:
                    tiles[g] = rows
                elif g == k + 1:
                    tiles[g] = after
                else:
                    new = jnp.where(block, 0.0, tiles[g])
                    for j in range(8):
                        new = new - column(tiles[g], first + j) * picked[j]
                    tiles[g] = new
            if ahead:
                pivot = coming
        if outside:
            right = jnp.concatenate(tiles[start:stop], axis=0)
            high, middle, low = thirds(right)
            right = jnp.concatenate([high, middle, high, low, high, middle], axis=0).astype(BF16)
            update = dot(left, right)
            block = inside(8 * start, 8 * stop)
            for i, g in enumerate(outside):
                tiles[g] = jnp.where(block, 0.0, tiles[g]) - update[8 * i : 8 * i + 8]
    return jnp.concatenate(tiles, axis=0)


def build_kernel(facts, given, operator, table_at, out, table, one, two, edge, sems):
    size = operator.shape[0]
    middle = LEAF + 128
    copies = [
        pltpu.make_async_copy(source, target, sems.at[i])
        for i, (source, target) in enumerate(
            (
                (operator.at[pl.ds(LEAF, 128)], one),
                (table_at, table),
                (operator.at[pl.ds(middle, size - middle)], two),
                (operator.at[pl.ds(0, LEAF)], edge),
                (given, out),
            )
        )
    ]
    for copy in copies:
        copy.start()
    flag = jnp.max(facts[0:1, :])
    for copy in copies[:2]:
        copy.wait()

    @pl.when(flag <= 0.0)
    def _():
        for copy in copies[2:]:
            copy.wait()

    @pl.when(flag > 0.0)
    def _():
        labels = lax.broadcasted_iota(jnp.int32, table.shape, 0).astype(F32)
        picked = jnp.where(labels == facts[1:2, 0:1], table[...], 0.0)
        shift = facts[2:3, 0:1] * jnp.sum(picked, axis=0, keepdims=True)
        border, near, far = slice(0, LEAF), slice(LEAF, middle), slice(middle, size)

        def shifted(ref, span):
            block = ref[:, span]
            ids = lax.broadcasted_iota(jnp.int32, block.shape, 0)
            diagonal = ids == lax.broadcasted_iota(jnp.int32, block.shape, 1)
            return block - jnp.where(diagonal, shift[:, span], 0.0)

        right = split(one[:, border]), split(one[:, far])
        inverse = split(spd_inverse(shifted(one, near)))
        for copy in copies[2:]:
            copy.wait()
        left = split(two[:, near])
        solved_far = split(product(inverse, right[1]))
        inner = shifted(two, far) - product(left, solved_far)
        solved = split(product(inverse, right[0]))
        coupled = split(two[:, border] - product(left, solved))
        left = split(edge[:, near])
        merged = shifted(edge, border) - product(left, solved)
        across = split(edge[:, far] - product(left, solved_far))
        inverse = split(spd_inverse(inner))
        solved = split(product(inverse, coupled))
        out[...] = merged - product(across, solved)


def halves(shape):
    return lax.broadcasted_iota(jnp.int32, shape, 1) < FACE


def turn(tile):
    return pltpu.roll(tile, FACE, 1)


def leaf_rows(place, mine, theirs):
    across, third, lead = place[0], place[1], place[2]
    is_alpha = lead == 0
    left = halves((FACE, 128))

    def load(alpha, block, tile):
        spot = pl.ds(pl.multiple_of(block * FACE, FACE), FACE)
        span = slice(128 * tile, 128 * tile + 128)
        own = is_alpha if alpha else jnp.logical_not(is_alpha)
        return jnp.where(own, mine[spot, span], theirs[spot, span])

    def alpha_rows(block):
        sides = load(True, block, 0)
        ends = load(True, block, 1)
        sides = jnp.where(across == 0, turn(sides), sides)
        tiles = (
            jnp.where(left, sides, 0.0),
            jnp.where(left, jnp.where(third == 0, 0.0, ends), sides),
            jnp.where(left & (third == 0), ends, 0.0),
        )
        return jnp.concatenate(tiles, axis=1), turn(ends)

    def beta_rows(block):
        sides = load(False, block, 0)
        ends = load(False, block, 1)
        other = turn(sides)
        near_far = jnp.where(across == 0, other, sides)
        far_near = jnp.where(across == 0, sides, other)
        flipped = turn(ends)
        tiles = (
            jnp.where(left, 0.0, far_near),
            jnp.where(left & (third == 0), flipped, 0.0),
            jnp.where(
                third == 0,
                jnp.where(left, 0.0, near_far),
                jnp.where(left, far_near, ends),
            ),
        )
        return jnp.concatenate(tiles, axis=1), ends

    return alpha_rows, beta_rows


def either(flag, one, other):
    return [jnp.where(flag, x, y) for x, y in zip(one, other)]


def stacked(one, two, start, stop):
    parts = []
    if start < CUT:
        parts.append(one[start : min(stop, CUT), :])
    if stop > CUT:
        parts.append(two[max(start, CUT) - CUT : stop - CUT, :])
    return jnp.concatenate(parts, axis=0)


def stack(one, two, start, value):
    stop = start + value.shape[0]
    if start < CUT:
        one[start : min(stop, CUT), :] = value[: CUT - start]
    if stop > CUT:
        two[max(start, CUT) - CUT : stop - CUT, :] = value[max(CUT - start, 0) :]


def first_kernel(place, mine, theirs, message_one, near_rest, solved_high, solved_low):
    alpha_rows, beta_rows = leaf_rows(place, mine, theirs)
    near = jnp.where(place[0] == 0, 1, 0)
    tiles_a, meet_a = alpha_rows(3)
    tiles_b, meet_b = beta_rows(2)
    system = (meet_a + meet_b)[:, :FACE]
    right = split(tiles_a + tiles_b)
    tiles_a, meet_a = alpha_rows(near)
    tiles_b, meet_b = beta_rows(near)
    direct = jnp.concatenate([tiles_a, tiles_b], axis=0)
    coupling = split(jnp.concatenate([meet_a, meet_b], axis=0)[:, :FACE])
    inverse = split(spd_inverse(system, panel=8))
    solved = split(product(inverse, right))
    merged = direct - product(coupling, solved)
    for i in range(3):
        stack(message_one, near_rest, 128 * i, merged[:, 128 * i : 128 * i + 128])
    solved_high[...], solved_low[...] = solved


def face_kernel(place, mine, theirs, near_rest, solved_high, solved_low, message_two, link):
    alpha_rows, beta_rows = leaf_rows(place, mine, theirs)
    direct, coupling = either(place[1] == 0, beta_rows(3), alpha_rows(2))
    solved = solved_high[...], solved_low[...]
    merged = direct - product(split(coupling[:, :FACE]), solved)
    message_two[0 : 384 - CUT, :] = near_rest[...]
    message_two[384 - CUT : 448 - CUT, :] = merged[:, 128:256]
    message_two[448 - CUT :, :] = merged[:, 256:384]
    link[...] = merged[:, 0:128]


def second_kernel(
    place, own, received, mine, theirs, solved_high, solved_low, inverse_high, inverse_low, outer, direct, coupling
):
    alpha_rows, beta_rows = leaf_rows(place, mine, theirs)
    third, lead = place[1], place[2]
    far = jnp.where(place[0] == 0, 0, 1)
    direct[0:64, :], coupling[0:64, :] = alpha_rows(far)
    at_two = alpha_rows(2)
    at_far = beta_rows(far)
    at_three = beta_rows(3)
    direct[64:128, :], coupling[64:128, :] = either(third == 0, at_two, at_far)
    direct[128:192, :], coupling[128:192, :] = either(third == 0, at_far, at_three)
    spot = pl.ds(pl.multiple_of(lead * 96, 32), 96)
    solved = solved_high[...], solved_low[...]
    outer[...] = direct[spot, :] - product(split(coupling[spot, :][:, :FACE]), solved)
    inverse_high[...], inverse_low[...] = split(spd_inverse(own[0:128, :] + received[0:128, :]))


def assemble(alpha, beta):
    rows = (alpha or beta)[0].shape[0]
    left = halves((rows, 128))
    blank = jnp.zeros((rows, 128), F32)
    if alpha is None:
        tiles = (
            jnp.where(left, 0.0, turn(beta[0])),
            blank,
            jnp.where(left, 0.0, beta[0]),
            beta[1],
        )
        return jnp.concatenate(tiles, axis=1)
    turned = turn(alpha[1])
    middle = jnp.where(left, turn(alpha[0]), turned)
    if beta is None:
        tiles = jnp.where(left, alpha[0], 0.0), middle, jnp.where(left, turned, 0.0), blank
        return jnp.concatenate(tiles, axis=1)
    tiles = (
        jnp.where(left, alpha[0], turn(beta[0])),
        middle,
        jnp.where(left, turned, beta[0]),
        beta[1],
    )
    return jnp.concatenate(tiles, axis=1)


def exchange_kernel(
    place,
    own_one,
    own_two,
    received_one,
    gathered_two,
    link,
    inverse_high,
    inverse_low,
    message_one,
    message_two,
    right_high,
    right_low,
):
    is_alpha = place[0] == 0
    received_two = gathered_two.at[1 - place[0]]

    def both(mine, other):
        return jnp.where(is_alpha, mine, other), jnp.where(is_alpha, other, mine)

    def part(start, stop):
        return both(stacked(own_one, own_two, start, stop), stacked(received_one, received_two, start, stop))

    one, two = part(128, 256), part(256, 384)
    right = split(assemble((one[0], two[0]), (one[1], two[1])))
    face, back = part(384, 448), part(448, 512)
    direct = jnp.concatenate(
        [assemble((face[0], back[0]), None), assemble(None, (face[1], back[1]))], axis=0
    )
    mine = link[...]
    other = jnp.transpose(stacked(received_one, received_two, 128, 256))[0:FACE]
    coupling = jnp.concatenate(
        [jnp.where(is_alpha, mine, other), jnp.where(is_alpha, other, mine)], axis=0
    )
    solved = split(product(split(coupling), (inverse_high[...], inverse_low[...])))
    merged = direct - product(solved, right)
    for i in range(4):
        stack(message_one, message_two, 128 * i, merged[:, 128 * i : 128 * i + 128])
    right_high[...], right_low[...] = right


def rest_columns(one, two):
    return jnp.concatenate(
        [stacked(one, two, 128 * i, 128 * i + 128) for i in range(1, 4)], axis=1
    )


def third_kernel(
    place,
    own_one,
    own_two,
    received,
    outer,
    inverse_high,
    inverse_low,
    right_high,
    right_low,
    half,
    solved_high,
    solved_low,
):
    mine = outer[:, 128:256], outer[:, 256:384]
    direct = jnp.where(place[0] == 0, assemble(mine, None), assemble(None, mine))
    solved = split(product(split(outer[:, 0:128]), (inverse_high[...], inverse_low[...])))
    merged = direct - product(solved, (right_high[...], right_low[...]))
    coupling = split(merged[:, 0:128])
    right = split(rest_columns(own_one, own_two))
    inverse = split(spd_inverse(own_one[0:128, :] + received[0:128, :]))
    solved = split(product(coupling, inverse))
    half[...] = merged[:, 128:512] - product(solved, right)
    solved_high[...], solved_low[...] = solved


def last_kernel(place, half, received_one, gathered_two, solved_high, solved_low, out):
    third = place[1]
    received_two = gathered_two.at[1 - third]
    width = 6 * FACE
    mine = pl.multiple_of(third * width, 128)
    other = pl.multiple_of((1 - third) * width, 128)
    out[:, pl.ds(mine, width)] = half[...]
    solved = solved_high[...], solved_low[...]
    out[:, pl.ds(other, width)] = -product(solved, split(rest_columns(received_one, received_two)))


def shapes(*sizes):
    return [jax.ShapeDtypeStruct(size, F32) for size in sizes]


def pair(*size):
    return [jax.ShapeDtypeStruct(size, BF16)] * 2


def run(kernel, out_shape, *operands, scalars=1, **options):
    smem = pl.BlockSpec(memory_space=pltpu.SMEM)
    vmem = pl.BlockSpec(memory_space=pltpu.VMEM)
    return pl.pallas_call(
        kernel,
        out_shape=out_shape,
        in_specs=[smem] * scalars + [vmem] * (len(operands) - scalars),
        out_specs=[vmem] * len(out_shape),
        compiler_params=pltpu.CompilerParams(vmem_limit_bytes=32 * 1024 * 1024),
        **options,
    )(*operands)


def body(leaf_maps, leaf_operator, region_eps, wave_sq, region_labels, build_flags):
    across = lax.axis_index("bx") % 2
    upward = lax.axis_index("by")
    place = jnp.stack([across, upward // 2 % 2, upward % 2]).astype(jnp.int32)
    size = leaf_operator.shape[0]
    facts = sum(
        lax.pad(x.reshape((1, 1)).astype(F32), jnp.float32(0), ((i, 7 - i, 0), (0, 127, 0)))
        for i, x in enumerate((build_flags, region_labels, wave_sq))
    )
    mine = pl.pallas_call(
        build_kernel,
        out_shape=jax.ShapeDtypeStruct((LEAF, LEAF), F32),
        in_specs=[pl.BlockSpec(memory_space=pltpu.VMEM)]
        + [pl.BlockSpec(memory_space=pltpu.HBM)] * 3,
        out_specs=pl.BlockSpec(memory_space=pltpu.VMEM),
        scratch_shapes=[
            pltpu.VMEM(region_eps.shape, F32),
            pltpu.VMEM((128, size), F32),
            pltpu.VMEM((size - LEAF - 128, size), F32),
            pltpu.VMEM((LEAF, size), F32),
            pltpu.SemaphoreType.DMA((5,)),
        ],
        compiler_params=pltpu.CompilerParams(vmem_limit_bytes=32 * 1024 * 1024),
        name="leaf_build",
    )(
        facts,
        *(
            pltpu.with_memory_space_constraint(x, pltpu.HBM)
            for x in (leaf_maps[0, 0], leaf_operator, region_eps)
        ),
    )
    theirs = swapped(mine, "by", 0)
    one, near_rest, *solved = run(
        first_kernel,
        shapes((CUT, 128), (384 - CUT, 128)) + pair(FACE, 6 * FACE),
        place,
        mine,
        theirs,
        name="first_merge",
    )
    received_one = swapped(one, "bx", 0)
    two, link = run(
        face_kernel,
        shapes((512 - CUT, 128), (FACE, 128)),
        place,
        mine,
        theirs,
        near_rest,
        *solved,
        name="first_faces",
    )
    received_two = gathered(two, "bx", 0)
    *inverse, outer = run(
        second_kernel,
        pair(128, 128) + shapes((96, 6 * FACE)),
        place,
        one,
        received_one,
        mine,
        theirs,
        *solved,
        scratch_shapes=[pltpu.VMEM((192, 6 * FACE), F32), pltpu.VMEM((192, 128), F32)],
        cost_estimate=LONG,
        name="second_inverse",
    )
    one, two, *right = run(
        exchange_kernel,
        shapes((CUT, 128), (512 - CUT, 128)) + pair(128, 8 * FACE),
        place,
        one,
        two,
        received_one,
        received_two,
        link,
        *inverse,
        name="second_merge",
    )
    received_one = swapped(one, "by", 1)
    received_two = gathered(two, "by", 1)
    half, *solved = run(
        third_kernel,
        shapes((96, 6 * FACE)) + pair(96, 128),
        place,
        one,
        two,
        received_one,
        outer,
        *inverse,
        *right,
        cost_estimate=LONG,
        name="third_inverse",
    )
    (result,) = run(
        last_kernel,
        shapes((96, 12 * FACE)),
        place,
        half,
        received_one,
        received_two,
        *solved,
        name="third_merge",
    )
    return result.reshape((1, 1, 96, 12 * FACE))


def solution(mesh):
    placed = (
        P(("freq", "bx"), "by", None, None),
        P(),
        P(),
        P("freq"),
        P("bx", "by"),
        P("bx", "by"),
    )
    return jax.shard_map(
        body,
        mesh=mesh,
        in_specs=placed,
        out_specs=P(("freq", "bx"), "by", None, None),
        check_vma=False,
    )
```

```python
import jax
import jax.numpy as jnp
from jax import lax
from jax.experimental import pallas as pl
from jax.experimental.pallas import tpu as pltpu
from jax.sharding import PartitionSpec as P

FACE = 64
LEAF = 4 * FACE
CUT = 176
F32 = jnp.float32
BF16 = jnp.bfloat16


LONG = pl.CostEstimate(flops=10**10, bytes_accessed=10**8, transcendentals=10**6)


def swapped(shard, axis, stride):
    return lax.ppermute(shard, axis, [(i, i ^ 1 << stride) for i in range(lax.axis_size(axis))])


def split(x):
    high = x.astype(BF16)
    return high, (x - high.astype(F32)).astype(BF16)


def thirds(x):
    high = x.astype(BF16).astype(F32)
    rest = x - high
    middle = rest.astype(BF16).astype(F32)
    return high, middle, (rest - middle).astype(BF16).astype(F32)


def dot(a, b):
    return jnp.dot(a, b, preferred_element_type=F32)


def product(a, b):
    (a_high, a_low), (b_high, b_low) = a, b
    depth = a_high.shape[1]
    if depth % 128 and depth != FACE:
        return dot(a_high, b_high) + (dot(a_high, b_low) + dot(a_low, b_high))
    twice = dot(
        jnp.concatenate([a_high, a_low], axis=1), jnp.concatenate([b_high, b_high], axis=0)
    )
    return twice + dot(a_high, b_low)


def spd_inverse(matrix, panel=4, look=2, half=4):
    size = matrix.shape[0]
    shape = (8, size)
    count = size // 8
    tiles = [matrix[8 * g : 8 * g + 8] for g in range(count)]
    lane = lax.broadcasted_iota(jnp.int32, shape, 1)
    sub = lax.broadcasted_iota(jnp.int32, shape, 0)

    def column(tile, c):
        return jnp.broadcast_to(tile[:, c : c + 1], shape)

    def row(tile, r):
        return jnp.broadcast_to(tile[r : r + 1, :], shape)

    def inside(start, stop):
        return (lane >= start) & (lane < stop)

    pivot = [column(tiles[0], j) for j in range(8)]
    for start in range(0, count, panel):
        stop = min(start + panel, count)
        last = min(stop + look, count)
        outside = [*range(last, count), *range(start)]
        if outside:
            strip = jnp.concatenate([tiles[g] for g in outside], axis=0)[:, 8 * start : 8 * stop]
            high, middle, low = thirds(strip)
            left = jnp.concatenate([high, high, middle, high, low, middle], axis=1).astype(BF16)
        for k in range(start, stop):
            first = 8 * k
            block = inside(first, first + 8)
            rows = jnp.where(block, (lane - first == sub).astype(F32), tiles[k])
            ahead = k + 1 < count
            if ahead:
                after = jnp.where(block, 0.0, tiles[k + 1])
                side = [column(tiles[k + 1], first + j) for j in range(8)]
            scale = None
            for p in range(8):
                inverse = pl.reciprocal(row(pivot[p], p), approx=True)
                factor = jnp.where(sub == p, 0.0, pivot[p]) * inverse
                picked = row(rows, p)
                if ahead:
                    edge = side[p]
                    factor_ahead = edge * inverse
                    if p == half:
                        coming = [column(after, first + 8 + j) for j in range(8)]
                    if p >= half:
                        for j in range(8):
                            coming[j] = coming[j] - factor_ahead * row(edge, j)
                    after = after - factor_ahead * picked
                for j in range(p + 1, 8):
                    element = row(pivot[j], p)
                    pivot[j] = pivot[j] - factor * element
                    if ahead:
                        side[j] = side[j] - factor_ahead * element
                rows = rows - factor * picked
                scale = inverse if scale is None else jnp.where(sub == p, inverse, scale)
            rows = rows * scale
            picked = [row(rows, j) for j in range(8)]
            for g in range(start, last):
                if g == k:
                    tiles[g] = rows
                elif g == k + 1:
                    tiles[g] = after
                else:
                    terms = [column(tiles[g], first + j) * picked[j] for j in range(8)]
                    while len(terms) > 1:
                        terms = [x + y for x, y in zip(terms[::2], terms[1::2])]
                    tiles[g] = jnp.where(block, 0.0, tiles[g]) - terms[0]
            if ahead:
                pivot = coming
        if outside:
            right = jnp.concatenate(tiles[start:stop], axis=0)
            high, middle, low = thirds(right)
            right = jnp.concatenate([high, middle, high, low, high, middle], axis=0).astype(BF16)
            update = dot(left, right)
            block = inside(8 * start, 8 * stop)
            for i, g in enumerate(outside):
                tiles[g] = jnp.where(block, 0.0, tiles[g]) - update[8 * i : 8 * i + 8]
    return jnp.concatenate(tiles, axis=0)


def build_kernel(facts, given, operator, table_at, out, table, one, two, edge, sems):
    size = operator.shape[0]
    middle = LEAF + 128
    copies = [
        pltpu.make_async_copy(source, target, sems.at[i])
        for i, (source, target) in enumerate(
            (
                (operator.at[pl.ds(LEAF, 128)], one),
                (table_at, table),
                (operator.at[pl.ds(middle, size - middle)], two),
                (operator.at[pl.ds(0, LEAF)], edge),
                (given, out),
            )
        )
    ]
    for copy in copies:
        copy.start()
    flag = jnp.max(facts[0:1, :])
    for copy in copies[:2]:
        copy.wait()

    @pl.when(flag <= 0.0)
    def _():
        for copy in copies[2:]:
            copy.wait()

    @pl.when(flag > 0.0)
    def _():
        labels = lax.broadcasted_iota(jnp.int32, table.shape, 0).astype(F32)
        picked = jnp.where(labels == facts[1:2, 0:1], table[...], 0.0)
        shift = facts[2:3, 0:1] * jnp.sum(picked, axis=0, keepdims=True)
        border, near, far = slice(0, LEAF), slice(LEAF, middle), slice(middle, size)

        def shifted(ref, span):
            block = ref[:, span]
            ids = lax.broadcasted_iota(jnp.int32, block.shape, 0)
            diagonal = ids == lax.broadcasted_iota(jnp.int32, block.shape, 1)
            return block - jnp.where(diagonal, shift[:, span], 0.0)

        right = split(one[:, border]), split(one[:, far])
        inverse = split(spd_inverse(shifted(one, near)))
        for copy in copies[2:]:
            copy.wait()
        left = split(two[:, near])
        solved_far = split(product(inverse, right[1]))
        inner = shifted(two, far) - product(left, solved_far)
        solved = split(product(inverse, right[0]))
        coupled = split(two[:, border] - product(left, solved))
        left = split(edge[:, near])
        merged = shifted(edge, border) - product(left, solved)
        across = split(edge[:, far] - product(left, solved_far))
        inverse = split(spd_inverse(inner))
        solved = split(product(inverse, coupled))
        out[...] = merged - product(across, solved)


def halves(shape):
    return lax.broadcasted_iota(jnp.int32, shape, 1) < FACE


def turn(tile):
    return pltpu.roll(tile, FACE, 1)


def leaf_rows(place, mine, theirs):
    across, third, lead = place[0], place[1], place[2]
    is_alpha = lead == 0
    left = halves((FACE, 128))

    def load(alpha, block, tile):
        spot = pl.ds(pl.multiple_of(block * FACE, FACE), FACE)
        span = slice(128 * tile, 128 * tile + 128)
        own = is_alpha if alpha else jnp.logical_not(is_alpha)
        return jnp.where(own, mine[spot, span], theirs[spot, span])

    def alpha_rows(block):
        sides = load(True, block, 0)
        ends = load(True, block, 1)
        sides = jnp.where(across == 0, turn(sides), sides)
        tiles = (
            jnp.where(left, sides, 0.0),
            jnp.where(left, jnp.where(third == 0, 0.0, ends), sides),
            jnp.where(left & (third == 0), ends, 0.0),
        )
        return jnp.concatenate(tiles, axis=1), turn(ends)

    def beta_rows(block):
        sides = load(False, block, 0)
        ends = load(False, block, 1)
        other = turn(sides)
        near_far = jnp.where(across == 0, other, sides)
        far_near = jnp.where(across == 0, sides, other)
        flipped = turn(ends)
        tiles = (
            jnp.where(left, 0.0, far_near),
            jnp.where(left & (third == 0), flipped, 0.0),
            jnp.where(
                third == 0,
                jnp.where(left, 0.0, near_far),
                jnp.where(left, far_near, ends),
            ),
        )
        return jnp.concatenate(tiles, axis=1), ends

    return alpha_rows, beta_rows


def either(flag, one, other):
    return [jnp.where(flag, x, y) for x, y in zip(one, other)]


def stacked(one, two, start, stop):
    parts = []
    if start < CUT:
        parts.append(one[start : min(stop, CUT), :])
    if stop > CUT:
        parts.append(two[max(start, CUT) - CUT : stop - CUT, :])
    return jnp.concatenate(parts, axis=0)


def stack(one, two, start, value):
    stop = start + value.shape[0]
    if start < CUT:
        one[start : min(stop, CUT), :] = value[: CUT - start]
    if stop > CUT:
        two[max(start, CUT) - CUT : stop - CUT, :] = value[max(CUT - start, 0) :]


def first_kernel(place, mine, theirs, message_one, message_two, link, solved_high, solved_low):
    alpha_rows, beta_rows = leaf_rows(place, mine, theirs)
    near = jnp.where(place[0] == 0, 1, 0)
    tiles_a, meet_a = alpha_rows(3)
    tiles_b, meet_b = beta_rows(2)
    system = (meet_a + meet_b)[:, :FACE]
    right = split(tiles_a + tiles_b)
    parts = [alpha_rows(near), beta_rows(near), either(place[1] == 0, beta_rows(3), alpha_rows(2))]
    direct = jnp.concatenate([tiles for tiles, _ in parts], axis=0)
    coupling = split(jnp.concatenate([meet for _, meet in parts], axis=0)[:, :FACE])
    inverse = split(spd_inverse(system, panel=8))
    solved = split(product(inverse, right))
    merged = direct - product(coupling, solved)
    for i in range(3):
        stack(message_one, message_two, 128 * i, merged[0:128, 128 * i : 128 * i + 128])
    stack(message_one, message_two, 384, merged[128:192, 128:256])
    stack(message_one, message_two, 448, merged[128:192, 256:384])
    link[...] = merged[128:192, 0:128]
    solved_high[...], solved_low[...] = solved


def second_kernel(
    place, own, received, mine, theirs, solved_high, solved_low, inverse_high, inverse_low, outer, direct, coupling
):
    alpha_rows, beta_rows = leaf_rows(place, mine, theirs)
    third, lead = place[1], place[2]
    far = jnp.where(place[0] == 0, 0, 1)
    direct[0:64, :], coupling[0:64, :] = alpha_rows(far)
    at_two = alpha_rows(2)
    at_far = beta_rows(far)
    at_three = beta_rows(3)
    direct[64:128, :], coupling[64:128, :] = either(third == 0, at_two, at_far)
    direct[128:192, :], coupling[128:192, :] = either(third == 0, at_far, at_three)
    spot = pl.ds(pl.multiple_of(lead * 96, 32), 96)
    solved = solved_high[...], solved_low[...]
    outer[...] = direct[spot, :] - product(split(coupling[spot, :][:, :FACE]), solved)
    inverse_high[...], inverse_low[...] = split(spd_inverse(own[0:128, :] + received[0:128, :]))


def assemble(alpha, beta):
    rows = (alpha or beta)[0].shape[0]
    left = halves((rows, 128))
    blank = jnp.zeros((rows, 128), F32)
    if alpha is None:
        tiles = (
            jnp.where(left, 0.0, turn(beta[0])),
            blank,
            jnp.where(left, 0.0, beta[0]),
            beta[1],
        )
        return jnp.concatenate(tiles, axis=1)
    turned = turn(alpha[1])
    middle = jnp.where(left, turn(alpha[0]), turned)
    if beta is None:
        tiles = jnp.where(left, alpha[0], 0.0), middle, jnp.where(left, turned, 0.0), blank
        return jnp.concatenate(tiles, axis=1)
    tiles = (
        jnp.where(left, alpha[0], turn(beta[0])),
        middle,
        jnp.where(left, turned, beta[0]),
        beta[1],
    )
    return jnp.concatenate(tiles, axis=1)


def exchange_kernel(
    place,
    own_one,
    own_two,
    received_one,
    received_two,
    link,
    inverse_high,
    inverse_low,
    message_one,
    message_two,
    right_high,
    right_low,
):
    is_alpha = place[0] == 0

    def both(mine, other):
        return jnp.where(is_alpha, mine, other), jnp.where(is_alpha, other, mine)

    def part(start, stop):
        return both(stacked(own_one, own_two, start, stop), stacked(received_one, received_two, start, stop))

    one, two = part(128, 256), part(256, 384)
    right = split(assemble((one[0], two[0]), (one[1], two[1])))
    face, back = part(384, 448), part(448, 512)
    direct = jnp.concatenate(
        [assemble((face[0], back[0]), None), assemble(None, (face[1], back[1]))], axis=0
    )
    mine = link[...]
    other = jnp.transpose(stacked(received_one, received_two, 128, 256))[0:FACE]
    coupling = jnp.concatenate(
        [jnp.where(is_alpha, mine, other), jnp.where(is_alpha, other, mine)], axis=0
    )
    solved = split(product(split(coupling), (inverse_high[...], inverse_low[...])))
    merged = direct - product(solved, right)
    for i in range(4):
        stack(message_one, message_two, 128 * i, merged[:, 128 * i : 128 * i + 128])
    right_high[...], right_low[...] = right


def rest_columns(one, two):
    return jnp.concatenate(
        [stacked(one, two, 128 * i, 128 * i + 128) for i in range(1, 4)], axis=1
    )


def outer_kernel(place, outer, inverse_high, inverse_low, right_high, right_low, rows):
    mine = outer[:, 128:256], outer[:, 256:384]
    direct = jnp.where(place[0] == 0, assemble(mine, None), assemble(None, mine))
    solved = split(product(split(outer[:, 0:128]), (inverse_high[...], inverse_low[...])))
    rows[...] = direct - product(solved, (right_high[...], right_low[...]))


def third_kernel(own_one, own_two, received, rows, half, solved_high, solved_low):
    coupling = split(rows[:, 0:128])
    right = split(rest_columns(own_one, own_two))
    inverse = split(spd_inverse(own_one[0:128, :] + received[0:128, :]))
    solved = split(product(coupling, inverse))
    half[...] = rows[:, 128:512] - product(solved, right)
    solved_high[...], solved_low[...] = solved


def last_kernel(place, half, received_one, received_two, solved_high, solved_low, out):
    third = place[1]
    width = 6 * FACE
    mine = pl.multiple_of(third * width, 128)
    other = pl.multiple_of((1 - third) * width, 128)
    out[:, pl.ds(mine, width)] = half[...]
    solved = solved_high[...], solved_low[...]
    out[:, pl.ds(other, width)] = -product(solved, split(rest_columns(received_one, received_two)))


def shapes(*sizes):
    return [jax.ShapeDtypeStruct(size, F32) for size in sizes]


def pair(*size):
    return [jax.ShapeDtypeStruct(size, BF16)] * 2


def run(kernel, out_shape, *operands, scalars=1, **options):
    smem = pl.BlockSpec(memory_space=pltpu.SMEM)
    vmem = pl.BlockSpec(memory_space=pltpu.VMEM)
    return pl.pallas_call(
        kernel,
        out_shape=out_shape,
        in_specs=[smem] * scalars + [vmem] * (len(operands) - scalars),
        out_specs=[vmem] * len(out_shape),
        compiler_params=pltpu.CompilerParams(vmem_limit_bytes=32 * 1024 * 1024),
        **options,
    )(*operands)


def body(leaf_maps, leaf_operator, region_eps, wave_sq, region_labels, build_flags):
    across = lax.axis_index("bx") % 2
    upward = lax.axis_index("by")
    place = jnp.stack([across, upward // 2 % 2, upward % 2]).astype(jnp.int32)
    size = leaf_operator.shape[0]
    facts = sum(
        lax.pad(x.reshape((1, 1)).astype(F32), jnp.float32(0), ((i, 7 - i, 0), (0, 127, 0)))
        for i, x in enumerate((build_flags, region_labels, wave_sq))
    )
    mine = pl.pallas_call(
        build_kernel,
        out_shape=jax.ShapeDtypeStruct((LEAF, LEAF), F32),
        in_specs=[pl.BlockSpec(memory_space=pltpu.VMEM)]
        + [pl.BlockSpec(memory_space=pltpu.HBM)] * 3,
        out_specs=pl.BlockSpec(memory_space=pltpu.VMEM),
        scratch_shapes=[
            pltpu.VMEM(region_eps.shape, F32),
            pltpu.VMEM((128, size), F32),
            pltpu.VMEM((size - LEAF - 128, size), F32),
            pltpu.VMEM((LEAF, size), F32),
            pltpu.SemaphoreType.DMA((5,)),
        ],
        compiler_params=pltpu.CompilerParams(vmem_limit_bytes=32 * 1024 * 1024),
        name="leaf_build",
    )(
        facts,
        *(
            pltpu.with_memory_space_constraint(x, pltpu.HBM)
            for x in (leaf_maps[0, 0], leaf_operator, region_eps)
        ),
    )
    theirs = swapped(mine, "by", 0)
    one, two, link, *solved = run(
        first_kernel,
        shapes((CUT, 128), (512 - CUT, 128), (FACE, 128)) + pair(FACE, 6 * FACE),
        place,
        mine,
        theirs,
        name="first_merge",
    )
    received_one = swapped(one, "bx", 0)
    received_two = swapped(two, "bx", 0)
    *inverse, outer = run(
        second_kernel,
        pair(128, 128) + shapes((96, 6 * FACE)),
        place,
        one,
        received_one,
        mine,
        theirs,
        *solved,
        scratch_shapes=[pltpu.VMEM((192, 6 * FACE), F32), pltpu.VMEM((192, 128), F32)],
        cost_estimate=LONG,
        name="second_inverse",
    )
    one, two, *right = run(
        exchange_kernel,
        shapes((CUT, 128), (512 - CUT, 128)) + pair(128, 8 * FACE),
        place,
        one,
        two,
        received_one,
        received_two,
        link,
        *inverse,
        name="second_merge",
    )
    received_one = swapped(one, "by", 1)
    received_two = swapped(two, "by", 1)
    (rows,) = run(
        outer_kernel, shapes((96, 8 * FACE)), place, outer, *inverse, *right, name="second_rows"
    )
    half, *solved = run(
        third_kernel,
        shapes((96, 6 * FACE)) + pair(96, 128),
        one,
        two,
        received_one,
        rows,
        scalars=0,
        cost_estimate=LONG,
        name="third_inverse",
    )
    (result,) = run(
        last_kernel,
        shapes((96, 12 * FACE)),
        place,
        half,
        received_one,
        received_two,
        *solved,
        name="third_merge",
    )
    return result.reshape((1, 1, 96, 12 * FACE))


def solution(mesh):
    placed = (
        P(("freq", "bx"), "by", None, None),
        P(),
        P(),
        P("freq"),
        P("bx", "by"),
        P("bx", "by"),
    )
    return jax.shard_map(
        body,
        mesh=mesh,
        in_specs=placed,
        out_specs=P(("freq", "bx"), "by", None, None),
        check_vma=False,
    )
```

```python
import jax
import jax.numpy as jnp
from jax import lax
from jax.experimental import pallas as pl
from jax.experimental.pallas import tpu as pltpu
from jax.sharding import PartitionSpec as P

FACE = 64
LEAF = 4 * FACE
CUT = 176
F32 = jnp.float32
BF16 = jnp.bfloat16


LONG = pl.CostEstimate(flops=10**10, bytes_accessed=10**8, transcendentals=10**6)


def swapped(shard, axis, stride):
    return lax.ppermute(shard, axis, [(i, i ^ 1 << stride) for i in range(lax.axis_size(axis))])


def split(x):
    high = x.astype(BF16)
    return high, (x - high.astype(F32)).astype(BF16)


def thirds(x):
    high = x.astype(BF16).astype(F32)
    rest = x - high
    middle = rest.astype(BF16).astype(F32)
    return high, middle, (rest - middle).astype(BF16).astype(F32)


def dot(a, b):
    return jnp.dot(a, b, preferred_element_type=F32)


def product(a, b):
    (a_high, a_low), (b_high, b_low) = a, b
    depth = a_high.shape[1]
    if depth % 128 and depth != FACE:
        return dot(a_high, b_high) + (dot(a_high, b_low) + dot(a_low, b_high))
    twice = dot(
        jnp.concatenate([a_high, a_low], axis=1), jnp.concatenate([b_high, b_high], axis=0)
    )
    return twice + dot(a_high, b_low)


def spd_inverse(matrix, panel=4, look=2, half=6):
    size = matrix.shape[0]
    shape = (8, size)
    count = size // 8
    tiles = [matrix[8 * g : 8 * g + 8] for g in range(count)]
    lane = lax.broadcasted_iota(jnp.int32, shape, 1)
    sub = lax.broadcasted_iota(jnp.int32, shape, 0)

    def column(tile, c):
        return jnp.broadcast_to(tile[:, c : c + 1], shape)

    def row(tile, r):
        return jnp.broadcast_to(tile[r : r + 1, :], shape)

    def inside(start, stop):
        return (lane >= start) & (lane < stop)

    pivot = [column(tiles[0], j) for j in range(8)]
    for start in range(0, count, panel):
        stop = min(start + panel, count)
        last = min(stop + look, count)
        outside = [*range(last, count), *range(start)]
        if outside:
            strip = jnp.concatenate([tiles[g] for g in outside], axis=0)[:, 8 * start : 8 * stop]
            high, middle, low = thirds(strip)
            left = jnp.concatenate([high, high, middle, high, low, middle], axis=1).astype(BF16)
        for k in range(start, stop):
            first = 8 * k
            block = inside(first, first + 8)
            rows = jnp.where(block, (lane - first == sub).astype(F32), tiles[k])
            ahead = k + 1 < count
            if ahead:
                after = jnp.where(block, 0.0, tiles[k + 1])
                side = [column(tiles[k + 1], first + j) for j in range(8)]
            scale = None
            for p in range(8):
                inverse = pl.reciprocal(row(pivot[p], p), approx=True)
                factor = jnp.where(sub == p, 0.0, pivot[p]) * inverse
                picked = row(rows, p)
                if ahead:
                    edge = side[p]
                    factor_ahead = edge * inverse
                    if p == half:
                        coming = [column(after, first + 8 + j) for j in range(8)]
                    if p >= half:
                        for j in range(8):
                            coming[j] = coming[j] - factor_ahead * row(edge, j)
                    after = after - factor_ahead * picked
                for j in range(p + 1, 8):
                    element = row(pivot[j], p)
                    pivot[j] = pivot[j] - factor * element
                    if ahead:
                        side[j] = side[j] - factor_ahead * element
                rows = rows - factor * picked
                scale = inverse if scale is None else jnp.where(sub == p, inverse, scale)
            rows = rows * scale
            picked = [row(rows, j) for j in range(8)]
            for g in range(start, last):
                if g == k:
                    tiles[g] = rows
                elif g == k + 1:
                    tiles[g] = after
                else:
                    new = jnp.where(block, 0.0, tiles[g])
                    for j in range(8):
                        new = new - column(tiles[g], first + j) * picked[j]
                    tiles[g] = new
            if ahead:
                pivot = coming
        if outside:
            right = jnp.concatenate(tiles[start:stop], axis=0)
            high, middle, low = thirds(right)
            right = jnp.concatenate([high, middle, high, low, high, middle], axis=0).astype(BF16)
            update = dot(left, right)
            block = inside(8 * start, 8 * stop)
            for i, g in enumerate(outside):
                tiles[g] = jnp.where(block, 0.0, tiles[g]) - update[8 * i : 8 * i + 8]
    return jnp.concatenate(tiles, axis=0)


def build_kernel(label, flag, wave, given, operator, table_at, out, table, one, two, edge, sems):
    size = operator.shape[0]
    middle = LEAF + 128
    copies = [
        pltpu.make_async_copy(source, target, sems.at[i])
        for i, (source, target) in enumerate(
            (
                (operator.at[pl.ds(LEAF, 128)], one),
                (table_at, table),
                (operator.at[pl.ds(middle, size - middle)], two),
                (operator.at[pl.ds(0, LEAF)], edge),
                (given, out),
            )
        )
    ]
    flagged = flag[0, 0] > 0

    @pl.when(jnp.logical_not(flagged))
    def _():
        copies[4].start()
        copies[4].wait()

    @pl.when(flagged)
    def _():
        for copy in copies[:4]:
            copy.start()
        for copy in copies[:2]:
            copy.wait()
        shift = wave[0] * table[pl.ds(label[0, 0], 1), :]
        border, near, far = slice(0, LEAF), slice(LEAF, middle), slice(middle, size)

        def shifted(ref, span):
            block = ref[:, span]
            ids = lax.broadcasted_iota(jnp.int32, block.shape, 0)
            diagonal = ids == lax.broadcasted_iota(jnp.int32, block.shape, 1)
            return block - jnp.where(diagonal, shift[:, span], 0.0)

        right = split(one[:, border]), split(one[:, far])
        inverse = split(spd_inverse(shifted(one, near)))
        for copy in copies[2:4]:
            copy.wait()
        left = split(two[:, near])
        solved_far = split(product(inverse, right[1]))
        inner = shifted(two, far) - product(left, solved_far)
        solved = split(product(inverse, right[0]))
        coupled = split(two[:, border] - product(left, solved))
        left = split(edge[:, near])
        merged = shifted(edge, border) - product(left, solved)
        across = split(edge[:, far] - product(left, solved_far))
        inverse = split(spd_inverse(inner))
        solved = split(product(inverse, coupled))
        out[...] = merged - product(across, solved)


def halves(shape):
    return lax.broadcasted_iota(jnp.int32, shape, 1) < FACE


def turn(tile):
    return pltpu.roll(tile, FACE, 1)


def leaf_rows(place, mine, theirs):
    across, third, lead = place[0], place[1], place[2]
    is_alpha = lead == 0
    left = halves((FACE, 128))

    def load(alpha, block, tile):
        spot = pl.ds(pl.multiple_of(block * FACE, FACE), FACE)
        span = slice(128 * tile, 128 * tile + 128)
        own = is_alpha if alpha else jnp.logical_not(is_alpha)
        return jnp.where(own, mine[spot, span], theirs[spot, span])

    def alpha_rows(block):
        sides = load(True, block, 0)
        ends = load(True, block, 1)
        sides = jnp.where(across == 0, turn(sides), sides)
        tiles = (
            jnp.where(left, sides, 0.0),
            jnp.where(left, jnp.where(third == 0, 0.0, ends), sides),
            jnp.where(left & (third == 0), ends, 0.0),
        )
        return jnp.concatenate(tiles, axis=1), turn(ends)

    def beta_rows(block):
        sides = load(False, block, 0)
        ends = load(False, block, 1)
        other = turn(sides)
        near_far = jnp.where(across == 0, other, sides)
        far_near = jnp.where(across == 0, sides, other)
        flipped = turn(ends)
        tiles = (
            jnp.where(left, 0.0, far_near),
            jnp.where(left & (third == 0), flipped, 0.0),
            jnp.where(
                third == 0,
                jnp.where(left, 0.0, near_far),
                jnp.where(left, far_near, ends),
            ),
        )
        return jnp.concatenate(tiles, axis=1), ends

    return alpha_rows, beta_rows


def either(flag, one, other):
    return [jnp.where(flag, x, y) for x, y in zip(one, other)]


def stacked(one, two, start, stop):
    parts = []
    if start < CUT:
        parts.append(one[start : min(stop, CUT), :])
    if stop > CUT:
        parts.append(two[max(start, CUT) - CUT : stop - CUT, :])
    return jnp.concatenate(parts, axis=0)


def stack(one, two, start, value):
    stop = start + value.shape[0]
    if start < CUT:
        one[start : min(stop, CUT), :] = value[: CUT - start]
    if stop > CUT:
        two[max(start, CUT) - CUT : stop - CUT, :] = value[max(CUT - start, 0) :]


def first_kernel(place, mine, theirs, message_one, message_two, link, solved_high, solved_low):
    alpha_rows, beta_rows = leaf_rows(place, mine, theirs)
    near = jnp.where(place[0] == 0, 1, 0)
    tiles_a, meet_a = alpha_rows(3)
    tiles_b, meet_b = beta_rows(2)
    system = (meet_a + meet_b)[:, :FACE]
    right = split(tiles_a + tiles_b)
    parts = [alpha_rows(near), beta_rows(near), either(place[1] == 0, beta_rows(3), alpha_rows(2))]
    direct = jnp.concatenate([tiles for tiles, _ in parts], axis=0)
    coupling = split(jnp.concatenate([meet for _, meet in parts], axis=0)[:, :FACE])
    inverse = split(spd_inverse(system, panel=8))
    solved = split(product(inverse, right))
    merged = direct - product(coupling, solved)
    for i in range(3):
        stack(message_one, message_two, 128 * i, merged[0:128, 128 * i : 128 * i + 128])
    stack(message_one, message_two, 384, merged[128:192, 128:256])
    stack(message_one, message_two, 448, merged[128:192, 256:384])
    link[...] = merged[128:192, 0:128]
    solved_high[...], solved_low[...] = solved


def second_kernel(
    place, own, received, mine, theirs, solved_high, solved_low, inverse_high, inverse_low, outer, direct, coupling
):
    alpha_rows, beta_rows = leaf_rows(place, mine, theirs)
    third, lead = place[1], place[2]
    far = jnp.where(place[0] == 0, 0, 1)
    direct[0:64, :], coupling[0:64, :] = alpha_rows(far)
    at_two = alpha_rows(2)
    at_far = beta_rows(far)
    at_three = beta_rows(3)
    direct[64:128, :], coupling[64:128, :] = either(third == 0, at_two, at_far)
    direct[128:192, :], coupling[128:192, :] = either(third == 0, at_far, at_three)
    spot = pl.ds(pl.multiple_of(lead * 96, 32), 96)
    solved = solved_high[...], solved_low[...]
    outer[...] = direct[spot, :] - product(split(coupling[spot, :][:, :FACE]), solved)
    inverse_high[...], inverse_low[...] = split(spd_inverse(own[0:128, :] + received[0:128, :]))


def assemble(alpha, beta):
    rows = (alpha or beta)[0].shape[0]
    left = halves((rows, 128))
    blank = jnp.zeros((rows, 128), F32)
    if alpha is None:
        tiles = (
            jnp.where(left, 0.0, turn(beta[0])),
            blank,
            jnp.where(left, 0.0, beta[0]),
            beta[1],
        )
        return jnp.concatenate(tiles, axis=1)
    turned = turn(alpha[1])
    middle = jnp.where(left, turn(alpha[0]), turned)
    if beta is None:
        tiles = jnp.where(left, alpha[0], 0.0), middle, jnp.where(left, turned, 0.0), blank
        return jnp.concatenate(tiles, axis=1)
    tiles = (
        jnp.where(left, alpha[0], turn(beta[0])),
        middle,
        jnp.where(left, turned, beta[0]),
        beta[1],
    )
    return jnp.concatenate(tiles, axis=1)


def exchange_kernel(
    place,
    own_one,
    own_two,
    received_one,
    received_two,
    link,
    inverse_high,
    inverse_low,
    message_one,
    message_two,
    right_high,
    right_low,
):
    is_alpha = place[0] == 0

    def both(mine, other):
        return jnp.where(is_alpha, mine, other), jnp.where(is_alpha, other, mine)

    def part(start, stop):
        return both(stacked(own_one, own_two, start, stop), stacked(received_one, received_two, start, stop))

    one, two = part(128, 256), part(256, 384)
    right = split(assemble((one[0], two[0]), (one[1], two[1])))
    face, back = part(384, 448), part(448, 512)
    direct = jnp.concatenate(
        [assemble((face[0], back[0]), None), assemble(None, (face[1], back[1]))], axis=0
    )
    mine = link[...]
    other = jnp.transpose(stacked(received_one, received_two, 128, 256))[0:FACE]
    coupling = jnp.concatenate(
        [jnp.where(is_alpha, mine, other), jnp.where(is_alpha, other, mine)], axis=0
    )
    solved = split(product(split(coupling), (inverse_high[...], inverse_low[...])))
    merged = direct - product(solved, right)
    for i in range(4):
        stack(message_one, message_two, 128 * i, merged[:, 128 * i : 128 * i + 128])
    right_high[...], right_low[...] = right


def rest_columns(one, two):
    return jnp.concatenate(
        [stacked(one, two, 128 * i, 128 * i + 128) for i in range(1, 4)], axis=1
    )


def outer_kernel(place, outer, inverse_high, inverse_low, right_high, right_low, rows):
    mine = outer[:, 128:256], outer[:, 256:384]
    direct = jnp.where(place[0] == 0, assemble(mine, None), assemble(None, mine))
    solved = split(product(split(outer[:, 0:128]), (inverse_high[...], inverse_low[...])))
    rows[...] = direct - product(solved, (right_high[...], right_low[...]))


def third_kernel(own_one, own_two, received, rows, half, solved_high, solved_low):
    coupling = split(rows[:, 0:128])
    right = split(rest_columns(own_one, own_two))
    inverse = split(spd_inverse(own_one[0:128, :] + received[0:128, :]))
    solved = split(product(coupling, inverse))
    half[...] = rows[:, 128:512] - product(solved, right)
    solved_high[...], solved_low[...] = solved


def last_kernel(place, half, received_one, received_two, solved_high, solved_low, out):
    third = place[1]
    width = 6 * FACE
    mine = pl.multiple_of(third * width, 128)
    other = pl.multiple_of((1 - third) * width, 128)
    out[:, pl.ds(mine, width)] = half[...]
    solved = solved_high[...], solved_low[...]
    out[:, pl.ds(other, width)] = -product(solved, split(rest_columns(received_one, received_two)))


def shapes(*sizes):
    return [jax.ShapeDtypeStruct(size, F32) for size in sizes]


def pair(*size):
    return [jax.ShapeDtypeStruct(size, BF16)] * 2


def run(kernel, out_shape, *operands, scalars=1, **options):
    smem = pl.BlockSpec(memory_space=pltpu.SMEM)
    vmem = pl.BlockSpec(memory_space=pltpu.VMEM)
    return pl.pallas_call(
        kernel,
        out_shape=out_shape,
        in_specs=[smem] * scalars + [vmem] * (len(operands) - scalars),
        out_specs=[vmem] * len(out_shape),
        compiler_params=pltpu.CompilerParams(vmem_limit_bytes=32 * 1024 * 1024),
        **options,
    )(*operands)


def body(leaf_maps, leaf_operator, region_eps, wave_sq, region_labels, build_flags):
    across = lax.axis_index("bx") % 2
    upward = lax.axis_index("by")
    place = jnp.stack([across, upward // 2 % 2, upward % 2]).astype(jnp.int32)
    size = leaf_operator.shape[0]
    mine = pl.pallas_call(
        build_kernel,
        out_shape=jax.ShapeDtypeStruct((LEAF, LEAF), F32),
        in_specs=[pl.BlockSpec(memory_space=pltpu.SMEM)] * 3
        + [pl.BlockSpec(memory_space=pltpu.HBM)] * 3,
        out_specs=pl.BlockSpec(memory_space=pltpu.VMEM),
        scratch_shapes=[
            pltpu.VMEM(region_eps.shape, F32),
            pltpu.VMEM((128, size), F32),
            pltpu.VMEM((size - LEAF - 128, size), F32),
            pltpu.VMEM((LEAF, size), F32),
            pltpu.SemaphoreType.DMA((5,)),
        ],
        compiler_params=pltpu.CompilerParams(vmem_limit_bytes=32 * 1024 * 1024),
        name="leaf_build",
    )(
        region_labels,
        build_flags,
        wave_sq,
        *(
            pltpu.with_memory_space_constraint(x, pltpu.HBM)
            for x in (leaf_maps[0, 0], leaf_operator, region_eps)
        ),
    )
    theirs = swapped(mine, "by", 0)
    one, two, link, *solved = run(
        first_kernel,
        shapes((CUT, 128), (512 - CUT, 128), (FACE, 128)) + pair(FACE, 6 * FACE),
        place,
        mine,
        theirs,
        name="first_merge",
    )
    received_one = swapped(one, "bx", 0)
    received_two = swapped(two, "bx", 0)
    *inverse, outer = run(
        second_kernel,
        pair(128, 128) + shapes((96, 6 * FACE)),
        place,
        one,
        received_one,
        mine,
        theirs,
        *solved,
        scratch_shapes=[pltpu.VMEM((192, 6 * FACE), F32), pltpu.VMEM((192, 128), F32)],
        cost_estimate=LONG,
        name="second_inverse",
    )
    one, two, *right = run(
        exchange_kernel,
        shapes((CUT, 128), (512 - CUT, 128)) + pair(128, 8 * FACE),
        place,
        one,
        two,
        received_one,
        received_two,
        link,
        *inverse,
        name="second_merge",
    )
    received_one = swapped(one, "by", 1)
    received_two = swapped(two, "by", 1)
    (rows,) = run(
        outer_kernel, shapes((96, 8 * FACE)), place, outer, *inverse, *right, name="second_rows"
    )
    half, *solved = run(
        third_kernel,
        shapes((96, 6 * FACE)) + pair(96, 128),
        one,
        two,
        received_one,
        rows,
        scalars=0,
        cost_estimate=LONG,
        name="third_inverse",
    )
    (result,) = run(
        last_kernel,
        shapes((96, 12 * FACE)),
        place,
        half,
        received_one,
        received_two,
        *solved,
        name="third_merge",
    )
    return result.reshape((1, 1, 96, 12 * FACE))


def solution(mesh):
    placed = (
        P(("freq", "bx"), "by", None, None),
        P(),
        P(),
        P("freq"),
        P("bx", "by"),
        P("bx", "by"),
    )
    return jax.shard_map(
        body,
        mesh=mesh,
        in_specs=placed,
        out_specs=P(("freq", "bx"), "by", None, None),
        check_vma=False,
    )
```

```python
import jax
import jax.numpy as jnp
from jax import lax
from jax.experimental import pallas as pl
from jax.experimental.pallas import tpu as pltpu
from jax.sharding import PartitionSpec as P

FACE = 64
LEAF = 4 * FACE
CUT = 176
F32 = jnp.float32
BF16 = jnp.bfloat16


LONG = pl.CostEstimate(flops=10**10, bytes_accessed=10**8, transcendentals=10**6)


def swapped(shard, axis, stride):
    return lax.ppermute(shard, axis, [(i, i ^ 1 << stride) for i in range(lax.axis_size(axis))])


def split(x):
    high = x.astype(BF16)
    return high, (x - high.astype(F32)).astype(BF16)


def thirds(x):
    high = x.astype(BF16).astype(F32)
    rest = x - high
    middle = rest.astype(BF16).astype(F32)
    return high, middle, (rest - middle).astype(BF16).astype(F32)


def dot(a, b):
    return jnp.dot(a, b, preferred_element_type=F32)


def product(a, b):
    (a_high, a_low), (b_high, b_low) = a, b
    depth = a_high.shape[1]
    if depth % 128 and depth != FACE:
        return dot(a_high, b_high) + (dot(a_high, b_low) + dot(a_low, b_high))
    twice = dot(
        jnp.concatenate([a_high, a_low], axis=1), jnp.concatenate([b_high, b_high], axis=0)
    )
    return twice + dot(a_high, b_low)


def tree(terms):
    while len(terms) > 1:
        terms = [x + y for x, y in zip(terms[::2], terms[1::2])]
    return terms[0]


def minus(value, terms):
    for term in terms:
        value = value - term
    return value


def spd_inverse(matrix, panel=4, look=4, half=4):
    size = matrix.shape[0]
    shape = (8, size)
    count = size // 8
    tiles = [matrix[8 * g : 8 * g + 8] for g in range(count)]
    lane = lax.broadcasted_iota(jnp.int32, shape, 1)
    sub = lax.broadcasted_iota(jnp.int32, shape, 0)

    def column(tile, c):
        return jnp.broadcast_to(tile[:, c : c + 1], shape)

    def row(tile, r):
        return jnp.broadcast_to(tile[r : r + 1, :], shape)

    def inside(start, stop):
        return (lane >= start) & (lane < stop)

    pivot = [column(tiles[0], j) for j in range(8)]
    for start in range(0, count, panel):
        stop = min(start + panel, count)
        last = min(stop + look, count)
        outside = [*range(last, count), *range(start)]
        if outside:
            strip = jnp.concatenate([tiles[g] for g in outside], axis=0)[:, 8 * start : 8 * stop]
            high, middle, low = thirds(strip)
            left = jnp.concatenate([high, high, middle, high, low, middle], axis=1).astype(BF16)
        for k in range(start, stop):
            first = 8 * k
            block = inside(first, first + 8)
            rows = jnp.where(block, (lane - first == sub).astype(F32), tiles[k])
            ahead = k + 1 < count
            if ahead:
                after = jnp.where(block, 0.0, tiles[k + 1])
                side = [column(tiles[k + 1], first + j) for j in range(8)]
            scale = None
            for p in range(8):
                inverse = pl.reciprocal(row(pivot[p], p), approx=True)
                factor = jnp.where(sub == p, 0.0, pivot[p]) * inverse
                picked = row(rows, p)
                if ahead:
                    edge = side[p]
                    factor_ahead = edge * inverse
                    if p == half:
                        coming = [column(after, first + 8 + j) for j in range(8)]
                    if p >= half:
                        for j in range(8):
                            coming[j] = coming[j] - factor_ahead * row(edge, j)
                    after = after - factor_ahead * picked
                for j in range(p + 1, 8):
                    element = row(pivot[j], p)
                    pivot[j] = pivot[j] - factor * element
                    if ahead:
                        side[j] = side[j] - factor_ahead * element
                rows = rows - factor * picked
                scale = inverse if scale is None else jnp.where(sub == p, inverse, scale)
            rows = rows * scale
            picked = [row(rows, j) for j in range(8)]
            for g in range(start, last):
                if g == k:
                    tiles[g] = rows
                elif g == k + 1:
                    tiles[g] = after
                else:
                    terms = [column(tiles[g], first + j) * picked[j] for j in range(8)]
                    cleared = jnp.where(block, 0.0, tiles[g])
                    tiles[g] = cleared - tree(terms) if count <= panel else minus(cleared, terms)
            if ahead:
                pivot = coming
        if outside:
            right = jnp.concatenate(tiles[start:stop], axis=0)
            high, middle, low = thirds(right)
            right = jnp.concatenate([high, middle, high, low, high, middle], axis=0).astype(BF16)
            update = dot(left, right)
            block = inside(8 * start, 8 * stop)
            for i, g in enumerate(outside):
                tiles[g] = jnp.where(block, 0.0, tiles[g]) - update[8 * i : 8 * i + 8]
    return jnp.concatenate(tiles, axis=0)


def build_kernel(label, flag, wave, given, operator, table_at, out, table, one, two, edge, sems):
    size = operator.shape[0]
    middle = LEAF + 128
    copies = [
        pltpu.make_async_copy(source, target, sems.at[i])
        for i, (source, target) in enumerate(
            (
                (operator.at[pl.ds(LEAF, 128)], one),
                (table_at, table),
                (operator.at[pl.ds(middle, size - middle)], two),
                (operator.at[pl.ds(0, LEAF)], edge),
                (given, out),
            )
        )
    ]
    flagged = flag[0, 0] > 0

    @pl.when(jnp.logical_not(flagged))
    def _():
        copies[4].start()
        copies[4].wait()

    @pl.when(flagged)
    def _():
        for copy in copies[:4]:
            copy.start()
        for copy in copies[:2]:
            copy.wait()
        shift = wave[0] * table[pl.ds(label[0, 0], 1), :]
        border, near, far = slice(0, LEAF), slice(LEAF, middle), slice(middle, size)

        def shifted(ref, span):
            block = ref[:, span]
            ids = lax.broadcasted_iota(jnp.int32, block.shape, 0)
            diagonal = ids == lax.broadcasted_iota(jnp.int32, block.shape, 1)
            return block - jnp.where(diagonal, shift[:, span], 0.0)

        right = split(one[:, border]), split(one[:, far])
        inverse = split(spd_inverse(shifted(one, near)))
        for copy in copies[2:4]:
            copy.wait()
        left = split(two[:, near])
        solved_far = split(product(inverse, right[1]))
        inner = shifted(two, far) - product(left, solved_far)
        solved = split(product(inverse, right[0]))
        coupled = split(two[:, border] - product(left, solved))
        left = split(edge[:, near])
        merged = shifted(edge, border) - product(left, solved)
        across = split(edge[:, far] - product(left, solved_far))
        inverse = split(spd_inverse(inner))
        solved = split(product(inverse, coupled))
        out[...] = merged - product(across, solved)


def halves(shape):
    return lax.broadcasted_iota(jnp.int32, shape, 1) < FACE


def turn(tile):
    return pltpu.roll(tile, FACE, 1)


def leaf_rows(place, mine, theirs):
    across, third, lead = place[0], place[1], place[2]
    is_alpha = lead == 0
    left = halves((FACE, 128))

    def load(alpha, block, tile):
        spot = pl.ds(pl.multiple_of(block * FACE, FACE), FACE)
        span = slice(128 * tile, 128 * tile + 128)
        own = is_alpha if alpha else jnp.logical_not(is_alpha)
        return jnp.where(own, mine[spot, span], theirs[spot, span])

    def alpha_rows(block):
        sides = load(True, block, 0)
        ends = load(True, block, 1)
        sides = jnp.where(across == 0, turn(sides), sides)
        tiles = (
            jnp.where(left, sides, 0.0),
            jnp.where(left, jnp.where(third == 0, 0.0, ends), sides),
            jnp.where(left & (third == 0), ends, 0.0),
        )
        return jnp.concatenate(tiles, axis=1), turn(ends)

    def beta_rows(block):
        sides = load(False, block, 0)
        ends = load(False, block, 1)
        other = turn(sides)
        near_far = jnp.where(across == 0, other, sides)
        far_near = jnp.where(across == 0, sides, other)
        flipped = turn(ends)
        tiles = (
            jnp.where(left, 0.0, far_near),
            jnp.where(left & (third == 0), flipped, 0.0),
            jnp.where(
                third == 0,
                jnp.where(left, 0.0, near_far),
                jnp.where(left, far_near, ends),
            ),
        )
        return jnp.concatenate(tiles, axis=1), ends

    return alpha_rows, beta_rows


def either(flag, one, other):
    return [jnp.where(flag, x, y) for x, y in zip(one, other)]


def stacked(one, two, start, stop):
    parts = []
    if start < CUT:
        parts.append(one[start : min(stop, CUT), :])
    if stop > CUT:
        parts.append(two[max(start, CUT) - CUT : stop - CUT, :])
    return jnp.concatenate(parts, axis=0)


def stack(one, two, start, value):
    stop = start + value.shape[0]
    if start < CUT:
        one[start : min(stop, CUT), :] = value[: CUT - start]
    if stop > CUT:
        two[max(start, CUT) - CUT : stop - CUT, :] = value[max(CUT - start, 0) :]


def first_kernel(place, mine, theirs, message_one, message_two, link, solved_high, solved_low):
    alpha_rows, beta_rows = leaf_rows(place, mine, theirs)
    near = jnp.where(place[0] == 0, 1, 0)
    tiles_a, meet_a = alpha_rows(3)
    tiles_b, meet_b = beta_rows(2)
    system = (meet_a + meet_b)[:, :FACE]
    right = split(tiles_a + tiles_b)
    parts = [alpha_rows(near), beta_rows(near), either(place[1] == 0, beta_rows(3), alpha_rows(2))]
    direct = jnp.concatenate([tiles for tiles, _ in parts], axis=0)
    coupling = split(jnp.concatenate([meet for _, meet in parts], axis=0)[:, :FACE])
    inverse = split(spd_inverse(system, panel=8))
    solved = split(product(inverse, right))
    merged = direct - product(coupling, solved)
    for i in range(3):
        stack(message_one, message_two, 128 * i, merged[0:128, 128 * i : 128 * i + 128])
    stack(message_one, message_two, 384, merged[128:192, 128:256])
    stack(message_one, message_two, 448, merged[128:192, 256:384])
    link[...] = merged[128:192, 0:128]
    solved_high[...], solved_low[...] = solved


def second_kernel(
    place, own, received, mine, theirs, solved_high, solved_low, inverse_high, inverse_low, outer, direct, coupling
):
    alpha_rows, beta_rows = leaf_rows(place, mine, theirs)
    third, lead = place[1], place[2]
    far = jnp.where(place[0] == 0, 0, 1)
    direct[0:64, :], coupling[0:64, :] = alpha_rows(far)
    at_two = alpha_rows(2)
    at_far = beta_rows(far)
    at_three = beta_rows(3)
    direct[64:128, :], coupling[64:128, :] = either(third == 0, at_two, at_far)
    direct[128:192, :], coupling[128:192, :] = either(third == 0, at_far, at_three)
    spot = pl.ds(pl.multiple_of(lead * 96, 32), 96)
    solved = solved_high[...], solved_low[...]
    outer[...] = direct[spot, :] - product(split(coupling[spot, :][:, :FACE]), solved)
    inverse_high[...], inverse_low[...] = split(spd_inverse(own[0:128, :] + received[0:128, :]))


def assemble(alpha, beta):
    rows = (alpha or beta)[0].shape[0]
    left = halves((rows, 128))
    blank = jnp.zeros((rows, 128), F32)
    if alpha is None:
        tiles = (
            jnp.where(left, 0.0, turn(beta[0])),
            blank,
            jnp.where(left, 0.0, beta[0]),
            beta[1],
        )
        return jnp.concatenate(tiles, axis=1)
    turned = turn(alpha[1])
    middle = jnp.where(left, turn(alpha[0]), turned)
    if beta is None:
        tiles = jnp.where(left, alpha[0], 0.0), middle, jnp.where(left, turned, 0.0), blank
        return jnp.concatenate(tiles, axis=1)
    tiles = (
        jnp.where(left, alpha[0], turn(beta[0])),
        middle,
        jnp.where(left, turned, beta[0]),
        beta[1],
    )
    return jnp.concatenate(tiles, axis=1)


def exchange_kernel(
    place,
    own_one,
    own_two,
    received_one,
    received_two,
    link,
    inverse_high,
    inverse_low,
    message_one,
    message_two,
    right_high,
    right_low,
):
    is_alpha = place[0] == 0

    def both(mine, other):
        return jnp.where(is_alpha, mine, other), jnp.where(is_alpha, other, mine)

    def part(start, stop):
        return both(stacked(own_one, own_two, start, stop), stacked(received_one, received_two, start, stop))

    one, two = part(128, 256), part(256, 384)
    right = split(assemble((one[0], two[0]), (one[1], two[1])))
    face, back = part(384, 448), part(448, 512)
    direct = jnp.concatenate(
        [assemble((face[0], back[0]), None), assemble(None, (face[1], back[1]))], axis=0
    )
    mine = link[...]
    other = jnp.transpose(stacked(received_one, received_two, 128, 256))[0:FACE]
    coupling = jnp.concatenate(
        [jnp.where(is_alpha, mine, other), jnp.where(is_alpha, other, mine)], axis=0
    )
    solved = split(product(split(coupling), (inverse_high[...], inverse_low[...])))
    merged = direct - product(solved, right)
    for i in range(4):
        stack(message_one, message_two, 128 * i, merged[:, 128 * i : 128 * i + 128])
    right_high[...], right_low[...] = right


def rest_columns(one, two):
    return jnp.concatenate(
        [stacked(one, two, 128 * i, 128 * i + 128) for i in range(1, 4)], axis=1
    )


def outer_kernel(place, outer, inverse_high, inverse_low, right_high, right_low, rows):
    mine = outer[:, 128:256], outer[:, 256:384]
    direct = jnp.where(place[0] == 0, assemble(mine, None), assemble(None, mine))
    solved = split(product(split(outer[:, 0:128]), (inverse_high[...], inverse_low[...])))
    rows[...] = direct - product(solved, (right_high[...], right_low[...]))


def third_kernel(own_one, own_two, received, rows, half, solved_high, solved_low):
    coupling = split(rows[:, 0:128])
    right = split(rest_columns(own_one, own_two))
    inverse = split(spd_inverse(own_one[0:128, :] + received[0:128, :]))
    solved = split(product(coupling, inverse))
    half[...] = rows[:, 128:512] - product(solved, right)
    solved_high[...], solved_low[...] = solved


def last_kernel(place, half, received_one, received_two, solved_high, solved_low, out):
    third = place[1]
    width = 6 * FACE
    mine = pl.multiple_of(third * width, 128)
    other = pl.multiple_of((1 - third) * width, 128)
    out[:, pl.ds(mine, width)] = half[...]
    solved = solved_high[...], solved_low[...]
    out[:, pl.ds(other, width)] = -product(solved, split(rest_columns(received_one, received_two)))


def shapes(*sizes):
    return [jax.ShapeDtypeStruct(size, F32) for size in sizes]


def pair(*size):
    return [jax.ShapeDtypeStruct(size, BF16)] * 2


def run(kernel, out_shape, *operands, scalars=1, **options):
    smem = pl.BlockSpec(memory_space=pltpu.SMEM)
    vmem = pl.BlockSpec(memory_space=pltpu.VMEM)
    return pl.pallas_call(
        kernel,
        out_shape=out_shape,
        in_specs=[smem] * scalars + [vmem] * (len(operands) - scalars),
        out_specs=[vmem] * len(out_shape),
        compiler_params=pltpu.CompilerParams(vmem_limit_bytes=32 * 1024 * 1024),
        **options,
    )(*operands)


def body(leaf_maps, leaf_operator, region_eps, wave_sq, region_labels, build_flags):
    across = lax.axis_index("bx") % 2
    upward = lax.axis_index("by")
    place = jnp.stack([across, upward // 2 % 2, upward % 2]).astype(jnp.int32)
    size = leaf_operator.shape[0]
    mine = pl.pallas_call(
        build_kernel,
        out_shape=jax.ShapeDtypeStruct((LEAF, LEAF), F32),
        in_specs=[pl.BlockSpec(memory_space=pltpu.SMEM)] * 3
        + [pl.BlockSpec(memory_space=pltpu.HBM)] * 3,
        out_specs=pl.BlockSpec(memory_space=pltpu.VMEM),
        scratch_shapes=[
            pltpu.VMEM(region_eps.shape, F32),
            pltpu.VMEM((128, size), F32),
            pltpu.VMEM((size - LEAF - 128, size), F32),
            pltpu.VMEM((LEAF, size), F32),
            pltpu.SemaphoreType.DMA((5,)),
        ],
        compiler_params=pltpu.CompilerParams(vmem_limit_bytes=32 * 1024 * 1024),
        name="leaf_build",
    )(
        region_labels,
        build_flags,
        wave_sq,
        *(
            pltpu.with_memory_space_constraint(x, pltpu.HBM)
            for x in (leaf_maps[0, 0], leaf_operator, region_eps)
        ),
    )
    theirs = swapped(mine, "by", 0)
    one, two, link, *solved = run(
        first_kernel,
        shapes((CUT, 128), (512 - CUT, 128), (FACE, 128)) + pair(FACE, 6 * FACE),
        place,
        mine,
        theirs,
        name="first_merge",
    )
    received_one = swapped(one, "bx", 0)
    received_two = swapped(two, "bx", 0)
    *inverse, outer = run(
        second_kernel,
        pair(128, 128) + shapes((96, 6 * FACE)),
        place,
        one,
        received_one,
        mine,
        theirs,
        *solved,
        scratch_shapes=[pltpu.VMEM((192, 6 * FACE), F32), pltpu.VMEM((192, 128), F32)],
        cost_estimate=LONG,
        name="second_inverse",
    )
    one, two, *right = run(
        exchange_kernel,
        shapes((CUT, 128), (512 - CUT, 128)) + pair(128, 8 * FACE),
        place,
        one,
        two,
        received_one,
        received_two,
        link,
        *inverse,
        name="second_merge",
    )
    received_one = swapped(one, "by", 1)
    received_two = swapped(two, "by", 1)
    (rows,) = run(
        outer_kernel, shapes((96, 8 * FACE)), place, outer, *inverse, *right, name="second_rows"
    )
    half, *solved = run(
        third_kernel,
        shapes((96, 6 * FACE)) + pair(96, 128),
        one,
        two,
        received_one,
        rows,
        scalars=0,
        cost_estimate=LONG,
        name="third_inverse",
    )
    (result,) = run(
        last_kernel,
        shapes((96, 12 * FACE)),
        place,
        half,
        received_one,
        received_two,
        *solved,
        name="third_merge",
    )
    return result.reshape((1, 1, 96, 12 * FACE))


def solution(mesh):
    placed = (
        P(("freq", "bx"), "by", None, None),
        P(),
        P(),
        P("freq"),
        P("bx", "by"),
        P("bx", "by"),
    )
    return jax.shard_map(
        body,
        mesh=mesh,
        in_specs=placed,
        out_specs=P(("freq", "bx"), "by", None, None),
        check_vma=False,
    )
```

```python
import jax
import jax.numpy as jnp
from jax import lax
from jax.experimental import pallas as pl
from jax.experimental.pallas import tpu as pltpu
from jax.sharding import PartitionSpec as P

FACE = 64
LEAF = 4 * FACE
CUT = 192
F32 = jnp.float32
BF16 = jnp.bfloat16


LONG = pl.CostEstimate(flops=10**10, bytes_accessed=10**8, transcendentals=10**6)


def swapped(shard, axis, stride):
    return lax.ppermute(shard, axis, [(i, i ^ 1 << stride) for i in range(lax.axis_size(axis))])


def split(x):
    high = x.astype(BF16)
    return high, (x - high.astype(F32)).astype(BF16)


def thirds(x):
    high = x.astype(BF16).astype(F32)
    rest = x - high
    middle = rest.astype(BF16).astype(F32)
    return high, middle, (rest - middle).astype(BF16).astype(F32)


def dot(a, b):
    return jnp.dot(a, b, preferred_element_type=F32)


def product(a, b):
    (a_high, a_low), (b_high, b_low) = a, b
    depth = a_high.shape[1]
    if depth % 128 and depth != FACE:
        return dot(a_high, b_high) + (dot(a_high, b_low) + dot(a_low, b_high))
    twice = dot(
        jnp.concatenate([a_high, a_low], axis=1), jnp.concatenate([b_high, b_high], axis=0)
    )
    return twice + dot(a_high, b_low)


def tree(terms):
    while len(terms) > 1:
        terms = [x + y for x, y in zip(terms[::2], terms[1::2])]
    return terms[0]


def minus(value, terms):
    for term in terms:
        value = value - term
    return value


def spd_inverse(matrix, left=None, panel=4, look=4, half=4):
    size = matrix.shape[0]
    shape = (8, size)
    count = size // 8
    tiles = [matrix[8 * g : 8 * g + 8] for g in range(count)]
    lane = lax.broadcasted_iota(jnp.int32, shape, 1)
    sub = lax.broadcasted_iota(jnp.int32, shape, 0)

    def column(tile, c):
        return jnp.broadcast_to(tile[:, c : c + 1], shape)

    def row(tile, r):
        return jnp.broadcast_to(tile[r : r + 1, :], shape)

    def inside(start, stop):
        return (lane >= start) & (lane < stop)

    pivot = [column(tiles[0], j) for j in range(8)]
    for start in range(0, count, panel):
        stop = min(start + panel, count)
        last = min(stop + look, count)
        outside = [*range(last, count), *range(start if left is None else 0)]
        if outside:
            strip = jnp.concatenate([tiles[g] for g in outside], axis=0)[:, 8 * start : 8 * stop]
            high, middle, low = thirds(strip)
            factors = jnp.concatenate([high, high, middle, high, low, middle], axis=1).astype(BF16)
        for k in range(start, stop):
            first = 8 * k
            block = inside(first, first + 8)
            rows = jnp.where(block, (lane - first == sub).astype(F32), tiles[k])
            ahead = k + 1 < count
            if ahead:
                after = jnp.where(block, 0.0, tiles[k + 1])
                side = [column(tiles[k + 1], first + j) for j in range(8)]
            scale = None
            for p in range(8):
                inverse = pl.reciprocal(row(pivot[p], p), approx=True)
                factor = jnp.where(sub == p, 0.0, pivot[p]) * inverse
                picked = row(rows, p)
                if ahead:
                    edge = side[p]
                    factor_ahead = edge * inverse
                    if p == half:
                        coming = [column(after, first + 8 + j) for j in range(8)]
                    if p >= half:
                        for j in range(8):
                            coming[j] = coming[j] - factor_ahead * row(edge, j)
                    after = after - factor_ahead * picked
                for j in range(p + 1, 8):
                    element = row(pivot[j], p)
                    pivot[j] = pivot[j] - factor * element
                    if ahead:
                        side[j] = side[j] - factor_ahead * element
                rows = rows - factor * picked
                scale = inverse if scale is None else jnp.where(sub == p, inverse, scale)
            rows = rows * scale
            picked = [row(rows, j) for j in range(8)]
            for g in range(start, last):
                if g == k:
                    tiles[g] = rows
                elif g == k + 1:
                    tiles[g] = after
                else:
                    terms = [column(tiles[g], first + j) * picked[j] for j in range(8)]
                    cleared = jnp.where(block, 0.0, tiles[g])
                    tiles[g] = cleared - tree(terms) if count <= panel else minus(cleared, terms)
            if ahead:
                pivot = coming
        solved = jnp.concatenate(tiles[start:stop], axis=0)
        if outside:
            high, middle, low = thirds(solved)
            right = jnp.concatenate([high, middle, high, low, high, middle], axis=0).astype(BF16)
            update = dot(factors, right)
            block = inside(8 * start, 8 * stop)
            for i, g in enumerate(outside):
                tiles[g] = jnp.where(block, 0.0, tiles[g]) - update[8 * i : 8 * i + 8]
        if left is not None:
            blanks = [jnp.zeros((rows, size), BF16) for rows in (8 * start, size - 8 * stop)]
            right = [
                jnp.concatenate([x for x in (blanks[0], part, blanks[1]) if x.shape[0]], axis=0)
                for part in split(solved)
            ]
            columns = lax.broadcasted_iota(jnp.int32, left.shape, 1)
            block = (columns >= 8 * start) & (columns < 8 * stop)
            left = jnp.where(block, 0.0, left) - product(split(left), right)
    return jnp.concatenate(tiles, axis=0) if left is None else left


def build_kernel(label, flag, wave, given, operator, table_at, out, table, one, two, edge, sems):
    size = operator.shape[0]
    middle = LEAF + 128
    copies = [
        pltpu.make_async_copy(source, target, sems.at[i])
        for i, (source, target) in enumerate(
            (
                (operator.at[pl.ds(LEAF, 128)], one),
                (table_at, table),
                (operator.at[pl.ds(middle, size - middle)], two),
                (operator.at[pl.ds(0, LEAF)], edge),
                (given, out),
            )
        )
    ]
    flagged = flag[0, 0] > 0

    @pl.when(jnp.logical_not(flagged))
    def _():
        copies[4].start()
        copies[4].wait()

    @pl.when(flagged)
    def _():
        for copy in copies[:4]:
            copy.start()
        for copy in copies[:2]:
            copy.wait()
        shift = wave[0] * table[pl.ds(label[0, 0], 1), :]
        border, near, far = slice(0, LEAF), slice(LEAF, middle), slice(middle, size)

        def shifted(ref, span):
            block = ref[:, span]
            ids = lax.broadcasted_iota(jnp.int32, block.shape, 0)
            diagonal = ids == lax.broadcasted_iota(jnp.int32, block.shape, 1)
            return block - jnp.where(diagonal, shift[:, span], 0.0)

        right = split(one[:, border]), split(one[:, far])
        inverse = split(spd_inverse(shifted(one, near)))
        for copy in copies[2:4]:
            copy.wait()
        left = split(two[:, near])
        solved_far = split(product(inverse, right[1]))
        inner = shifted(two, far) - product(left, solved_far)
        solved = split(product(inverse, right[0]))
        coupled = split(two[:, border] - product(left, solved))
        left = split(edge[:, near])
        merged = shifted(edge, border) - product(left, solved)
        across = split(edge[:, far] - product(left, solved_far))
        inverse = split(spd_inverse(inner))
        solved = split(product(inverse, coupled))
        out[...] = merged - product(across, solved)


def halves(shape):
    return lax.broadcasted_iota(jnp.int32, shape, 1) < FACE


def turn(tile):
    return pltpu.roll(tile, FACE, 1)


def leaf_rows(place, mine, theirs):
    across, third, lead = place[0], place[1], place[2]
    is_alpha = lead == 0
    left = halves((FACE, 128))

    def load(alpha, block, tile):
        spot = pl.ds(pl.multiple_of(block * FACE, FACE), FACE)
        span = slice(128 * tile, 128 * tile + 128)
        own = is_alpha if alpha else jnp.logical_not(is_alpha)
        return jnp.where(own, mine[spot, span], theirs[spot, span])

    def alpha_rows(block):
        sides = load(True, block, 0)
        ends = load(True, block, 1)
        sides = jnp.where(across == 0, turn(sides), sides)
        tiles = (
            jnp.where(left, sides, 0.0),
            jnp.where(left, jnp.where(third == 0, 0.0, ends), sides),
            jnp.where(left & (third == 0), ends, 0.0),
        )
        return jnp.concatenate(tiles, axis=1), turn(ends)

    def beta_rows(block):
        sides = load(False, block, 0)
        ends = load(False, block, 1)
        other = turn(sides)
        near_far = jnp.where(across == 0, other, sides)
        far_near = jnp.where(across == 0, sides, other)
        flipped = turn(ends)
        tiles = (
            jnp.where(left, 0.0, far_near),
            jnp.where(left & (third == 0), flipped, 0.0),
            jnp.where(
                third == 0,
                jnp.where(left, 0.0, near_far),
                jnp.where(left, far_near, ends),
            ),
        )
        return jnp.concatenate(tiles, axis=1), ends

    return alpha_rows, beta_rows


def either(flag, one, other):
    return [jnp.where(flag, x, y) for x, y in zip(one, other)]


def stacked(one, two, start, stop):
    parts = []
    if start < CUT:
        parts.append(one[start : min(stop, CUT), :])
    if stop > CUT:
        parts.append(two[max(start, CUT) - CUT : stop - CUT, :])
    return jnp.concatenate(parts, axis=0)


def stack(one, two, start, value):
    stop = start + value.shape[0]
    if start < CUT:
        one[start : min(stop, CUT), :] = value[: CUT - start]
    if stop > CUT:
        two[max(start, CUT) - CUT : stop - CUT, :] = value[max(CUT - start, 0) :]


def first_kernel(place, mine, theirs, message_one, message_two, solved_high, solved_low):
    alpha_rows, beta_rows = leaf_rows(place, mine, theirs)
    near = jnp.where(place[0] == 0, 1, 0)
    tiles_a, meet_a = alpha_rows(3)
    tiles_b, meet_b = beta_rows(2)
    system = (meet_a + meet_b)[:, :FACE]
    right = split(tiles_a + tiles_b)
    parts = [alpha_rows(near), beta_rows(near), either(place[1] == 0, beta_rows(3), alpha_rows(2))]
    direct = jnp.concatenate([tiles for tiles, _ in parts], axis=0)
    coupling = split(jnp.concatenate([meet for _, meet in parts], axis=0)[:, :FACE])
    inverse = split(spd_inverse(system, panel=8))
    solved = split(product(inverse, right))
    merged = direct - product(coupling, solved)
    message_one[...] = merged[:, 0:128]
    one = merged[0:128, 128:256]
    message_two[0:64, :] = jnp.where(halves((FACE, 128)), turn(one[0:64]), one[64:128])
    message_two[64:192, :] = merged[0:128, 256:384]
    message_two[192:256, :] = merged[128:192, 128:256]
    message_two[256:320, :] = merged[128:192, 256:384]
    solved_high[...], solved_low[...] = solved


def second_kernel(
    place, own, received, mine, theirs, first_high, first_low, solved_high, solved_low, outer, direct, coupling
):
    alpha_rows, beta_rows = leaf_rows(place, mine, theirs)
    third, lead = place[1], place[2]
    far = jnp.where(place[0] == 0, 0, 1)
    direct[0:64, :], coupling[0:64, :] = alpha_rows(far)
    at_two = alpha_rows(2)
    at_far = beta_rows(far)
    at_three = beta_rows(3)
    direct[64:128, :], coupling[64:128, :] = either(third == 0, at_two, at_far)
    direct[128:192, :], coupling[128:192, :] = either(third == 0, at_far, at_three)
    spot = pl.ds(pl.multiple_of(lead * 96, 32), 96)
    solved = first_high[...], first_low[...]
    rows = direct[spot, :] - product(split(coupling[spot, :][:, :FACE]), solved)
    outer[...] = rows
    faces = own[128:192, :], received[128:192, :]
    is_alpha = place[0] == 0
    left = [*either(is_alpha, faces, faces[::-1]), rows[:, 0:128]]
    system = own[0:128, :] + received[0:128, :]
    solved = spd_inverse(system, jnp.concatenate(left, axis=0))
    solved_high[...], solved_low[...] = split(solved)


def assemble(alpha, beta):
    rows = (alpha or beta)[0].shape[0]
    left = halves((rows, 128))
    blank = jnp.zeros((rows, 128), F32)
    if alpha is None:
        tiles = (
            jnp.where(left, 0.0, turn(beta[0])),
            blank,
            jnp.where(left, 0.0, beta[0]),
            beta[1],
        )
        return jnp.concatenate(tiles, axis=1)
    turned = turn(alpha[1])
    middle = jnp.where(left, turn(alpha[0]), turned)
    if beta is None:
        tiles = jnp.where(left, alpha[0], 0.0), middle, jnp.where(left, turned, 0.0), blank
        return jnp.concatenate(tiles, axis=1)
    tiles = (
        jnp.where(left, alpha[0], turn(beta[0])),
        middle,
        jnp.where(left, turned, beta[0]),
        beta[1],
    )
    return jnp.concatenate(tiles, axis=1)


def near_columns(one, two):
    other = two[0:64, :]
    across = jnp.concatenate([turn(other), other], axis=0)
    faces = jnp.concatenate([one[128:192, :]] * 2, axis=0)
    return jnp.where(halves((128, 128)), jnp.transpose(faces), across)


def exchange_kernel(
    place,
    own_one,
    own_two,
    received_one,
    received_two,
    solved_high,
    solved_low,
    message_one,
    message_two,
    right_high,
    right_low,
):
    is_alpha = place[0] == 0

    def both(mine, other):
        return jnp.where(is_alpha, mine, other), jnp.where(is_alpha, other, mine)

    one = both(near_columns(own_one, own_two), near_columns(received_one, received_two))
    two = both(own_two[64:192, :], received_two[64:192, :])
    face = both(own_two[192:256, :], received_two[192:256, :])
    back = both(own_two[256:320, :], received_two[256:320, :])
    right = split(assemble((one[0], two[0]), (one[1], two[1])))
    direct = jnp.concatenate(
        [assemble((face[0], back[0]), None), assemble(None, (face[1], back[1]))], axis=0
    )
    merged = direct + product((solved_high[0:128, :], solved_low[0:128, :]), right)
    for i in range(4):
        stack(message_one, message_two, 128 * i, merged[:, 128 * i : 128 * i + 128])
    right_high[...], right_low[...] = right


def rest_columns(one, two):
    return jnp.concatenate(
        [stacked(one, two, 128 * i, 128 * i + 128) for i in range(1, 4)], axis=1
    )


def outer_kernel(place, outer, solved_high, solved_low, right_high, right_low, rows):
    mine = outer[:, 128:256], outer[:, 256:384]
    direct = jnp.where(place[0] == 0, assemble(mine, None), assemble(None, mine))
    solved = solved_high[128:224, :], solved_low[128:224, :]
    rows[...] = direct + product(solved, (right_high[...], right_low[...]))


def third_kernel(own_one, own_two, received, rows, half, solved_high, solved_low):
    right = split(rest_columns(own_one, own_two))
    system = own_one[0:128, :] + received[0:128, :]
    solved = split(spd_inverse(system, rows[:, 0:128]))
    half[...] = rows[:, 128:512] + product(solved, right)
    solved_high[...], solved_low[...] = solved


def last_kernel(place, half, received_one, received_two, solved_high, solved_low, out):
    third = place[1]
    width = 6 * FACE
    mine = pl.multiple_of(third * width, 128)
    other = pl.multiple_of((1 - third) * width, 128)
    out[:, pl.ds(mine, width)] = half[...]
    solved = solved_high[...], solved_low[...]
    out[:, pl.ds(other, width)] = product(solved, split(rest_columns(received_one, received_two)))


def shapes(*sizes):
    return [jax.ShapeDtypeStruct(size, F32) for size in sizes]


def pair(*size):
    return [jax.ShapeDtypeStruct(size, BF16)] * 2


def run(kernel, out_shape, *operands, scalars=1, **options):
    smem = pl.BlockSpec(memory_space=pltpu.SMEM)
    vmem = pl.BlockSpec(memory_space=pltpu.VMEM)
    return pl.pallas_call(
        kernel,
        out_shape=out_shape,
        in_specs=[smem] * scalars + [vmem] * (len(operands) - scalars),
        out_specs=[vmem] * len(out_shape),
        compiler_params=pltpu.CompilerParams(vmem_limit_bytes=32 * 1024 * 1024),
        **options,
    )(*operands)


def body(leaf_maps, leaf_operator, region_eps, wave_sq, region_labels, build_flags):
    across = lax.axis_index("bx") % 2
    upward = lax.axis_index("by")
    place = jnp.stack([across, upward // 2 % 2, upward % 2]).astype(jnp.int32)
    size = leaf_operator.shape[0]
    mine = pl.pallas_call(
        build_kernel,
        out_shape=jax.ShapeDtypeStruct((LEAF, LEAF), F32),
        in_specs=[pl.BlockSpec(memory_space=pltpu.SMEM)] * 3
        + [pl.BlockSpec(memory_space=pltpu.HBM)] * 3,
        out_specs=pl.BlockSpec(memory_space=pltpu.VMEM),
        scratch_shapes=[
            pltpu.VMEM(region_eps.shape, F32),
            pltpu.VMEM((128, size), F32),
            pltpu.VMEM((size - LEAF - 128, size), F32),
            pltpu.VMEM((LEAF, size), F32),
            pltpu.SemaphoreType.DMA((5,)),
        ],
        compiler_params=pltpu.CompilerParams(vmem_limit_bytes=32 * 1024 * 1024),
        name="leaf_build",
    )(
        region_labels,
        build_flags,
        wave_sq,
        *(
            pltpu.with_memory_space_constraint(x, pltpu.HBM)
            for x in (leaf_maps[0, 0], leaf_operator, region_eps)
        ),
    )
    theirs = swapped(mine, "by", 0)
    one, two, *solved = run(
        first_kernel,
        shapes((192, 128), (320, 128)) + pair(FACE, 6 * FACE),
        place,
        mine,
        theirs,
        name="first_merge",
    )
    received_one = swapped(one, "bx", 0)
    received_two = swapped(two, "bx", 0)
    *solved, outer = run(
        second_kernel,
        pair(224, 128) + shapes((96, 6 * FACE)),
        place,
        one,
        received_one,
        mine,
        theirs,
        *solved,
        scratch_shapes=[pltpu.VMEM((192, 6 * FACE), F32), pltpu.VMEM((192, 128), F32)],
        cost_estimate=LONG,
        name="second_inverse",
    )
    one, two, *right = run(
        exchange_kernel,
        shapes((CUT, 128), (512 - CUT, 128)) + pair(128, 8 * FACE),
        place,
        one,
        two,
        received_one,
        received_two,
        *solved,
        name="second_merge",
    )
    received_one = swapped(one, "by", 1)
    received_two = swapped(two, "by", 1)
    (rows,) = run(
        outer_kernel, shapes((96, 8 * FACE)), place, outer, *solved, *right, name="second_rows"
    )
    half, *solved = run(
        third_kernel,
        shapes((96, 6 * FACE)) + pair(96, 128),
        one,
        two,
        received_one,
        rows,
        scalars=0,
        cost_estimate=LONG,
        name="third_inverse",
    )
    (result,) = run(
        last_kernel,
        shapes((96, 12 * FACE)),
        place,
        half,
        received_one,
        received_two,
        *solved,
        name="third_merge",
    )
    return result.reshape((1, 1, 96, 12 * FACE))


def solution(mesh):
    placed = (
        P(("freq", "bx"), "by", None, None),
        P(),
        P(),
        P("freq"),
        P("bx", "by"),
        P("bx", "by"),
    )
    return jax.shard_map(
        body,
        mesh=mesh,
        in_specs=placed,
        out_specs=P(("freq", "bx"), "by", None, None),
        check_vma=False,
    )
```

```python
import jax
import jax.numpy as jnp
from jax import lax
from jax.experimental import pallas as pl
from jax.experimental.pallas import tpu as pltpu
from jax.sharding import PartitionSpec as P

FACE = 64
LEAF = 4 * FACE
CUT_TWO, CUT_THREE = 160, 128
F32 = jnp.float32
BF16 = jnp.bfloat16


LONG = pl.CostEstimate(flops=10**10, bytes_accessed=10**8, transcendentals=10**6)


def swapped(shard, axis, stride):
    return lax.ppermute(shard, axis, [(i, i ^ 1 << stride) for i in range(lax.axis_size(axis))])


def split(x):
    high = x.astype(BF16)
    return high, (x - high.astype(F32)).astype(BF16)


def thirds(x):
    high = x.astype(BF16).astype(F32)
    rest = x - high
    middle = rest.astype(BF16).astype(F32)
    return high, middle, (rest - middle).astype(BF16).astype(F32)


def dot(a, b):
    return jnp.dot(a, b, preferred_element_type=F32)


def product(a, b):
    (a_high, a_low), (b_high, b_low) = a, b
    depth = a_high.shape[1]
    if depth % 128 and depth != FACE:
        return dot(a_high, b_high) + (dot(a_high, b_low) + dot(a_low, b_high))
    twice = dot(
        jnp.concatenate([a_high, a_low], axis=1), jnp.concatenate([b_high, b_high], axis=0)
    )
    return twice + dot(a_high, b_low)


def tree(terms):
    while len(terms) > 1:
        terms = [x + y for x, y in zip(terms[::2], terms[1::2])]
    return terms[0]


def minus(value, terms):
    for term in terms:
        value = value - term
    return value


def spd_inverse(matrix, left=None, panel=4, look=4, half=4):
    size = matrix.shape[0]
    shape = (8, size)
    count = size // 8
    tiles = [matrix[8 * g : 8 * g + 8] for g in range(count)]
    lane = lax.broadcasted_iota(jnp.int32, shape, 1)
    sub = lax.broadcasted_iota(jnp.int32, shape, 0)

    def column(tile, c):
        return jnp.broadcast_to(tile[:, c : c + 1], shape)

    def row(tile, r):
        return jnp.broadcast_to(tile[r : r + 1, :], shape)

    def inside(start, stop):
        return (lane >= start) & (lane < stop)

    pivot = [column(tiles[0], j) for j in range(8)]
    for start in range(0, count, panel):
        stop = min(start + panel, count)
        last = min(stop + look, count)
        outside = [*range(last, count), *range(start if left is None else 0)]
        if outside:
            strip = jnp.concatenate([tiles[g] for g in outside], axis=0)[:, 8 * start : 8 * stop]
            high, middle, low = thirds(strip)
            factors = jnp.concatenate([high, high, middle, high, low, middle], axis=1).astype(BF16)
        for k in range(start, stop):
            first = 8 * k
            block = inside(first, first + 8)
            rows = jnp.where(block, (lane - first == sub).astype(F32), tiles[k])
            ahead = k + 1 < count
            if ahead:
                after = jnp.where(block, 0.0, tiles[k + 1])
                side = [column(tiles[k + 1], first + j) for j in range(8)]
            scale = None
            for p in range(8):
                inverse = pl.reciprocal(row(pivot[p], p), approx=True)
                factor = jnp.where(sub == p, 0.0, pivot[p]) * inverse
                picked = row(rows, p)
                if ahead:
                    edge = side[p]
                    factor_ahead = edge * inverse
                    if p == half:
                        coming = [column(after, first + 8 + j) for j in range(8)]
                    if p >= half:
                        for j in range(8):
                            coming[j] = coming[j] - factor_ahead * row(edge, j)
                    after = after - factor_ahead * picked
                for j in range(p + 1, 8):
                    element = row(pivot[j], p)
                    pivot[j] = pivot[j] - factor * element
                    if ahead:
                        side[j] = side[j] - factor_ahead * element
                rows = rows - factor * picked
                scale = inverse if scale is None else jnp.where(sub == p, inverse, scale)
            rows = rows * scale
            picked = [row(rows, j) for j in range(8)]
            for g in range(start, last):
                if g == k:
                    tiles[g] = rows
                elif g == k + 1:
                    tiles[g] = after
                else:
                    terms = [column(tiles[g], first + j) * picked[j] for j in range(8)]
                    cleared = jnp.where(block, 0.0, tiles[g])
                    tiles[g] = cleared - tree(terms) if count <= panel else minus(cleared, terms)
            if ahead:
                pivot = coming
        solved = jnp.concatenate(tiles[start:stop], axis=0)
        if outside:
            high, middle, low = thirds(solved)
            right = jnp.concatenate([high, middle, high, low, high, middle], axis=0).astype(BF16)
            update = dot(factors, right)
            block = inside(8 * start, 8 * stop)
            for i, g in enumerate(outside):
                tiles[g] = jnp.where(block, 0.0, tiles[g]) - update[8 * i : 8 * i + 8]
        if left is not None:
            blanks = [jnp.zeros((rows, size), BF16) for rows in (8 * start, size - 8 * stop)]
            right = [
                jnp.concatenate([x for x in (blanks[0], part, blanks[1]) if x.shape[0]], axis=0)
                for part in split(solved)
            ]
            columns = lax.broadcasted_iota(jnp.int32, left.shape, 1)
            block = (columns >= 8 * start) & (columns < 8 * stop)
            left = jnp.where(block, 0.0, left) - product(split(left), right)
    return jnp.concatenate(tiles, axis=0) if left is None else left


def build_kernel(label, flag, wave, given, operator, table_at, out, table, one, two, edge, sems):
    size = operator.shape[0]
    middle = LEAF + 128
    copies = [
        pltpu.make_async_copy(source, target, sems.at[i])
        for i, (source, target) in enumerate(
            (
                (operator.at[pl.ds(LEAF, 128)], one),
                (table_at, table),
                (operator.at[pl.ds(middle, size - middle)], two),
                (operator.at[pl.ds(0, LEAF)], edge),
                (given, out),
            )
        )
    ]
    flagged = flag[0, 0] > 0

    @pl.when(jnp.logical_not(flagged))
    def _():
        copies[4].start()
        copies[4].wait()

    @pl.when(flagged)
    def _():
        for copy in copies[:4]:
            copy.start()
        for copy in copies[:2]:
            copy.wait()
        shift = wave[0] * table[pl.ds(label[0, 0], 1), :]
        border, near, far = slice(0, LEAF), slice(LEAF, middle), slice(middle, size)

        def shifted(ref, span):
            block = ref[:, span]
            ids = lax.broadcasted_iota(jnp.int32, block.shape, 0)
            diagonal = ids == lax.broadcasted_iota(jnp.int32, block.shape, 1)
            return block - jnp.where(diagonal, shift[:, span], 0.0)

        right = split(one[:, border]), split(one[:, far])
        inverse = split(spd_inverse(shifted(one, near)))
        for copy in copies[2:4]:
            copy.wait()
        left = split(two[:, near])
        solved_far = split(product(inverse, right[1]))
        inner = shifted(two, far) - product(left, solved_far)
        solved = split(product(inverse, right[0]))
        coupled = split(two[:, border] - product(left, solved))
        left = split(edge[:, near])
        merged = shifted(edge, border) - product(left, solved)
        across = split(edge[:, far] - product(left, solved_far))
        inverse = split(spd_inverse(inner))
        solved = split(product(inverse, coupled))
        out[...] = merged - product(across, solved)


def halves(shape):
    return lax.broadcasted_iota(jnp.int32, shape, 1) < FACE


def turn(tile):
    return pltpu.roll(tile, FACE, 1)


def leaf_rows(place, mine, theirs):
    across, third, lead = place[0], place[1], place[2]
    is_alpha = lead == 0
    left = halves((FACE, 128))

    def load(alpha, block, tile):
        spot = pl.ds(pl.multiple_of(block * FACE, FACE), FACE)
        span = slice(128 * tile, 128 * tile + 128)
        own = is_alpha if alpha else jnp.logical_not(is_alpha)
        return jnp.where(own, mine[spot, span], theirs[spot, span])

    def alpha_rows(block):
        sides = load(True, block, 0)
        ends = load(True, block, 1)
        sides = jnp.where(across == 0, turn(sides), sides)
        tiles = (
            jnp.where(left, sides, 0.0),
            jnp.where(left, jnp.where(third == 0, 0.0, ends), sides),
            jnp.where(left & (third == 0), ends, 0.0),
        )
        return jnp.concatenate(tiles, axis=1), turn(ends)

    def beta_rows(block):
        sides = load(False, block, 0)
        ends = load(False, block, 1)
        other = turn(sides)
        near_far = jnp.where(across == 0, other, sides)
        far_near = jnp.where(across == 0, sides, other)
        flipped = turn(ends)
        tiles = (
            jnp.where(left, 0.0, far_near),
            jnp.where(left & (third == 0), flipped, 0.0),
            jnp.where(
                third == 0,
                jnp.where(left, 0.0, near_far),
                jnp.where(left, far_near, ends),
            ),
        )
        return jnp.concatenate(tiles, axis=1), ends

    return alpha_rows, beta_rows


def either(flag, one, other):
    return [jnp.where(flag, x, y) for x, y in zip(one, other)]


def stacked(one, two, start, stop):
    cut = one.shape[0]
    parts = []
    if start < cut:
        parts.append(one[start : min(stop, cut), :])
    if stop > cut:
        parts.append(two[max(start, cut) - cut : stop - cut, :])
    return jnp.concatenate(parts, axis=0)


def stack(one, two, start, value):
    cut = one.shape[0]
    stop = start + value.shape[0]
    if start < cut:
        one[start : min(stop, cut), :] = value[: cut - start]
    if stop > cut:
        two[max(start, cut) - cut : stop - cut, :] = value[max(cut - start, 0) :]


def first_kernel(place, mine, theirs, message_one, message_two, link, solved_high, solved_low):
    alpha_rows, beta_rows = leaf_rows(place, mine, theirs)
    near = jnp.where(place[0] == 0, 1, 0)
    tiles_a, meet_a = alpha_rows(3)
    tiles_b, meet_b = beta_rows(2)
    system = (meet_a + meet_b)[:, :FACE]
    right = split(tiles_a + tiles_b)
    parts = [alpha_rows(near), beta_rows(near), either(place[1] == 0, beta_rows(3), alpha_rows(2))]
    direct = jnp.concatenate([tiles for tiles, _ in parts], axis=0)
    coupling = split(jnp.concatenate([meet for _, meet in parts], axis=0)[:, :FACE])
    inverse = split(spd_inverse(system, panel=8))
    solved = split(product(inverse, right))
    merged = direct - product(coupling, solved)
    for i in range(3):
        stack(message_one, message_two, 128 * i, merged[0:128, 128 * i : 128 * i + 128])
    stack(message_one, message_two, 384, merged[128:192, 128:256])
    stack(message_one, message_two, 448, merged[128:192, 256:384])
    link[...] = merged[128:192, 0:128]
    solved_high[...], solved_low[...] = solved


def rows_kernel(place, mine, theirs, solved_high, solved_low, outer, direct, coupling):
    alpha_rows, beta_rows = leaf_rows(place, mine, theirs)
    third, lead = place[1], place[2]
    far = jnp.where(place[0] == 0, 0, 1)
    direct[0:64, :], coupling[0:64, :] = alpha_rows(far)
    at_two = alpha_rows(2)
    at_far = beta_rows(far)
    at_three = beta_rows(3)
    direct[64:128, :], coupling[64:128, :] = either(third == 0, at_two, at_far)
    direct[128:192, :], coupling[128:192, :] = either(third == 0, at_far, at_three)
    spot = pl.ds(pl.multiple_of(lead * 96, 32), 96)
    solved = solved_high[...], solved_low[...]
    outer[...] = direct[spot, :] - product(split(coupling[spot, :][:, :FACE]), solved)


def second_kernel(own, received, outer, inverse_high, inverse_low, outer_high, outer_low):
    outer_high[...], outer_low[...] = split(outer[:, 0:128])
    system = own[0:128, :] + received[0:128, :]
    inverse_high[...], inverse_low[...] = split(spd_inverse(system))


def assemble(alpha, beta):
    rows = (alpha or beta)[0].shape[0]
    left = halves((rows, 128))
    blank = jnp.zeros((rows, 128), F32)
    if alpha is None:
        tiles = (
            jnp.where(left, 0.0, turn(beta[0])),
            blank,
            jnp.where(left, 0.0, beta[0]),
            beta[1],
        )
        return jnp.concatenate(tiles, axis=1)
    turned = turn(alpha[1])
    middle = jnp.where(left, turn(alpha[0]), turned)
    if beta is None:
        tiles = jnp.where(left, alpha[0], 0.0), middle, jnp.where(left, turned, 0.0), blank
        return jnp.concatenate(tiles, axis=1)
    tiles = (
        jnp.where(left, alpha[0], turn(beta[0])),
        middle,
        jnp.where(left, turned, beta[0]),
        beta[1],
    )
    return jnp.concatenate(tiles, axis=1)


def exchange_kernel(
    place,
    own_one,
    own_two,
    received_one,
    received_two,
    link,
    inverse_high,
    inverse_low,
    message_one,
    message_two,
    right_high,
    right_low,
):
    is_alpha = place[0] == 0

    def both(mine, other):
        return jnp.where(is_alpha, mine, other), jnp.where(is_alpha, other, mine)

    def part(start, stop):
        return both(stacked(own_one, own_two, start, stop), stacked(received_one, received_two, start, stop))

    one, two = part(128, 256), part(256, 384)
    right = split(assemble((one[0], two[0]), (one[1], two[1])))
    face, back = part(384, 448), part(448, 512)
    direct = jnp.concatenate(
        [assemble((face[0], back[0]), None), assemble(None, (face[1], back[1]))], axis=0
    )
    mine = link[...]
    other = jnp.transpose(stacked(received_one, received_two, 128, 256))[0:FACE]
    coupling = jnp.concatenate(
        [jnp.where(is_alpha, mine, other), jnp.where(is_alpha, other, mine)], axis=0
    )
    solved = split(product(split(coupling), (inverse_high[...], inverse_low[...])))
    merged = direct - product(solved, right)
    for i in range(4):
        stack(message_one, message_two, 128 * i, merged[:, 128 * i : 128 * i + 128])
    right_high[...], right_low[...] = right


def rest_columns(one, two):
    return jnp.concatenate(
        [stacked(one, two, 128 * i, 128 * i + 128) for i in range(1, 4)], axis=1
    )


def outer_kernel(place, outer, outer_high, outer_low, inverse_high, inverse_low, right_high, right_low, rows):
    mine = outer[:, 128:256], outer[:, 256:384]
    direct = jnp.where(place[0] == 0, assemble(mine, None), assemble(None, mine))
    solved = split(product((outer_high[...], outer_low[...]), (inverse_high[...], inverse_low[...])))
    rows[...] = direct - product(solved, (right_high[...], right_low[...]))


def third_kernel(own_one, own_two, received, rows, half, solved_high, solved_low):
    right = split(rest_columns(own_one, own_two))
    system = own_one[0:128, :] + received[0:128, :]
    solved = split(spd_inverse(system, rows[:, 0:128]))
    half[...] = rows[:, 128:512] + product(solved, right)
    solved_high[...], solved_low[...] = solved


def last_kernel(place, half, received_one, received_two, solved_high, solved_low, out):
    third = place[1]
    width = 6 * FACE
    mine = pl.multiple_of(third * width, 128)
    other = pl.multiple_of((1 - third) * width, 128)
    out[:, pl.ds(mine, width)] = half[...]
    solved = solved_high[...], solved_low[...]
    out[:, pl.ds(other, width)] = product(solved, split(rest_columns(received_one, received_two)))


def shapes(*sizes):
    return [jax.ShapeDtypeStruct(size, F32) for size in sizes]


def pair(*size):
    return [jax.ShapeDtypeStruct(size, BF16)] * 2


def run(kernel, out_shape, *operands, scalars=1, **options):
    smem = pl.BlockSpec(memory_space=pltpu.SMEM)
    vmem = pl.BlockSpec(memory_space=pltpu.VMEM)
    return pl.pallas_call(
        kernel,
        out_shape=out_shape,
        in_specs=[smem] * scalars + [vmem] * (len(operands) - scalars),
        out_specs=[vmem] * len(out_shape),
        compiler_params=pltpu.CompilerParams(vmem_limit_bytes=32 * 1024 * 1024),
        **options,
    )(*operands)


def body(leaf_maps, leaf_operator, region_eps, wave_sq, region_labels, build_flags):
    across = lax.axis_index("bx") % 2
    upward = lax.axis_index("by")
    place = jnp.stack([across, upward // 2 % 2, upward % 2]).astype(jnp.int32)
    size = leaf_operator.shape[0]
    mine = pl.pallas_call(
        build_kernel,
        out_shape=jax.ShapeDtypeStruct((LEAF, LEAF), F32),
        in_specs=[pl.BlockSpec(memory_space=pltpu.SMEM)] * 3
        + [pl.BlockSpec(memory_space=pltpu.HBM)] * 3,
        out_specs=pl.BlockSpec(memory_space=pltpu.VMEM),
        scratch_shapes=[
            pltpu.VMEM(region_eps.shape, F32),
            pltpu.VMEM((128, size), F32),
            pltpu.VMEM((size - LEAF - 128, size), F32),
            pltpu.VMEM((LEAF, size), F32),
            pltpu.SemaphoreType.DMA((5,)),
        ],
        compiler_params=pltpu.CompilerParams(vmem_limit_bytes=32 * 1024 * 1024),
        name="leaf_build",
    )(
        region_labels,
        build_flags,
        wave_sq,
        *(
            pltpu.with_memory_space_constraint(x, pltpu.HBM)
            for x in (leaf_maps[0, 0], leaf_operator, region_eps)
        ),
    )
    theirs = swapped(mine, "by", 0)
    one, two, link, *solved = run(
        first_kernel,
        shapes((CUT_TWO, 128), (512 - CUT_TWO, 128), (FACE, 128)) + pair(FACE, 6 * FACE),
        place,
        mine,
        theirs,
        name="first_merge",
    )
    received_one = swapped(one, "bx", 0)
    received_two = swapped(two, "bx", 0)
    (outer,) = run(
        rows_kernel,
        shapes((96, 6 * FACE)),
        place,
        mine,
        theirs,
        *solved,
        scratch_shapes=[pltpu.VMEM((192, 6 * FACE), F32), pltpu.VMEM((192, 128), F32)],
        name="first_rows",
    )
    *inverse, outer_high, outer_low = run(
        second_kernel,
        pair(128, 128) + pair(96, 128),
        one,
        received_one,
        outer,
        scalars=0,
        cost_estimate=LONG,
        name="second_inverse",
    )
    one, two, *right = run(
        exchange_kernel,
        shapes((CUT_THREE, 128), (512 - CUT_THREE, 128)) + pair(128, 8 * FACE),
        place,
        one,
        two,
        received_one,
        received_two,
        link,
        *inverse,
        name="second_merge",
    )
    received_one = swapped(one, "by", 1)
    received_two = swapped(two, "by", 1)
    (rows,) = run(
        outer_kernel,
        shapes((96, 8 * FACE)),
        place,
        outer,
        outer_high,
        outer_low,
        *inverse,
        *right,
        name="second_rows",
    )
    half, *solved = run(
        third_kernel,
        shapes((96, 6 * FACE)) + pair(96, 128),
        one,
        two,
        received_one,
        rows,
        scalars=0,
        cost_estimate=LONG,
        name="third_inverse",
    )
    (result,) = run(
        last_kernel,
        shapes((96, 12 * FACE)),
        place,
        half,
        received_one,
        received_two,
        *solved,
        name="third_merge",
    )
    return result.reshape((1, 1, 96, 12 * FACE))


def solution(mesh):
    placed = (
        P(("freq", "bx"), "by", None, None),
        P(),
        P(),
        P("freq"),
        P("bx", "by"),
        P("bx", "by"),
    )
    return jax.shard_map(
        body,
        mesh=mesh,
        in_specs=placed,
        out_specs=P(("freq", "bx"), "by", None, None),
        check_vma=False,
    )
```

```python
import jax
import jax.numpy as jnp
from jax import lax
from jax.experimental import pallas as pl
from jax.experimental.pallas import tpu as pltpu
from jax.sharding import PartitionSpec as P

FACE = 64
LEAF = 4 * FACE
CUT_TWO, CUT_THREE = 240, 128
F32 = jnp.float32
BF16 = jnp.bfloat16


LONG = pl.CostEstimate(flops=10**10, bytes_accessed=10**8, transcendentals=10**6)


def swapped(shard, axis, stride):
    return lax.ppermute(shard, axis, [(i, i ^ 1 << stride) for i in range(lax.axis_size(axis))])


def split(x):
    high = x.astype(BF16)
    return high, (x - high.astype(F32)).astype(BF16)


def thirds(x):
    high = x.astype(BF16).astype(F32)
    rest = x - high
    middle = rest.astype(BF16).astype(F32)
    return high, middle, (rest - middle).astype(BF16).astype(F32)


def dot(a, b):
    return jnp.dot(a, b, preferred_element_type=F32)


def product(a, b):
    (a_high, a_low), (b_high, b_low) = a, b
    depth = a_high.shape[1]
    if depth % 128 and depth != FACE:
        return dot(a_high, b_high) + (dot(a_high, b_low) + dot(a_low, b_high))
    twice = dot(
        jnp.concatenate([a_high, a_low], axis=1), jnp.concatenate([b_high, b_high], axis=0)
    )
    return twice + dot(a_high, b_low)


def tree(terms):
    while len(terms) > 1:
        terms = [x + y for x, y in zip(terms[::2], terms[1::2])]
    return terms[0]


def minus(value, terms):
    for term in terms:
        value = value - term
    return value


def spd_inverse(matrix, left=None, both=False, panel=4, look=4, half=4):
    size = matrix.shape[0]
    shape = (8, size)
    count = size // 8
    tiles = [matrix[8 * g : 8 * g + 8] for g in range(count)]
    lane = lax.broadcasted_iota(jnp.int32, shape, 1)
    sub = lax.broadcasted_iota(jnp.int32, shape, 0)

    def column(tile, c):
        return jnp.broadcast_to(tile[:, c : c + 1], shape)

    def row(tile, r):
        return jnp.broadcast_to(tile[r : r + 1, :], shape)

    def inside(start, stop):
        return (lane >= start) & (lane < stop)

    pivot = [column(tiles[0], j) for j in range(8)]
    head = row(pivot[0], 0)
    for start in range(0, count, panel):
        stop = min(start + panel, count)
        last = min(stop + look, count)
        outside = [*range(last, count), *range(start if left is None or both else 0)]
        if outside:
            strip = jnp.concatenate([tiles[g] for g in outside], axis=0)[:, 8 * start : 8 * stop]
            high, middle, low = thirds(strip)
            factors = jnp.concatenate([high, high, middle, high, low, middle], axis=1).astype(BF16)
        for k in range(start, stop):
            first = 8 * k
            block = inside(first, first + 8)
            rows = jnp.where(block, (lane - first == sub).astype(F32), tiles[k])
            ahead = k + 1 < count
            if ahead:
                after = jnp.where(block, 0.0, tiles[k + 1])
                side = [column(tiles[k + 1], first + j) for j in range(8)]
            scale = None
            for p in range(8):
                inverse = pl.reciprocal(head, approx=True)
                if p < 7:
                    element = row(pivot[p + 1], p)
                    head = row(pivot[p + 1], p + 1) - element * (element * inverse)
                factor = jnp.where(sub == p, 0.0, pivot[p]) * inverse
                picked = row(rows, p)
                if ahead:
                    edge = side[p]
                    factor_ahead = edge * inverse
                    if p == half:
                        coming = [column(after, first + 8 + j) for j in range(8)]
                    if p == 7:
                        element = row(edge, 0)
                        head = row(coming[0], 0) - element * (element * inverse)
                    if p >= half:
                        for j in range(8):
                            coming[j] = coming[j] - factor_ahead * row(edge, j)
                    after = after - factor_ahead * picked
                for j in range(p + 1, 8):
                    element = row(pivot[j], p)
                    pivot[j] = pivot[j] - factor * element
                    if ahead:
                        side[j] = side[j] - factor_ahead * element
                rows = rows - factor * picked
                scale = inverse if scale is None else jnp.where(sub == p, inverse, scale)
            rows = rows * scale
            picked = [row(rows, j) for j in range(8)]
            for g in range(start, last):
                if g == k:
                    tiles[g] = rows
                elif g == k + 1:
                    tiles[g] = after
                else:
                    terms = [column(tiles[g], first + j) * picked[j] for j in range(8)]
                    cleared = jnp.where(block, 0.0, tiles[g])
                    tiles[g] = cleared - tree(terms) if count <= panel else minus(cleared, terms)
            if ahead:
                pivot = coming
        solved = jnp.concatenate(tiles[start:stop], axis=0)
        if outside:
            high, middle, low = thirds(solved)
            right = jnp.concatenate([high, middle, high, low, high, middle], axis=0).astype(BF16)
            update = dot(factors, right)
            block = inside(8 * start, 8 * stop)
            for i, g in enumerate(outside):
                tiles[g] = jnp.where(block, 0.0, tiles[g]) - update[8 * i : 8 * i + 8]
        if left is not None:
            blanks = [jnp.zeros((rows, size), BF16) for rows in (8 * start, size - 8 * stop)]
            right = [
                jnp.concatenate([x for x in (blanks[0], part, blanks[1]) if x.shape[0]], axis=0)
                for part in split(solved)
            ]
            columns = lax.broadcasted_iota(jnp.int32, left.shape, 1)
            block = (columns >= 8 * start) & (columns < 8 * stop)
            left = jnp.where(block, 0.0, left) - product(split(left), right)
    if left is not None and not both:
        return left
    whole = jnp.concatenate(tiles, axis=0)
    return (whole, left) if both else whole


def build_kernel(label, flag, wave, given, operator, table_at, out, table, one, two, edge, sems):
    size = operator.shape[0]
    middle = LEAF + 128
    copies = [
        pltpu.make_async_copy(source, target, sems.at[i])
        for i, (source, target) in enumerate(
            (
                (operator.at[pl.ds(LEAF, 128)], one),
                (table_at, table),
                (operator.at[pl.ds(middle, size - middle)], two),
                (operator.at[pl.ds(0, LEAF)], edge),
                (given, out),
            )
        )
    ]
    flagged = flag[0, 0] > 0

    @pl.when(jnp.logical_not(flagged))
    def _():
        copies[4].start()
        copies[4].wait()

    @pl.when(flagged)
    def _():
        for copy in copies[:4]:
            copy.start()
        for copy in copies[:2]:
            copy.wait()
        shift = wave[0] * table[pl.ds(label[0, 0], 1), :]
        border, near, far = slice(0, LEAF), slice(LEAF, middle), slice(middle, size)

        def shifted(ref, span):
            block = ref[:, span]
            ids = lax.broadcasted_iota(jnp.int32, block.shape, 0)
            diagonal = ids == lax.broadcasted_iota(jnp.int32, block.shape, 1)
            return block - jnp.where(diagonal, shift[:, span], 0.0)

        right = split(one[:, border]), split(one[:, far])
        copies[2].wait()
        inverse, left = spd_inverse(shifted(one, near), two[:, near], both=True)
        copies[3].wait()
        left = split(left)
        inner = shifted(two, far) + product(left, right[1])
        coupled = split(two[:, border] + product(left, right[0]))
        left = split(edge[:, near])
        left = split(product(left, split(inverse)))
        merged = shifted(edge, border) - product(left, right[0])
        across = split(edge[:, far] - product(left, right[1]))
        inverse = split(spd_inverse(inner))
        solved = split(product(inverse, coupled))
        out[...] = merged - product(across, solved)


def halves(shape):
    return lax.broadcasted_iota(jnp.int32, shape, 1) < FACE


def turn(tile):
    return pltpu.roll(tile, FACE, 1)


def leaf_rows(place, mine, theirs):
    across, third, lead = place[0], place[1], place[2]
    is_alpha = lead == 0
    left = halves((FACE, 128))

    def load(alpha, block, tile):
        spot = pl.ds(pl.multiple_of(block * FACE, FACE), FACE)
        span = slice(128 * tile, 128 * tile + 128)
        own = is_alpha if alpha else jnp.logical_not(is_alpha)
        return jnp.where(own, mine[spot, span], theirs[spot, span])

    def alpha_rows(block):
        sides = load(True, block, 0)
        ends = load(True, block, 1)
        sides = jnp.where(across == 0, turn(sides), sides)
        tiles = (
            jnp.where(left, sides, 0.0),
            jnp.where(left, jnp.where(third == 0, 0.0, ends), sides),
            jnp.where(left & (third == 0), ends, 0.0),
        )
        return jnp.concatenate(tiles, axis=1), turn(ends)

    def beta_rows(block):
        sides = load(False, block, 0)
        ends = load(False, block, 1)
        other = turn(sides)
        near_far = jnp.where(across == 0, other, sides)
        far_near = jnp.where(across == 0, sides, other)
        flipped = turn(ends)
        tiles = (
            jnp.where(left, 0.0, far_near),
            jnp.where(left & (third == 0), flipped, 0.0),
            jnp.where(
                third == 0,
                jnp.where(left, 0.0, near_far),
                jnp.where(left, far_near, ends),
            ),
        )
        return jnp.concatenate(tiles, axis=1), ends

    return alpha_rows, beta_rows


def either(flag, one, other):
    return [jnp.where(flag, x, y) for x, y in zip(one, other)]


def stacked(one, two, start, stop):
    cut = one.shape[0]
    parts = []
    if start < cut:
        parts.append(one[start : min(stop, cut), :])
    if stop > cut:
        parts.append(two[max(start, cut) - cut : stop - cut, :])
    return jnp.concatenate(parts, axis=0)


def stack(one, two, start, value):
    cut = one.shape[0]
    stop = start + value.shape[0]
    if start < cut:
        one[start : min(stop, cut), :] = value[: cut - start]
    if stop > cut:
        two[max(start, cut) - cut : stop - cut, :] = value[max(cut - start, 0) :]


def first_kernel(place, mine, theirs, message_one, message_two, link, solved_high, solved_low):
    alpha_rows, beta_rows = leaf_rows(place, mine, theirs)
    near = jnp.where(place[0] == 0, 1, 0)
    tiles_a, meet_a = alpha_rows(3)
    tiles_b, meet_b = beta_rows(2)
    system = (meet_a + meet_b)[:, :FACE]
    right = split(tiles_a + tiles_b)
    parts = [alpha_rows(near), beta_rows(near), either(place[1] == 0, beta_rows(3), alpha_rows(2))]
    direct = jnp.concatenate([tiles for tiles, _ in parts], axis=0)
    coupling = split(jnp.concatenate([meet for _, meet in parts], axis=0)[:, :FACE])
    inverse = split(spd_inverse(system, panel=8))
    solved = split(product(inverse, right))
    merged = direct - product(coupling, solved)
    for i in range(3):
        stack(message_one, message_two, 128 * i, merged[0:128, 128 * i : 128 * i + 128])
    stack(message_one, message_two, 384, merged[128:192, 128:256])
    stack(message_one, message_two, 448, merged[128:192, 256:384])
    link[...] = merged[128:192, 0:128]
    solved_high[...], solved_low[...] = solved


def rows_kernel(place, mine, theirs, solved_high, solved_low, outer, direct, coupling):
    alpha_rows, beta_rows = leaf_rows(place, mine, theirs)
    third, lead = place[1], place[2]
    far = jnp.where(place[0] == 0, 0, 1)
    direct[0:64, :], coupling[0:64, :] = alpha_rows(far)
    at_two = alpha_rows(2)
    at_far = beta_rows(far)
    at_three = beta_rows(3)
    direct[64:128, :], coupling[64:128, :] = either(third == 0, at_two, at_far)
    direct[128:192, :], coupling[128:192, :] = either(third == 0, at_far, at_three)
    spot = pl.ds(pl.multiple_of(lead * 96, 32), 96)
    solved = solved_high[...], solved_low[...]
    outer[...] = direct[spot, :] - product(split(coupling[spot, :][:, :FACE]), solved)


def second_kernel(own, received, outer, inverse_high, inverse_low, outer_high, outer_low):
    outer_high[...], outer_low[...] = split(outer[:, 0:128])
    system = own[0:128, :] + received[0:128, :]
    inverse_high[...], inverse_low[...] = split(spd_inverse(system))


def assemble(alpha, beta):
    rows = (alpha or beta)[0].shape[0]
    left = halves((rows, 128))
    blank = jnp.zeros((rows, 128), F32)
    if alpha is None:
        tiles = (
            jnp.where(left, 0.0, turn(beta[0])),
            blank,
            jnp.where(left, 0.0, beta[0]),
            beta[1],
        )
        return jnp.concatenate(tiles, axis=1)
    turned = turn(alpha[1])
    middle = jnp.where(left, turn(alpha[0]), turned)
    if beta is None:
        tiles = jnp.where(left, alpha[0], 0.0), middle, jnp.where(left, turned, 0.0), blank
        return jnp.concatenate(tiles, axis=1)
    tiles = (
        jnp.where(left, alpha[0], turn(beta[0])),
        middle,
        jnp.where(left, turned, beta[0]),
        beta[1],
    )
    return jnp.concatenate(tiles, axis=1)


def exchange_kernel(
    place,
    own_one,
    own_two,
    received_one,
    received_two,
    link,
    inverse_high,
    inverse_low,
    message_one,
    message_two,
    right_high,
    right_low,
):
    is_alpha = place[0] == 0

    def both(mine, other):
        return jnp.where(is_alpha, mine, other), jnp.where(is_alpha, other, mine)

    def part(start, stop):
        return both(stacked(own_one, own_two, start, stop), stacked(received_one, received_two, start, stop))

    one, two = part(128, 256), part(256, 384)
    right = split(assemble((one[0], two[0]), (one[1], two[1])))
    face, back = part(384, 448), part(448, 512)
    direct = jnp.concatenate(
        [assemble((face[0], back[0]), None), assemble(None, (face[1], back[1]))], axis=0
    )
    mine = link[...]
    other = jnp.transpose(stacked(received_one, received_two, 128, 256))[0:FACE]
    coupling = jnp.concatenate(
        [jnp.where(is_alpha, mine, other), jnp.where(is_alpha, other, mine)], axis=0
    )
    solved = split(product(split(coupling), (inverse_high[...], inverse_low[...])))
    merged = direct - product(solved, right)
    for i in range(4):
        stack(message_one, message_two, 128 * i, merged[:, 128 * i : 128 * i + 128])
    right_high[...], right_low[...] = right


def rest_columns(one, two):
    return jnp.concatenate(
        [stacked(one, two, 128 * i, 128 * i + 128) for i in range(1, 4)], axis=1
    )


def outer_kernel(place, outer, outer_high, outer_low, inverse_high, inverse_low, right_high, right_low, rows):
    mine = outer[:, 128:256], outer[:, 256:384]
    direct = jnp.where(place[0] == 0, assemble(mine, None), assemble(None, mine))
    solved = split(product((outer_high[...], outer_low[...]), (inverse_high[...], inverse_low[...])))
    rows[...] = direct - product(solved, (right_high[...], right_low[...]))


def third_kernel(own_one, own_two, received, rows, half, solved_high, solved_low):
    right = split(rest_columns(own_one, own_two))
    system = own_one[0:128, :] + received[0:128, :]
    solved = split(spd_inverse(system, rows[:, 0:128]))
    half[...] = rows[:, 128:512] + product(solved, right)
    solved_high[...], solved_low[...] = solved


def last_kernel(place, half, received_one, received_two, solved_high, solved_low, out):
    third = place[1]
    width = 6 * FACE
    mine = pl.multiple_of(third * width, 128)
    other = pl.multiple_of((1 - third) * width, 128)
    out[:, pl.ds(mine, width)] = half[...]
    solved = solved_high[...], solved_low[...]
    out[:, pl.ds(other, width)] = product(solved, split(rest_columns(received_one, received_two)))


def shapes(*sizes):
    return [jax.ShapeDtypeStruct(size, F32) for size in sizes]


def pair(*size):
    return [jax.ShapeDtypeStruct(size, BF16)] * 2


def run(kernel, out_shape, *operands, scalars=1, **options):
    smem = pl.BlockSpec(memory_space=pltpu.SMEM)
    vmem = pl.BlockSpec(memory_space=pltpu.VMEM)
    return pl.pallas_call(
        kernel,
        out_shape=out_shape,
        in_specs=[smem] * scalars + [vmem] * (len(operands) - scalars),
        out_specs=[vmem] * len(out_shape),
        compiler_params=pltpu.CompilerParams(vmem_limit_bytes=32 * 1024 * 1024),
        **options,
    )(*operands)


def body(leaf_maps, leaf_operator, region_eps, wave_sq, region_labels, build_flags):
    across = lax.axis_index("bx") % 2
    upward = lax.axis_index("by")
    place = jnp.stack([across, upward // 2 % 2, upward % 2]).astype(jnp.int32)
    size = leaf_operator.shape[0]
    mine = pl.pallas_call(
        build_kernel,
        out_shape=jax.ShapeDtypeStruct((LEAF, LEAF), F32),
        in_specs=[pl.BlockSpec(memory_space=pltpu.SMEM)] * 3
        + [pl.BlockSpec(memory_space=pltpu.HBM)] * 3,
        out_specs=pl.BlockSpec(memory_space=pltpu.VMEM),
        scratch_shapes=[
            pltpu.VMEM(region_eps.shape, F32),
            pltpu.VMEM((128, size), F32),
            pltpu.VMEM((size - LEAF - 128, size), F32),
            pltpu.VMEM((LEAF, size), F32),
            pltpu.SemaphoreType.DMA((5,)),
        ],
        compiler_params=pltpu.CompilerParams(vmem_limit_bytes=32 * 1024 * 1024),
        name="leaf_build",
    )(
        region_labels,
        build_flags,
        wave_sq,
        *(
            pltpu.with_memory_space_constraint(x, pltpu.HBM)
            for x in (leaf_maps[0, 0], leaf_operator, region_eps)
        ),
    )
    theirs = swapped(mine, "by", 0)
    one, two, link, *solved = run(
        first_kernel,
        shapes((CUT_TWO, 128), (512 - CUT_TWO, 128), (FACE, 128)) + pair(FACE, 6 * FACE),
        place,
        mine,
        theirs,
        name="first_merge",
    )
    received_one = swapped(one, "bx", 0)
    received_two = swapped(two, "bx", 0)
    (outer,) = run(
        rows_kernel,
        shapes((96, 6 * FACE)),
        place,
        mine,
        theirs,
        *solved,
        scratch_shapes=[pltpu.VMEM((192, 6 * FACE), F32), pltpu.VMEM((192, 128), F32)],
        name="first_rows",
    )
    *inverse, outer_high, outer_low = run(
        second_kernel,
        pair(128, 128) + pair(96, 128),
        one,
        received_one,
        outer,
        scalars=0,
        cost_estimate=LONG,
        name="second_inverse",
    )
    one, two, *right = run(
        exchange_kernel,
        shapes((CUT_THREE, 128), (512 - CUT_THREE, 128)) + pair(128, 8 * FACE),
        place,
        one,
        two,
        received_one,
        received_two,
        link,
        *inverse,
        name="second_merge",
    )
    received_one = swapped(one, "by", 1)
    received_two = swapped(two, "by", 1)
    (rows,) = run(
        outer_kernel,
        shapes((96, 8 * FACE)),
        place,
        outer,
        outer_high,
        outer_low,
        *inverse,
        *right,
        name="second_rows",
    )
    half, *solved = run(
        third_kernel,
        shapes((96, 6 * FACE)) + pair(96, 128),
        one,
        two,
        received_one,
        rows,
        scalars=0,
        cost_estimate=LONG,
        name="third_inverse",
    )
    (result,) = run(
        last_kernel,
        shapes((96, 12 * FACE)),
        place,
        half,
        received_one,
        received_two,
        *solved,
        name="third_merge",
    )
    return result.reshape((1, 1, 96, 12 * FACE))


def solution(mesh):
    placed = (
        P(("freq", "bx"), "by", None, None),
        P(),
        P(),
        P("freq"),
        P("bx", "by"),
        P("bx", "by"),
    )
    return jax.shard_map(
        body,
        mesh=mesh,
        in_specs=placed,
        out_specs=P(("freq", "bx"), "by", None, None),
        check_vma=False,
    )
```

```python
import jax
import jax.numpy as jnp
from jax import lax
from jax.experimental import pallas as pl
from jax.experimental.pallas import tpu as pltpu
from jax.sharding import PartitionSpec as P

FACE = 64
LEAF = 4 * FACE
CUT_TWO, CUT_THREE = 192, 128
F32 = jnp.float32
BF16 = jnp.bfloat16


LONG = pl.CostEstimate(flops=10**10, bytes_accessed=10**8, transcendentals=10**6)


def swapped(shard, axis, stride):
    return lax.ppermute(shard, axis, [(i, i ^ 1 << stride) for i in range(lax.axis_size(axis))])


def split(x):
    high = x.astype(BF16)
    return high, (x - high.astype(F32)).astype(BF16)


def thirds(x):
    high = x.astype(BF16).astype(F32)
    rest = x - high
    middle = rest.astype(BF16).astype(F32)
    return high, middle, (rest - middle).astype(BF16).astype(F32)


def dot(a, b):
    return jnp.dot(a, b, preferred_element_type=F32)


def product(a, b):
    (a_high, a_low), (b_high, b_low) = a, b
    depth = a_high.shape[1]
    if depth % 128 and depth != FACE:
        return dot(a_high, b_high) + (dot(a_high, b_low) + dot(a_low, b_high))
    twice = dot(
        jnp.concatenate([a_high, a_low], axis=1), jnp.concatenate([b_high, b_high], axis=0)
    )
    return twice + dot(a_high, b_low)


def tree(terms):
    while len(terms) > 1:
        terms = [x + y for x, y in zip(terms[::2], terms[1::2])]
    return terms[0]


def minus(value, terms):
    for term in terms:
        value = value - term
    return value


def spd_inverse(matrix, left=None, both=False, panel=4, look=4, half=2):
    size = matrix.shape[0]
    shape = (8, size)
    count = size // 8
    tiles = [matrix[8 * g : 8 * g + 8] for g in range(count)]
    lane = lax.broadcasted_iota(jnp.int32, shape, 1)
    sub = lax.broadcasted_iota(jnp.int32, shape, 0)

    def column(tile, c):
        return jnp.broadcast_to(tile[:, c : c + 1], shape)

    def row(tile, r):
        return jnp.broadcast_to(tile[r : r + 1, :], shape)

    def inside(start, stop):
        return (lane >= start) & (lane < stop)

    pivot = [column(tiles[0], j) for j in range(8)]
    head = row(pivot[0], 0)
    for start in range(0, count, panel):
        stop = min(start + panel, count)
        last = min(stop + look, count)
        outside = [*range(last, count), *range(start if left is None or both else 0)]
        if outside:
            strip = jnp.concatenate([tiles[g] for g in outside], axis=0)[:, 8 * start : 8 * stop]
            high, middle, low = thirds(strip)
            factors = jnp.concatenate([high, high, middle, high, low, middle], axis=1).astype(BF16)
        for k in range(start, stop):
            first = 8 * k
            block = inside(first, first + 8)
            rows = jnp.where(block, (lane - first == sub).astype(F32), tiles[k])
            ahead = k + 1 < count
            if ahead:
                after = jnp.where(block, 0.0, tiles[k + 1])
                side = [column(tiles[k + 1], first + j) for j in range(8)]
            scale = None
            for p in range(8):
                inverse = pl.reciprocal(head, approx=True)
                if p < 7:
                    element = row(pivot[p + 1], p)
                    head = row(pivot[p + 1], p + 1) - element * (element * inverse)
                factor = jnp.where(sub == p, 0.0, pivot[p]) * inverse
                picked = row(rows, p)
                if ahead:
                    edge = side[p]
                    factor_ahead = edge * inverse
                    if p == half:
                        coming = [column(after, first + 8 + j) for j in range(8)]
                    if p == 7:
                        element = row(edge, 0)
                        head = row(coming[0], 0) - element * (element * inverse)
                    if p >= half:
                        for j in range(8):
                            coming[j] = coming[j] - factor_ahead * row(edge, j)
                    after = after - factor_ahead * picked
                for j in range(p + 1, 8):
                    element = row(pivot[j], p)
                    pivot[j] = pivot[j] - factor * element
                    if ahead:
                        side[j] = side[j] - factor_ahead * element
                rows = rows - factor * picked
                scale = inverse if scale is None else jnp.where(sub == p, inverse, scale)
            rows = rows * scale
            picked = [row(rows, j) for j in range(8)]
            for g in range(start, last):
                if g == k:
                    tiles[g] = rows
                elif g == k + 1:
                    tiles[g] = after
                else:
                    terms = [column(tiles[g], first + j) * picked[j] for j in range(8)]
                    cleared = jnp.where(block, 0.0, tiles[g])
                    tiles[g] = cleared - tree(terms) if count <= 8 else minus(cleared, terms)
            if ahead:
                pivot = coming
        solved = jnp.concatenate(tiles[start:stop], axis=0)
        if outside:
            high, middle, low = thirds(solved)
            right = jnp.concatenate([high, middle, high, low, high, middle], axis=0).astype(BF16)
            update = dot(factors, right)
            block = inside(8 * start, 8 * stop)
            for i, g in enumerate(outside):
                tiles[g] = jnp.where(block, 0.0, tiles[g]) - update[8 * i : 8 * i + 8]
        if left is not None:
            blanks = [jnp.zeros((rows, size), BF16) for rows in (8 * start, size - 8 * stop)]
            right = [
                jnp.concatenate([x for x in (blanks[0], part, blanks[1]) if x.shape[0]], axis=0)
                for part in split(solved)
            ]
            columns = lax.broadcasted_iota(jnp.int32, left.shape, 1)
            block = (columns >= 8 * start) & (columns < 8 * stop)
            left = jnp.where(block, 0.0, left) - product(split(left), right)
    if left is not None and not both:
        return left
    whole = jnp.concatenate(tiles, axis=0)
    return (whole, left) if both else whole


def build_kernel(label, flag, wave, given, operator, table_at, out, table, one, two, edge, sems):
    size = operator.shape[0]
    middle = LEAF + 128
    copies = [
        pltpu.make_async_copy(source, target, sems.at[i])
        for i, (source, target) in enumerate(
            (
                (operator.at[pl.ds(LEAF, 128)], one),
                (table_at, table),
                (operator.at[pl.ds(middle, size - middle)], two),
                (operator.at[pl.ds(0, LEAF)], edge),
                (given, out),
            )
        )
    ]
    flagged = flag[0, 0] > 0

    @pl.when(jnp.logical_not(flagged))
    def _():
        copies[4].start()
        copies[4].wait()

    @pl.when(flagged)
    def _():
        for copy in copies[:4]:
            copy.start()
        for copy in copies[:2]:
            copy.wait()
        shift = wave[0] * table[pl.ds(label[0, 0], 1), :]
        border, near, far = slice(0, LEAF), slice(LEAF, middle), slice(middle, size)

        def shifted(ref, span):
            block = ref[:, span]
            ids = lax.broadcasted_iota(jnp.int32, block.shape, 0)
            diagonal = ids == lax.broadcasted_iota(jnp.int32, block.shape, 1)
            return block - jnp.where(diagonal, shift[:, span], 0.0)

        right = split(one[:, border]), split(one[:, far])
        copies[2].wait()
        inverse, left = spd_inverse(shifted(one, near), two[:, near], both=True)
        copies[3].wait()
        left = split(left)
        inner = shifted(two, far) + product(left, right[1])
        coupled = split(two[:, border] + product(left, right[0]))
        left = split(edge[:, near])
        left = split(product(left, split(inverse)))
        merged = shifted(edge, border) - product(left, right[0])
        across = split(edge[:, far] - product(left, right[1]))
        inverse = split(spd_inverse(inner))
        solved = split(product(inverse, coupled))
        out[...] = merged - product(across, solved)


def halves(shape):
    return lax.broadcasted_iota(jnp.int32, shape, 1) < FACE


def turn(tile):
    return pltpu.roll(tile, FACE, 1)


def leaf_rows(place, mine, theirs):
    across, third, lead = place[0], place[1], place[2]
    is_alpha = lead == 0
    left = halves((FACE, 128))

    def load(alpha, block, tile):
        spot = pl.ds(pl.multiple_of(block * FACE, FACE), FACE)
        span = slice(128 * tile, 128 * tile + 128)
        own = is_alpha if alpha else jnp.logical_not(is_alpha)
        return jnp.where(own, mine[spot, span], theirs[spot, span])

    def alpha_rows(block):
        sides = load(True, block, 0)
        ends = load(True, block, 1)
        sides = jnp.where(across == 0, turn(sides), sides)
        tiles = (
            jnp.where(left, sides, 0.0),
            jnp.where(left, jnp.where(third == 0, 0.0, ends), sides),
            jnp.where(left & (third == 0), ends, 0.0),
        )
        return jnp.concatenate(tiles, axis=1), turn(ends)

    def beta_rows(block):
        sides = load(False, block, 0)
        ends = load(False, block, 1)
        other = turn(sides)
        near_far = jnp.where(across == 0, other, sides)
        far_near = jnp.where(across == 0, sides, other)
        flipped = turn(ends)
        tiles = (
            jnp.where(left, 0.0, far_near),
            jnp.where(left & (third == 0), flipped, 0.0),
            jnp.where(
                third == 0,
                jnp.where(left, 0.0, near_far),
                jnp.where(left, far_near, ends),
            ),
        )
        return jnp.concatenate(tiles, axis=1), ends

    return alpha_rows, beta_rows


def either(flag, one, other):
    return [jnp.where(flag, x, y) for x, y in zip(one, other)]


def stacked(one, two, start, stop):
    cut = one.shape[0]
    parts = []
    if start < cut:
        parts.append(one[start : min(stop, cut), :])
    if stop > cut:
        parts.append(two[max(start, cut) - cut : stop - cut, :])
    return jnp.concatenate(parts, axis=0)


def stack(one, two, start, value):
    cut = one.shape[0]
    stop = start + value.shape[0]
    if start < cut:
        one[start : min(stop, cut), :] = value[: cut - start]
    if stop > cut:
        two[max(start, cut) - cut : stop - cut, :] = value[max(cut - start, 0) :]


def first_kernel(
    place,
    mine,
    theirs,
    message_one,
    message_two,
    link,
    outer_high,
    outer_low,
    right_high,
    right_low,
):
    alpha_rows, beta_rows = leaf_rows(place, mine, theirs)
    third, lead = place[1], place[2]
    near = jnp.where(place[0] == 0, 1, 0)
    tiles_a, meet_a = alpha_rows(3)
    tiles_b, meet_b = beta_rows(2)
    system = (meet_a + meet_b)[:, :FACE]
    right = split(tiles_a + tiles_b)
    parts = [alpha_rows(near), beta_rows(near), either(third == 0, beta_rows(3), alpha_rows(2))]
    direct = jnp.concatenate([tiles for tiles, _ in parts], axis=0)
    one, far = alpha_rows(1 - near)[1], beta_rows(1 - near)[1]
    two = jnp.where(third == 0, alpha_rows(2)[1], far)
    three = jnp.where(third == 0, far, beta_rows(3)[1])
    outer = [
        jnp.where(lead == 0, one, jnp.concatenate([two[32:], three[:32]], axis=0)),
        jnp.where(lead == 0, two[:32], three[32:]),
    ]
    left = jnp.concatenate([meet for _, meet in parts] + outer, axis=0)[:, :FACE]
    solved = split(spd_inverse(system, left, half=4))
    outer_high[...], outer_low[...] = [x[192:288] for x in solved]
    right_high[...], right_low[...] = right
    merged = direct + product([x[0:192] for x in solved], right)
    for i in range(3):
        stack(message_one, message_two, 128 * i, merged[0:128, 128 * i : 128 * i + 128])
    stack(message_one, message_two, 384, merged[128:192, 128:256])
    stack(message_one, message_two, 448, merged[128:192, 256:384])
    link[...] = merged[128:192, 0:128]


def rows_kernel(place, mine, theirs, outer_high, outer_low, right_high, right_low, outer, direct):
    alpha_rows, beta_rows = leaf_rows(place, mine, theirs)
    third, lead = place[1], place[2]
    far = jnp.where(place[0] == 0, 0, 1)
    at_far = beta_rows(far)[0]
    direct[0:64, :] = alpha_rows(far)[0]
    direct[64:128, :] = jnp.where(third == 0, alpha_rows(2)[0], at_far)
    direct[128:192, :] = jnp.where(third == 0, at_far, beta_rows(3)[0])
    spot = pl.ds(pl.multiple_of(lead * 96, 32), 96)
    solved, right = (outer_high[...], outer_low[...]), (right_high[...], right_low[...])
    outer[...] = direct[spot, :] + product(solved, right)


def second_kernel(own, received, outer, inverse_high, inverse_low, outer_high, outer_low):
    outer_high[...], outer_low[...] = split(outer[:, 0:128])
    system = own[0:128, :] + received[0:128, :]
    inverse_high[...], inverse_low[...] = split(spd_inverse(system))


def assemble(alpha, beta):
    rows = (alpha or beta)[0].shape[0]
    left = halves((rows, 128))
    blank = jnp.zeros((rows, 128), F32)
    if alpha is None:
        tiles = (
            jnp.where(left, 0.0, turn(beta[0])),
            blank,
            jnp.where(left, 0.0, beta[0]),
            beta[1],
        )
        return jnp.concatenate(tiles, axis=1)
    turned = turn(alpha[1])
    middle = jnp.where(left, turn(alpha[0]), turned)
    if beta is None:
        tiles = jnp.where(left, alpha[0], 0.0), middle, jnp.where(left, turned, 0.0), blank
        return jnp.concatenate(tiles, axis=1)
    tiles = (
        jnp.where(left, alpha[0], turn(beta[0])),
        middle,
        jnp.where(left, turned, beta[0]),
        beta[1],
    )
    return jnp.concatenate(tiles, axis=1)


def exchange_kernel(
    place,
    own_one,
    own_two,
    received_one,
    received_two,
    link,
    inverse_high,
    inverse_low,
    message_one,
    message_two,
    right_high,
    right_low,
):
    is_alpha = place[0] == 0

    def both(mine, other):
        return jnp.where(is_alpha, mine, other), jnp.where(is_alpha, other, mine)

    def part(start, stop):
        return both(stacked(own_one, own_two, start, stop), stacked(received_one, received_two, start, stop))

    one, two = part(128, 256), part(256, 384)
    right = split(assemble((one[0], two[0]), (one[1], two[1])))
    face, back = part(384, 448), part(448, 512)
    direct = jnp.concatenate(
        [assemble((face[0], back[0]), None), assemble(None, (face[1], back[1]))], axis=0
    )
    mine = link[...]
    other = jnp.transpose(stacked(received_one, received_two, 128, 256))[0:FACE]
    coupling = jnp.concatenate(
        [jnp.where(is_alpha, mine, other), jnp.where(is_alpha, other, mine)], axis=0
    )
    solved = split(product(split(coupling), (inverse_high[...], inverse_low[...])))
    merged = direct - product(solved, right)
    for i in range(4):
        stack(message_one, message_two, 128 * i, merged[:, 128 * i : 128 * i + 128])
    right_high[...], right_low[...] = right


def rest_columns(one, two):
    return jnp.concatenate(
        [stacked(one, two, 128 * i, 128 * i + 128) for i in range(1, 4)], axis=1
    )


def outer_kernel(place, outer, outer_high, outer_low, inverse_high, inverse_low, right_high, right_low, rows):
    mine = outer[:, 128:256], outer[:, 256:384]
    direct = jnp.where(place[0] == 0, assemble(mine, None), assemble(None, mine))
    solved = split(product((outer_high[...], outer_low[...]), (inverse_high[...], inverse_low[...])))
    rows[...] = direct - product(solved, (right_high[...], right_low[...]))


def third_kernel(own_one, own_two, received, rows, half, solved_high, solved_low):
    right = split(rest_columns(own_one, own_two))
    system = own_one[0:128, :] + received[0:128, :]
    solved = split(spd_inverse(system, rows[:, 0:128]))
    half[...] = rows[:, 128:512] + product(solved, right)
    solved_high[...], solved_low[...] = solved


def last_kernel(place, half, received_one, received_two, solved_high, solved_low, out):
    third = place[1]
    width = 6 * FACE
    mine = pl.multiple_of(third * width, 128)
    other = pl.multiple_of((1 - third) * width, 128)
    out[:, pl.ds(mine, width)] = half[...]
    solved = solved_high[...], solved_low[...]
    out[:, pl.ds(other, width)] = product(solved, split(rest_columns(received_one, received_two)))


def shapes(*sizes):
    return [jax.ShapeDtypeStruct(size, F32) for size in sizes]


def pair(*size):
    return [jax.ShapeDtypeStruct(size, BF16)] * 2


def run(kernel, out_shape, *operands, scalars=1, **options):
    smem = pl.BlockSpec(memory_space=pltpu.SMEM)
    vmem = pl.BlockSpec(memory_space=pltpu.VMEM)
    return pl.pallas_call(
        kernel,
        out_shape=out_shape,
        in_specs=[smem] * scalars + [vmem] * (len(operands) - scalars),
        out_specs=[vmem] * len(out_shape),
        compiler_params=pltpu.CompilerParams(vmem_limit_bytes=32 * 1024 * 1024),
        **options,
    )(*operands)


def body(leaf_maps, leaf_operator, region_eps, wave_sq, region_labels, build_flags):
    across = lax.axis_index("bx") % 2
    upward = lax.axis_index("by")
    place = jnp.stack([across, upward // 2 % 2, upward % 2]).astype(jnp.int32)
    size = leaf_operator.shape[0]
    mine = pl.pallas_call(
        build_kernel,
        out_shape=jax.ShapeDtypeStruct((LEAF, LEAF), F32),
        in_specs=[pl.BlockSpec(memory_space=pltpu.SMEM)] * 3
        + [pl.BlockSpec(memory_space=pltpu.HBM)] * 3,
        out_specs=pl.BlockSpec(memory_space=pltpu.VMEM),
        scratch_shapes=[
            pltpu.VMEM(region_eps.shape, F32),
            pltpu.VMEM((128, size), F32),
            pltpu.VMEM((size - LEAF - 128, size), F32),
            pltpu.VMEM((LEAF, size), F32),
            pltpu.SemaphoreType.DMA((5,)),
        ],
        compiler_params=pltpu.CompilerParams(vmem_limit_bytes=32 * 1024 * 1024),
        name="leaf_build",
    )(
        region_labels,
        build_flags,
        wave_sq,
        *(
            pltpu.with_memory_space_constraint(x, pltpu.HBM)
            for x in (leaf_maps[0, 0], leaf_operator, region_eps)
        ),
    )
    theirs = swapped(mine, "by", 0)
    one, two, link, *solved = run(
        first_kernel,
        shapes((CUT_TWO, 128), (512 - CUT_TWO, 128), (FACE, 128))
        + pair(96, FACE)
        + pair(FACE, 6 * FACE),
        place,
        mine,
        theirs,
        name="first_merge",
    )
    received_one = swapped(one, "bx", 0)
    received_two = swapped(two, "bx", 0)
    (outer,) = run(
        rows_kernel,
        shapes((96, 6 * FACE)),
        place,
        mine,
        theirs,
        *solved,
        scratch_shapes=[pltpu.VMEM((192, 6 * FACE), F32)],
        name="first_rows",
    )
    *inverse, outer_high, outer_low = run(
        second_kernel,
        pair(128, 128) + pair(96, 128),
        one,
        received_one,
        outer,
        scalars=0,
        cost_estimate=LONG,
        name="second_inverse",
    )
    one, two, *right = run(
        exchange_kernel,
        shapes((CUT_THREE, 128), (512 - CUT_THREE, 128)) + pair(128, 8 * FACE),
        place,
        one,
        two,
        received_one,
        received_two,
        link,
        *inverse,
        name="second_merge",
    )
    received_one = swapped(one, "by", 1)
    received_two = swapped(two, "by", 1)
    (rows,) = run(
        outer_kernel,
        shapes((96, 8 * FACE)),
        place,
        outer,
        outer_high,
        outer_low,
        *inverse,
        *right,
        name="second_rows",
    )
    half, *solved = run(
        third_kernel,
        shapes((96, 6 * FACE)) + pair(96, 128),
        one,
        two,
        received_one,
        rows,
        scalars=0,
        cost_estimate=LONG,
        name="third_inverse",
    )
    (result,) = run(
        last_kernel,
        shapes((96, 12 * FACE)),
        place,
        half,
        received_one,
        received_two,
        *solved,
        name="third_merge",
    )
    return result.reshape((1, 1, 96, 12 * FACE))


def solution(mesh):
    placed = (
        P(("freq", "bx"), "by", None, None),
        P(),
        P(),
        P("freq"),
        P("bx", "by"),
        P("bx", "by"),
    )
    return jax.shard_map(
        body,
        mesh=mesh,
        in_specs=placed,
        out_specs=P(("freq", "bx"), "by", None, None),
        check_vma=False,
    )
```

```python
import jax
import jax.numpy as jnp
from jax import lax
from jax.experimental import pallas as pl
from jax.experimental.pallas import tpu as pltpu
from jax.sharding import PartitionSpec as P

FACE = 64
LEAF = 4 * FACE
CUT_TWO, CUT_THREE = 192, 144
F32 = jnp.float32
BF16 = jnp.bfloat16


LONG = pl.CostEstimate(flops=10**10, bytes_accessed=10**8, transcendentals=10**6)


def swapped(shard, axis, stride):
    return lax.ppermute(shard, axis, [(i, i ^ 1 << stride) for i in range(lax.axis_size(axis))])


def split(x):
    high = x.astype(BF16)
    return high, (x - high.astype(F32)).astype(BF16)


def thirds(x):
    high = x.astype(BF16).astype(F32)
    rest = x - high
    middle = rest.astype(BF16).astype(F32)
    return high, middle, (rest - middle).astype(BF16).astype(F32)


def dot(a, b):
    return jnp.dot(a, b, preferred_element_type=F32)


def product(a, b):
    (a_high, a_low), (b_high, b_low) = a, b
    depth = a_high.shape[1]
    if depth % 128 and depth != FACE:
        return dot(a_high, b_high) + (dot(a_high, b_low) + dot(a_low, b_high))
    twice = dot(
        jnp.concatenate([a_high, a_low], axis=1), jnp.concatenate([b_high, b_high], axis=0)
    )
    return twice + dot(a_high, b_low)


def tree(terms):
    while len(terms) > 1:
        terms = [x + y for x, y in zip(terms[::2], terms[1::2])]
    return terms[0]


def minus(value, terms):
    for term in terms:
        value = value - term
    return value


def spd_inverse(matrix, left=None, both=False, panel=4, look=3, half=4):
    size = matrix.shape[0]
    shape = (8, size)
    count = size // 8
    tiles = [matrix[8 * g : 8 * g + 8] for g in range(count)]
    lane = lax.broadcasted_iota(jnp.int32, shape, 1)
    sub = lax.broadcasted_iota(jnp.int32, shape, 0)

    def column(tile, c):
        return jnp.broadcast_to(tile[:, c : c + 1], shape)

    def row(tile, r):
        return jnp.broadcast_to(tile[r : r + 1, :], shape)

    def inside(start, stop):
        return (lane >= start) & (lane < stop)

    pivot = [column(tiles[0], j) for j in range(8)]
    head = row(pivot[0], 0)
    for start in range(0, count, panel):
        stop = min(start + panel, count)
        last = min(stop + look, count)
        outside = [*range(last, count), *range(start if left is None or both else 0)]
        if outside:
            strip = jnp.concatenate([tiles[g] for g in outside], axis=0)[:, 8 * start : 8 * stop]
            high, middle, low = thirds(strip)
            factors = jnp.concatenate([high, high, middle, high, low, middle], axis=1).astype(BF16)
        for k in range(start, stop):
            first = 8 * k
            block = inside(first, first + 8)
            rows = jnp.where(block, (lane - first == sub).astype(F32), tiles[k])
            ahead = k + 1 < count
            if ahead:
                after = jnp.where(block, 0.0, tiles[k + 1])
                side = [column(tiles[k + 1], first + j) for j in range(8)]
            scale = None
            for p in range(8):
                inverse = pl.reciprocal(head, approx=True)
                if p < 7:
                    element = row(pivot[p + 1], p)
                    head = row(pivot[p + 1], p + 1) - element * (element * inverse)
                factor = jnp.where(sub == p, 0.0, pivot[p]) * inverse
                picked = row(rows, p)
                if ahead:
                    edge = side[p]
                    factor_ahead = edge * inverse
                    if p == half:
                        coming = [column(after, first + 8 + j) for j in range(8)]
                    if p == 7:
                        element = row(edge, 0)
                        head = row(coming[0], 0) - element * (element * inverse)
                    if p >= half:
                        for j in range(8):
                            coming[j] = coming[j] - factor_ahead * row(edge, j)
                    after = after - factor_ahead * picked
                for j in range(p + 1, 8):
                    element = row(pivot[j], p)
                    pivot[j] = pivot[j] - factor * element
                    if ahead:
                        side[j] = side[j] - factor_ahead * element
                rows = rows - factor * picked
                scale = inverse if scale is None else jnp.where(sub == p, inverse, scale)
            rows = rows * scale
            picked = [row(rows, j) for j in range(8)]
            for g in range(start, last):
                if g == k:
                    tiles[g] = rows
                elif g == k + 1:
                    tiles[g] = after
                else:
                    terms = [column(tiles[g], first + j) * picked[j] for j in range(8)]
                    cleared = jnp.where(block, 0.0, tiles[g])
                    tiles[g] = cleared - tree(terms) if count <= panel else minus(cleared, terms)
            if ahead:
                pivot = coming
        solved = jnp.concatenate(tiles[start:stop], axis=0)
        if outside:
            high, middle, low = thirds(solved)
            right = jnp.concatenate([high, middle, high, low, high, middle], axis=0).astype(BF16)
            update = dot(factors, right)
            block = inside(8 * start, 8 * stop)
            for i, g in enumerate(outside):
                tiles[g] = jnp.where(block, 0.0, tiles[g]) - update[8 * i : 8 * i + 8]
        if left is not None:
            blanks = [jnp.zeros((rows, size), BF16) for rows in (8 * start, size - 8 * stop)]
            right = [
                jnp.concatenate([x for x in (blanks[0], part, blanks[1]) if x.shape[0]], axis=0)
                for part in split(solved)
            ]
            columns = lax.broadcasted_iota(jnp.int32, left.shape, 1)
            block = (columns >= 8 * start) & (columns < 8 * stop)
            left = jnp.where(block, 0.0, left) - product(split(left), right)
    if left is not None and not both:
        return left
    whole = jnp.concatenate(tiles, axis=0)
    return (whole, left) if both else whole


def build_kernel(label, flag, wave, given, operator, table_at, out, table, one, two, edge, sems):
    size = operator.shape[0]
    middle = LEAF + 128
    copies = [
        pltpu.make_async_copy(source, target, sems.at[i])
        for i, (source, target) in enumerate(
            (
                (operator.at[pl.ds(LEAF, 128)], one),
                (table_at, table),
                (operator.at[pl.ds(middle, size - middle)], two),
                (operator.at[pl.ds(0, LEAF)], edge),
                (given, out),
            )
        )
    ]
    flagged = flag[0, 0] > 0

    @pl.when(jnp.logical_not(flagged))
    def _():
        copies[4].start()
        copies[4].wait()

    @pl.when(flagged)
    def _():
        for copy in copies[:4]:
            copy.start()
        for copy in copies[:2]:
            copy.wait()
        shift = wave[0] * table[pl.ds(label[0, 0], 1), :]
        border, near, far = slice(0, LEAF), slice(LEAF, middle), slice(middle, size)

        def shifted(ref, span):
            block = ref[:, span]
            ids = lax.broadcasted_iota(jnp.int32, block.shape, 0)
            diagonal = ids == lax.broadcasted_iota(jnp.int32, block.shape, 1)
            return block - jnp.where(diagonal, shift[:, span], 0.0)

        right = split(one[:, border]), split(one[:, far])
        copies[2].wait()
        inverse, left = spd_inverse(shifted(one, near), two[:, near], both=True)
        copies[3].wait()
        left = split(left)
        inner = shifted(two, far) + product(left, right[1])
        coupled = split(two[:, border] + product(left, right[0]))
        left = split(edge[:, near])
        left = split(product(left, split(inverse)))
        merged = shifted(edge, border) - product(left, right[0])
        across = split(edge[:, far] - product(left, right[1]))
        inverse = split(spd_inverse(inner))
        solved = split(product(inverse, coupled))
        out[...] = merged - product(across, solved)


def halves(shape):
    return lax.broadcasted_iota(jnp.int32, shape, 1) < FACE


def turn(tile):
    return pltpu.roll(tile, FACE, 1)


def leaf_rows(place, mine, theirs):
    across, third, lead = place[0], place[1], place[2]
    is_alpha = lead == 0
    left = halves((FACE, 128))

    def load(alpha, block, tile):
        spot = pl.ds(pl.multiple_of(block * FACE, FACE), FACE)
        span = slice(128 * tile, 128 * tile + 128)
        own = is_alpha if alpha else jnp.logical_not(is_alpha)
        return jnp.where(own, mine[spot, span], theirs[spot, span])

    def alpha_rows(block):
        sides = load(True, block, 0)
        ends = load(True, block, 1)
        sides = jnp.where(across == 0, turn(sides), sides)
        tiles = (
            jnp.where(left, sides, 0.0),
            jnp.where(left, jnp.where(third == 0, 0.0, ends), sides),
            jnp.where(left & (third == 0), ends, 0.0),
        )
        return jnp.concatenate(tiles, axis=1), turn(ends)

    def beta_rows(block):
        sides = load(False, block, 0)
        ends = load(False, block, 1)
        other = turn(sides)
        near_far = jnp.where(across == 0, other, sides)
        far_near = jnp.where(across == 0, sides, other)
        flipped = turn(ends)
        tiles = (
            jnp.where(left, 0.0, far_near),
            jnp.where(left & (third == 0), flipped, 0.0),
            jnp.where(
                third == 0,
                jnp.where(left, 0.0, near_far),
                jnp.where(left, far_near, ends),
            ),
        )
        return jnp.concatenate(tiles, axis=1), ends

    return alpha_rows, beta_rows


def either(flag, one, other):
    return [jnp.where(flag, x, y) for x, y in zip(one, other)]


def stacked(one, two, start, stop):
    cut = one.shape[0]
    parts = []
    if start < cut:
        parts.append(one[start : min(stop, cut), :])
    if stop > cut:
        parts.append(two[max(start, cut) - cut : stop - cut, :])
    return jnp.concatenate(parts, axis=0)


def stack(one, two, start, value):
    cut = one.shape[0]
    stop = start + value.shape[0]
    if start < cut:
        one[start : min(stop, cut), :] = value[: cut - start]
    if stop > cut:
        two[max(start, cut) - cut : stop - cut, :] = value[max(cut - start, 0) :]


def first_kernel(place, mine, theirs, message_one, message_two, link, solved_high, solved_low):
    alpha_rows, beta_rows = leaf_rows(place, mine, theirs)
    near = jnp.where(place[0] == 0, 1, 0)
    tiles_a, meet_a = alpha_rows(3)
    tiles_b, meet_b = beta_rows(2)
    system = (meet_a + meet_b)[:, :FACE]
    right = split(tiles_a + tiles_b)
    parts = [alpha_rows(near), beta_rows(near), either(place[1] == 0, beta_rows(3), alpha_rows(2))]
    direct = jnp.concatenate([tiles for tiles, _ in parts], axis=0)
    coupling = split(jnp.concatenate([meet for _, meet in parts], axis=0)[:, :FACE])
    inverse = split(spd_inverse(system, panel=8, half=2))
    solved = split(product(inverse, right))
    merged = direct - product(coupling, solved)
    for i in range(3):
        stack(message_one, message_two, 128 * i, merged[0:128, 128 * i : 128 * i + 128])
    stack(message_one, message_two, 384, merged[128:192, 128:256])
    stack(message_one, message_two, 448, merged[128:192, 256:384])
    link[...] = merged[128:192, 0:128]
    solved_high[...], solved_low[...] = solved


def rows_kernel(place, mine, theirs, solved_high, solved_low, outer, direct, coupling):
    alpha_rows, beta_rows = leaf_rows(place, mine, theirs)
    third, lead = place[1], place[2]
    far = jnp.where(place[0] == 0, 0, 1)
    direct[0:64, :], coupling[0:64, :] = alpha_rows(far)
    at_two = alpha_rows(2)
    at_far = beta_rows(far)
    at_three = beta_rows(3)
    direct[64:128, :], coupling[64:128, :] = either(third == 0, at_two, at_far)
    direct[128:192, :], coupling[128:192, :] = either(third == 0, at_far, at_three)
    spot = pl.ds(pl.multiple_of(lead * 96, 32), 96)
    solved = solved_high[...], solved_low[...]
    outer[...] = direct[spot, :] - product(split(coupling[spot, :][:, :FACE]), solved)


def second_kernel(own, received, outer, inverse_high, inverse_low, outer_high, outer_low):
    outer_high[...], outer_low[...] = split(outer[:, 0:128])
    system = own[0:128, :] + received[0:128, :]
    inverse_high[...], inverse_low[...] = split(spd_inverse(system))


def assemble(alpha, beta):
    rows = (alpha or beta)[0].shape[0]
    left = halves((rows, 128))
    blank = jnp.zeros((rows, 128), F32)
    if alpha is None:
        tiles = (
            jnp.where(left, 0.0, turn(beta[0])),
            blank,
            jnp.where(left, 0.0, beta[0]),
            beta[1],
        )
        return jnp.concatenate(tiles, axis=1)
    turned = turn(alpha[1])
    middle = jnp.where(left, turn(alpha[0]), turned)
    if beta is None:
        tiles = jnp.where(left, alpha[0], 0.0), middle, jnp.where(left, turned, 0.0), blank
        return jnp.concatenate(tiles, axis=1)
    tiles = (
        jnp.where(left, alpha[0], turn(beta[0])),
        middle,
        jnp.where(left, turned, beta[0]),
        beta[1],
    )
    return jnp.concatenate(tiles, axis=1)


def exchange_kernel(
    place,
    own_one,
    own_two,
    received_one,
    received_two,
    link,
    inverse_high,
    inverse_low,
    message_one,
    message_two,
    right_high,
    right_low,
):
    is_alpha = place[0] == 0

    def both(mine, other):
        return jnp.where(is_alpha, mine, other), jnp.where(is_alpha, other, mine)

    def part(start, stop):
        return both(stacked(own_one, own_two, start, stop), stacked(received_one, received_two, start, stop))

    one, two = part(128, 256), part(256, 384)
    right = split(assemble((one[0], two[0]), (one[1], two[1])))
    face, back = part(384, 448), part(448, 512)
    direct = jnp.concatenate(
        [assemble((face[0], back[0]), None), assemble(None, (face[1], back[1]))], axis=0
    )
    mine = link[...]
    other = jnp.transpose(stacked(received_one, received_two, 128, 256))[0:FACE]
    coupling = jnp.concatenate(
        [jnp.where(is_alpha, mine, other), jnp.where(is_alpha, other, mine)], axis=0
    )
    solved = split(product(split(coupling), (inverse_high[...], inverse_low[...])))
    merged = direct - product(solved, right)
    for i in range(4):
        stack(message_one, message_two, 128 * i, merged[:, 128 * i : 128 * i + 128])
    right_high[...], right_low[...] = right


def rest_columns(one, two):
    return jnp.concatenate(
        [stacked(one, two, 128 * i, 128 * i + 128) for i in range(1, 4)], axis=1
    )


def outer_kernel(place, outer, outer_high, outer_low, inverse_high, inverse_low, right_high, right_low, rows):
    mine = outer[:, 128:256], outer[:, 256:384]
    direct = jnp.where(place[0] == 0, assemble(mine, None), assemble(None, mine))
    solved = split(product((outer_high[...], outer_low[...]), (inverse_high[...], inverse_low[...])))
    rows[...] = direct - product(solved, (right_high[...], right_low[...]))


def third_kernel(own_one, own_two, received, rows, half, solved_high, solved_low):
    right = split(rest_columns(own_one, own_two))
    system = own_one[0:128, :] + received[0:128, :]
    solved = split(spd_inverse(system, rows[:, 0:128]))
    half[...] = rows[:, 128:512] + product(solved, right)
    solved_high[...], solved_low[...] = solved


def last_kernel(
    place, half, received_one, received_two, solved_high, solved_low, out, other, sems
):
    third = place[1]
    width = 6 * FACE

    def copy(source, side, start, i):
        first = pl.multiple_of(side * width + start, 128)
        target = out.at[:, pl.ds(first, source.shape[1])]
        return pltpu.make_async_copy(source, target, sems.at[i])

    copies = [copy(half, third, 0, 0)]
    copies[0].start()
    solved = solved_high[...], solved_low[...]
    for i in range(3):
        right = split(stacked(received_one, received_two, 128 * i + 128, 128 * i + 256))
        other[i] = product(solved, right)
        copies.append(copy(other.at[i], 1 - third, 128 * i, i + 1))
        copies[-1].start()
    for x in copies:
        x.wait()


def shapes(*sizes):
    return [jax.ShapeDtypeStruct(size, F32) for size in sizes]


def pair(*size):
    return [jax.ShapeDtypeStruct(size, BF16)] * 2


def run(kernel, out_shape, *operands, scalars=1, out_space=pltpu.VMEM, **options):
    smem = pl.BlockSpec(memory_space=pltpu.SMEM)
    vmem = pl.BlockSpec(memory_space=pltpu.VMEM)
    return pl.pallas_call(
        kernel,
        out_shape=out_shape,
        in_specs=[smem] * scalars + [vmem] * (len(operands) - scalars),
        out_specs=[pl.BlockSpec(memory_space=out_space)] * len(out_shape),
        compiler_params=pltpu.CompilerParams(vmem_limit_bytes=32 * 1024 * 1024),
        **options,
    )(*operands)


def body(leaf_maps, leaf_operator, region_eps, wave_sq, region_labels, build_flags):
    across = lax.axis_index("bx") % 2
    upward = lax.axis_index("by")
    place = jnp.stack([across, upward // 2 % 2, upward % 2]).astype(jnp.int32)
    size = leaf_operator.shape[0]
    mine = pl.pallas_call(
        build_kernel,
        out_shape=jax.ShapeDtypeStruct((LEAF, LEAF), F32),
        in_specs=[pl.BlockSpec(memory_space=pltpu.SMEM)] * 3
        + [pl.BlockSpec(memory_space=pltpu.HBM)] * 3,
        out_specs=pl.BlockSpec(memory_space=pltpu.VMEM),
        scratch_shapes=[
            pltpu.VMEM(region_eps.shape, F32),
            pltpu.VMEM((128, size), F32),
            pltpu.VMEM((size - LEAF - 128, size), F32),
            pltpu.VMEM((LEAF, size), F32),
            pltpu.SemaphoreType.DMA((5,)),
        ],
        compiler_params=pltpu.CompilerParams(vmem_limit_bytes=32 * 1024 * 1024),
        name="leaf_build",
    )(
        region_labels,
        build_flags,
        wave_sq,
        *(
            pltpu.with_memory_space_constraint(x, pltpu.HBM)
            for x in (leaf_maps[0, 0], leaf_operator, region_eps)
        ),
    )
    theirs = swapped(mine, "by", 0)
    one, two, link, *solved = run(
        first_kernel,
        shapes((CUT_TWO, 128), (512 - CUT_TWO, 128), (FACE, 128)) + pair(FACE, 6 * FACE),
        place,
        mine,
        theirs,
        name="first_merge",
    )
    received_one = swapped(one, "bx", 0)
    received_two = swapped(two, "bx", 0)
    (outer,) = run(
        rows_kernel,
        shapes((96, 6 * FACE)),
        place,
        mine,
        theirs,
        *solved,
        scratch_shapes=[pltpu.VMEM((192, 6 * FACE), F32), pltpu.VMEM((192, 128), F32)],
        name="first_rows",
    )
    *inverse, outer_high, outer_low = run(
        second_kernel,
        pair(128, 128) + pair(96, 128),
        one,
        received_one,
        outer,
        scalars=0,
        cost_estimate=LONG,
        name="second_inverse",
    )
    one, two, *right = run(
        exchange_kernel,
        shapes((CUT_THREE, 128), (512 - CUT_THREE, 128)) + pair(128, 8 * FACE),
        place,
        one,
        two,
        received_one,
        received_two,
        link,
        *inverse,
        name="second_merge",
    )
    received_one = swapped(one, "by", 1)
    received_two = swapped(two, "by", 1)
    (rows,) = run(
        outer_kernel,
        shapes((96, 8 * FACE)),
        place,
        outer,
        outer_high,
        outer_low,
        *inverse,
        *right,
        name="second_rows",
    )
    half, *solved = run(
        third_kernel,
        shapes((96, 6 * FACE)) + pair(96, 128),
        one,
        two,
        received_one,
        rows,
        scalars=0,
        cost_estimate=LONG,
        name="third_inverse",
    )
    (result,) = run(
        last_kernel,
        shapes((96, 12 * FACE)),
        place,
        half,
        received_one,
        received_two,
        *solved,
        scratch_shapes=[pltpu.VMEM((3, 96, 128), F32), pltpu.SemaphoreType.DMA((4,))],
        out_space=pltpu.HBM,
        name="third_merge",
    )
    return result.reshape((1, 1, 96, 12 * FACE))


def solution(mesh):
    placed = (
        P(("freq", "bx"), "by", None, None),
        P(),
        P(),
        P("freq"),
        P("bx", "by"),
        P("bx", "by"),
    )
    return jax.shard_map(
        body,
        mesh=mesh,
        in_specs=placed,
        out_specs=P(("freq", "bx"), "by", None, None),
        check_vma=False,
    )
```

```python
import jax
import jax.numpy as jnp
from jax import lax
from jax.experimental import pallas as pl
from jax.experimental.pallas import tpu as pltpu
from jax.sharding import PartitionSpec as P

FACE = 64
LEAF = 4 * FACE
CUT_TWO, CUT_THREE = 192, 144
F32 = jnp.float32
BF16 = jnp.bfloat16


LONG = pl.CostEstimate(flops=10**10, bytes_accessed=10**8, transcendentals=10**6)


def swapped(shard, axis, stride):
    return lax.ppermute(shard, axis, [(i, i ^ 1 << stride) for i in range(lax.axis_size(axis))])


def split(x):
    high = x.astype(BF16)
    return high, (x - high.astype(F32)).astype(BF16)


def thirds(x):
    high = x.astype(BF16).astype(F32)
    rest = x - high
    middle = rest.astype(BF16).astype(F32)
    return high, middle, (rest - middle).astype(BF16).astype(F32)


def dot(a, b):
    return jnp.dot(a, b, preferred_element_type=F32)


def product(a, b):
    (a_high, a_low), (b_high, b_low) = a, b
    depth = a_high.shape[1]
    if depth % 128 and depth != FACE:
        return dot(a_high, b_high) + (dot(a_high, b_low) + dot(a_low, b_high))
    twice = dot(
        jnp.concatenate([a_high, a_low], axis=1), jnp.concatenate([b_high, b_high], axis=0)
    )
    return twice + dot(a_high, b_low)


def tree(terms):
    while len(terms) > 1:
        terms = [x + y for x, y in zip(terms[::2], terms[1::2])]
    return terms[0]


def minus(value, terms):
    for term in terms:
        value = value - term
    return value


def spd_inverse(matrix, left=None, both=False, panel=4, look=6, half=4):
    size = matrix.shape[0]
    shape = (8, size)
    count = size // 8
    tiles = [matrix[8 * g : 8 * g + 8] for g in range(count)]
    lane = lax.broadcasted_iota(jnp.int32, shape, 1)
    sub = lax.broadcasted_iota(jnp.int32, shape, 0)

    def column(tile, c):
        return jnp.broadcast_to(tile[:, c : c + 1], shape)

    def row(tile, r):
        return jnp.broadcast_to(tile[r : r + 1, :], shape)

    def inside(start, stop):
        return (lane >= start) & (lane < stop)

    pivot = [column(tiles[0], j) for j in range(8)]
    head = row(pivot[0], 0)
    for start in range(0, count, panel):
        stop = min(start + panel, count)
        last = min(stop + look, count)
        outside = [*range(last, count), *range(start if left is None or both else 0)]
        if outside:
            strip = jnp.concatenate([tiles[g] for g in outside], axis=0)[:, 8 * start : 8 * stop]
            high, middle, low = thirds(strip)
            factors = jnp.concatenate([high, high, middle, high, low, middle], axis=1).astype(BF16)
        for k in range(start, stop):
            first = 8 * k
            block = inside(first, first + 8)
            rows = jnp.where(block, (lane - first == sub).astype(F32), tiles[k])
            ahead = k + 1 < count
            if ahead:
                after = jnp.where(block, 0.0, tiles[k + 1])
                side = [column(tiles[k + 1], first + j) for j in range(8)]
            scale = None
            for p in range(8):
                inverse = pl.reciprocal(head, approx=True)
                if p < 7:
                    element = row(pivot[p + 1], p)
                    head = row(pivot[p + 1], p + 1) - element * (element * inverse)
                factor = jnp.where(sub == p, 0.0, pivot[p]) * inverse
                picked = row(rows, p)
                if ahead:
                    edge = side[p]
                    factor_ahead = edge * inverse
                    if p == half:
                        coming = [column(after, first + 8 + j) for j in range(8)]
                    if p == 7:
                        element = row(edge, 0)
                        head = row(coming[0], 0) - element * (element * inverse)
                    if p >= half:
                        for j in range(8):
                            coming[j] = coming[j] - factor_ahead * row(edge, j)
                    after = after - factor_ahead * picked
                for j in range(p + 1, 8):
                    element = row(pivot[j], p)
                    pivot[j] = pivot[j] - factor * element
                    if ahead:
                        side[j] = side[j] - factor_ahead * element
                rows = rows - factor * picked
                scale = inverse if scale is None else jnp.where(sub == p, inverse, scale)
            rows = rows * scale
            picked = [row(rows, j) for j in range(8)]
            for g in range(start, last):
                if g == k:
                    tiles[g] = rows
                elif g == k + 1:
                    tiles[g] = after
                else:
                    terms = [column(tiles[g], first + j) * picked[j] for j in range(8)]
                    cleared = jnp.where(block, 0.0, tiles[g])
                    tiles[g] = cleared - tree(terms) if count <= panel else minus(cleared, terms)
            if ahead:
                pivot = coming
        solved = jnp.concatenate(tiles[start:stop], axis=0)
        if outside:
            high, middle, low = thirds(solved)
            right = jnp.concatenate([high, middle, high, low, high, middle], axis=0).astype(BF16)
            update = dot(factors, right)
            block = inside(8 * start, 8 * stop)
            for i, g in enumerate(outside):
                tiles[g] = jnp.where(block, 0.0, tiles[g]) - update[8 * i : 8 * i + 8]
        if left is not None:
            blanks = [jnp.zeros((rows, size), BF16) for rows in (8 * start, size - 8 * stop)]
            right = [
                jnp.concatenate([x for x in (blanks[0], part, blanks[1]) if x.shape[0]], axis=0)
                for part in split(solved)
            ]
            columns = lax.broadcasted_iota(jnp.int32, left.shape, 1)
            block = (columns >= 8 * start) & (columns < 8 * stop)
            left = jnp.where(block, 0.0, left) - product(split(left), right)
    if left is not None and not both:
        return left
    whole = jnp.concatenate(tiles, axis=0)
    return (whole, left) if both else whole


def build_kernel(label, flag, wave, given, operator, table_at, out, table, one, two, edge, sems):
    size = operator.shape[0]
    middle = LEAF + 128
    copies = [
        pltpu.make_async_copy(source, target, sems.at[i])
        for i, (source, target) in enumerate(
            (
                (operator.at[pl.ds(LEAF, 128)], one),
                (table_at, table),
                (operator.at[pl.ds(middle, size - middle)], two),
                (operator.at[pl.ds(0, LEAF)], edge),
                (given, out),
            )
        )
    ]
    flagged = flag[0, 0] > 0

    @pl.when(jnp.logical_not(flagged))
    def _():
        copies[4].start()
        copies[4].wait()

    @pl.when(flagged)
    def _():
        for copy in copies[:4]:
            copy.start()
        for copy in copies[:2]:
            copy.wait()
        shift = wave[0] * table[pl.ds(label[0, 0], 1), :]
        border, near, far = slice(0, LEAF), slice(LEAF, middle), slice(middle, size)

        def shifted(ref, span):
            block = ref[:, span]
            ids = lax.broadcasted_iota(jnp.int32, block.shape, 0)
            diagonal = ids == lax.broadcasted_iota(jnp.int32, block.shape, 1)
            return block - jnp.where(diagonal, shift[:, span], 0.0)

        right = split(one[:, border]), split(one[:, far])
        copies[2].wait()
        inverse, left = spd_inverse(shifted(one, near), two[:, near], both=True)
        copies[3].wait()
        left = split(left)
        inner = shifted(two, far) + product(left, right[1])
        coupled = split(two[:, border] + product(left, right[0]))
        left = split(edge[:, near])
        left = split(product(left, split(inverse)))
        merged = shifted(edge, border) - product(left, right[0])
        across = split(edge[:, far] - product(left, right[1]))
        inverse = split(spd_inverse(inner))
        solved = split(product(inverse, coupled))
        out[...] = merged - product(across, solved)


def halves(shape):
    return lax.broadcasted_iota(jnp.int32, shape, 1) < FACE


def turn(tile):
    return pltpu.roll(tile, FACE, 1)


def leaf_rows(place, mine, theirs):
    across, third, lead = place[0], place[1], place[2]
    is_alpha = lead == 0
    left = halves((FACE, 128))

    def load(alpha, block, tile):
        spot = pl.ds(pl.multiple_of(block * FACE, FACE), FACE)
        span = slice(128 * tile, 128 * tile + 128)
        own = is_alpha if alpha else jnp.logical_not(is_alpha)
        return jnp.where(own, mine[spot, span], theirs[spot, span])

    def alpha_rows(block):
        sides = load(True, block, 0)
        ends = load(True, block, 1)
        sides = jnp.where(across == 0, turn(sides), sides)
        tiles = (
            jnp.where(left, sides, 0.0),
            jnp.where(left, jnp.where(third == 0, 0.0, ends), sides),
            jnp.where(left & (third == 0), ends, 0.0),
        )
        return jnp.concatenate(tiles, axis=1), turn(ends)

    def beta_rows(block):
        sides = load(False, block, 0)
        ends = load(False, block, 1)
        other = turn(sides)
        near_far = jnp.where(across == 0, other, sides)
        far_near = jnp.where(across == 0, sides, other)
        flipped = turn(ends)
        tiles = (
            jnp.where(left, 0.0, far_near),
            jnp.where(left & (third == 0), flipped, 0.0),
            jnp.where(
                third == 0,
                jnp.where(left, 0.0, near_far),
                jnp.where(left, far_near, ends),
            ),
        )
        return jnp.concatenate(tiles, axis=1), ends

    return alpha_rows, beta_rows


def either(flag, one, other):
    return [jnp.where(flag, x, y) for x, y in zip(one, other)]


def stacked(one, two, start, stop):
    cut = one.shape[0]
    parts = []
    if start < cut:
        parts.append(one[start : min(stop, cut), :])
    if stop > cut:
        parts.append(two[max(start, cut) - cut : stop - cut, :])
    return jnp.concatenate(parts, axis=0)


def stack(one, two, start, value):
    cut = one.shape[0]
    stop = start + value.shape[0]
    if start < cut:
        one[start : min(stop, cut), :] = value[: cut - start]
    if stop > cut:
        two[max(start, cut) - cut : stop - cut, :] = value[max(cut - start, 0) :]


def first_kernel(place, mine, theirs, message_one, message_two, link, solved_high, solved_low):
    alpha_rows, beta_rows = leaf_rows(place, mine, theirs)
    near = jnp.where(place[0] == 0, 1, 0)
    tiles_a, meet_a = alpha_rows(3)
    tiles_b, meet_b = beta_rows(2)
    system = (meet_a + meet_b)[:, :FACE]
    right = split(tiles_a + tiles_b)
    parts = [alpha_rows(near), beta_rows(near), either(place[1] == 0, beta_rows(3), alpha_rows(2))]
    direct = jnp.concatenate([tiles for tiles, _ in parts], axis=0)
    coupling = split(jnp.concatenate([meet for _, meet in parts], axis=0)[:, :FACE])
    inverse = split(spd_inverse(system, panel=8))
    solved = split(product(inverse, right))
    merged = direct - product(coupling, solved)
    for i in range(3):
        stack(message_one, message_two, 128 * i, merged[0:128, 128 * i : 128 * i + 128])
    stack(message_one, message_two, 384, merged[128:192, 128:256])
    stack(message_one, message_two, 448, merged[128:192, 256:384])
    link[...] = merged[128:192, 0:128]
    solved_high[...], solved_low[...] = solved


def rows_kernel(place, mine, theirs, solved_high, solved_low, outer, direct, coupling):
    alpha_rows, beta_rows = leaf_rows(place, mine, theirs)
    third, lead = place[1], place[2]
    far = jnp.where(place[0] == 0, 0, 1)
    direct[0:64, :], coupling[0:64, :] = alpha_rows(far)
    at_two = alpha_rows(2)
    at_far = beta_rows(far)
    at_three = beta_rows(3)
    direct[64:128, :], coupling[64:128, :] = either(third == 0, at_two, at_far)
    direct[128:192, :], coupling[128:192, :] = either(third == 0, at_far, at_three)
    spot = pl.ds(pl.multiple_of(lead * 96, 32), 96)
    solved = solved_high[...], solved_low[...]
    outer[...] = direct[spot, :] - product(split(coupling[spot, :][:, :FACE]), solved)


def second_kernel(own, received, outer, inverse_high, inverse_low, outer_high, outer_low):
    outer_high[...], outer_low[...] = split(outer[:, 0:128])
    system = own[0:128, :] + received[0:128, :]
    inverse_high[...], inverse_low[...] = split(spd_inverse(system))


def assemble(alpha, beta):
    rows = (alpha or beta)[0].shape[0]
    left = halves((rows, 128))
    blank = jnp.zeros((rows, 128), F32)
    if alpha is None:
        tiles = (
            jnp.where(left, 0.0, turn(beta[0])),
            blank,
            jnp.where(left, 0.0, beta[0]),
            beta[1],
        )
        return jnp.concatenate(tiles, axis=1)
    turned = turn(alpha[1])
    middle = jnp.where(left, turn(alpha[0]), turned)
    if beta is None:
        tiles = jnp.where(left, alpha[0], 0.0), middle, jnp.where(left, turned, 0.0), blank
        return jnp.concatenate(tiles, axis=1)
    tiles = (
        jnp.where(left, alpha[0], turn(beta[0])),
        middle,
        jnp.where(left, turned, beta[0]),
        beta[1],
    )
    return jnp.concatenate(tiles, axis=1)


def exchange_kernel(
    place,
    own_one,
    own_two,
    received_one,
    received_two,
    link,
    inverse_high,
    inverse_low,
    message_one,
    message_two,
    right_high,
    right_low,
):
    is_alpha = place[0] == 0

    def both(mine, other):
        return jnp.where(is_alpha, mine, other), jnp.where(is_alpha, other, mine)

    def part(start, stop):
        return both(stacked(own_one, own_two, start, stop), stacked(received_one, received_two, start, stop))

    one, two = part(128, 256), part(256, 384)
    right = split(assemble((one[0], two[0]), (one[1], two[1])))
    face, back = part(384, 448), part(448, 512)
    direct = jnp.concatenate(
        [assemble((face[0], back[0]), None), assemble(None, (face[1], back[1]))], axis=0
    )
    mine = link[...]
    other = jnp.transpose(stacked(received_one, received_two, 128, 256))[0:FACE]
    coupling = jnp.concatenate(
        [jnp.where(is_alpha, mine, other), jnp.where(is_alpha, other, mine)], axis=0
    )
    solved = split(product(split(coupling), (inverse_high[...], inverse_low[...])))
    merged = direct - product(solved, right)
    for i in range(4):
        stack(message_one, message_two, 128 * i, merged[:, 128 * i : 128 * i + 128])
    right_high[...], right_low[...] = right


def rest_columns(one, two):
    return jnp.concatenate(
        [stacked(one, two, 128 * i, 128 * i + 128) for i in range(1, 4)], axis=1
    )


def outer_kernel(place, outer, outer_high, outer_low, inverse_high, inverse_low, right_high, right_low, rows):
    mine = outer[:, 128:256], outer[:, 256:384]
    direct = jnp.where(place[0] == 0, assemble(mine, None), assemble(None, mine))
    solved = split(product((outer_high[...], outer_low[...]), (inverse_high[...], inverse_low[...])))
    rows[...] = direct - product(solved, (right_high[...], right_low[...]))


def third_kernel(own_one, own_two, received, rows, half, solved_high, solved_low):
    right = split(rest_columns(own_one, own_two))
    system = own_one[0:128, :] + received[0:128, :]
    solved = split(spd_inverse(system, rows[:, 0:128]))
    half[...] = rows[:, 128:512] + product(solved, right)
    solved_high[...], solved_low[...] = solved


def last_kernel(
    place, half, received_one, received_two, solved_high, solved_low, out, other, sems
):
    third = place[1]
    width = 6 * FACE

    def copy(source, side, start, i):
        first = pl.multiple_of(side * width + start, 128)
        target = out.at[:, pl.ds(first, source.shape[1])]
        return pltpu.make_async_copy(source, target, sems.at[i])

    copies = [copy(half, third, 0, 0)]
    copies[0].start()
    solved = solved_high[...], solved_low[...]
    for i in range(3):
        right = split(stacked(received_one, received_two, 128 * i + 128, 128 * i + 256))
        other[i] = product(solved, right)
        copies.append(copy(other.at[i], 1 - third, 128 * i, i + 1))
        copies[-1].start()
    for x in copies:
        x.wait()


def shapes(*sizes):
    return [jax.ShapeDtypeStruct(size, F32) for size in sizes]


def pair(*size):
    return [jax.ShapeDtypeStruct(size, BF16)] * 2


def run(kernel, out_shape, *operands, scalars=1, out_space=pltpu.VMEM, **options):
    smem = pl.BlockSpec(memory_space=pltpu.SMEM)
    vmem = pl.BlockSpec(memory_space=pltpu.VMEM)
    return pl.pallas_call(
        kernel,
        out_shape=out_shape,
        in_specs=[smem] * scalars + [vmem] * (len(operands) - scalars),
        out_specs=[pl.BlockSpec(memory_space=out_space)] * len(out_shape),
        compiler_params=pltpu.CompilerParams(vmem_limit_bytes=32 * 1024 * 1024),
        **options,
    )(*operands)


def body(leaf_maps, leaf_operator, region_eps, wave_sq, region_labels, build_flags):
    across = lax.axis_index("bx") % 2
    upward = lax.axis_index("by")
    place = jnp.stack([across, upward // 2 % 2, upward % 2]).astype(jnp.int32)
    size = leaf_operator.shape[0]
    mine = pl.pallas_call(
        build_kernel,
        out_shape=jax.ShapeDtypeStruct((LEAF, LEAF), F32),
        in_specs=[pl.BlockSpec(memory_space=pltpu.SMEM)] * 3
        + [pl.BlockSpec(memory_space=pltpu.HBM)] * 3,
        out_specs=pl.BlockSpec(memory_space=pltpu.VMEM),
        scratch_shapes=[
            pltpu.VMEM(region_eps.shape, F32),
            pltpu.VMEM((128, size), F32),
            pltpu.VMEM((size - LEAF - 128, size), F32),
            pltpu.VMEM((LEAF, size), F32),
            pltpu.SemaphoreType.DMA((5,)),
        ],
        compiler_params=pltpu.CompilerParams(vmem_limit_bytes=32 * 1024 * 1024),
        name="leaf_build",
    )(
        region_labels,
        build_flags,
        wave_sq,
        *(
            pltpu.with_memory_space_constraint(x, pltpu.HBM)
            for x in (leaf_maps[0, 0], leaf_operator, region_eps)
        ),
    )
    theirs = swapped(mine, "by", 0)
    one, two, link, *solved = run(
        first_kernel,
        shapes((CUT_TWO, 128), (512 - CUT_TWO, 128), (FACE, 128)) + pair(FACE, 6 * FACE),
        place,
        mine,
        theirs,
        name="first_merge",
    )
    received_one = swapped(one, "bx", 0)
    received_two = swapped(two, "bx", 0)
    (outer,) = run(
        rows_kernel,
        shapes((96, 6 * FACE)),
        place,
        mine,
        theirs,
        *solved,
        scratch_shapes=[pltpu.VMEM((192, 6 * FACE), F32), pltpu.VMEM((192, 128), F32)],
        name="first_rows",
    )
    *inverse, outer_high, outer_low = run(
        second_kernel,
        pair(128, 128) + pair(96, 128),
        one,
        received_one,
        outer,
        scalars=0,
        cost_estimate=LONG,
        name="second_inverse",
    )
    one, two, *right = run(
        exchange_kernel,
        shapes((CUT_THREE, 128), (512 - CUT_THREE, 128)) + pair(128, 8 * FACE),
        place,
        one,
        two,
        received_one,
        received_two,
        link,
        *inverse,
        name="second_merge",
    )
    received_one = swapped(one, "by", 1)
    received_two = swapped(two, "by", 1)
    (rows,) = run(
        outer_kernel,
        shapes((96, 8 * FACE)),
        place,
        outer,
        outer_high,
        outer_low,
        *inverse,
        *right,
        name="second_rows",
    )
    half, *solved = run(
        third_kernel,
        shapes((96, 6 * FACE)) + pair(96, 128),
        one,
        two,
        received_one,
        rows,
        scalars=0,
        cost_estimate=LONG,
        name="third_inverse",
    )
    (result,) = run(
        last_kernel,
        shapes((96, 12 * FACE)),
        place,
        half,
        received_one,
        received_two,
        *solved,
        scratch_shapes=[pltpu.VMEM((3, 96, 128), F32), pltpu.SemaphoreType.DMA((4,))],
        out_space=pltpu.HBM,
        name="third_merge",
    )
    return result.reshape((1, 1, 96, 12 * FACE))


def solution(mesh):
    placed = (
        P(("freq", "bx"), "by", None, None),
        P(),
        P(),
        P("freq"),
        P("bx", "by"),
        P("bx", "by"),
    )
    return jax.shard_map(
        body,
        mesh=mesh,
        in_specs=placed,
        out_specs=P(("freq", "bx"), "by", None, None),
        check_vma=False,
    )
```

```python
import jax
import jax.numpy as jnp
from jax import lax
from jax.experimental import pallas as pl
from jax.experimental.pallas import tpu as pltpu
from jax.sharding import PartitionSpec as P

FACE = 64
LEAF = 4 * FACE
CUT_TWO, CUT_THREE = 200, 160
F32 = jnp.float32
BF16 = jnp.bfloat16


LONG = pl.CostEstimate(flops=10**10, bytes_accessed=10**8, transcendentals=10**6)


def swapped(shard, axis, stride):
    return lax.ppermute(shard, axis, [(i, i ^ 1 << stride) for i in range(lax.axis_size(axis))])


def split(x):
    high = x.astype(BF16)
    return high, (x - high.astype(F32)).astype(BF16)


def thirds(x):
    high = x.astype(BF16).astype(F32)
    rest = x - high
    middle = rest.astype(BF16).astype(F32)
    return high, middle, (rest - middle).astype(BF16).astype(F32)


def dot(a, b):
    return jnp.dot(a, b, preferred_element_type=F32)


def product(a, b):
    (a_high, a_low), (b_high, b_low) = a, b
    depth = a_high.shape[1]
    if depth % 128 and depth != FACE:
        return dot(a_high, b_high) + (dot(a_high, b_low) + dot(a_low, b_high))
    twice = dot(
        jnp.concatenate([a_high, a_low], axis=1), jnp.concatenate([b_high, b_high], axis=0)
    )
    return twice + dot(a_high, b_low)


def tree(terms):
    while len(terms) > 1:
        terms = [x + y for x, y in zip(terms[::2], terms[1::2])]
    return terms[0]


def minus(value, terms):
    for term in terms:
        value = value - term
    return value


def spd_inverse(matrix, left=None, both=False, panel=4, look=4, half=4):
    size = matrix.shape[0]
    shape = (8, size)
    count = size // 8
    tiles = [matrix[8 * g : 8 * g + 8] for g in range(count)]
    lane = lax.broadcasted_iota(jnp.int32, shape, 1)
    sub = lax.broadcasted_iota(jnp.int32, shape, 0)

    def column(tile, c):
        return jnp.broadcast_to(tile[:, c : c + 1], shape)

    def row(tile, r):
        return jnp.broadcast_to(tile[r : r + 1, :], shape)

    def inside(start, stop):
        return (lane >= start) & (lane < stop)

    pivot = [column(tiles[0], j) for j in range(8)]
    head = row(pivot[0], 0)
    for start in range(0, count, panel):
        stop = min(start + panel, count)
        last = min(stop + look, count)
        outside = [*range(last, count), *range(start if left is None or both else 0)]
        if outside:
            strip = jnp.concatenate([tiles[g] for g in outside], axis=0)[:, 8 * start : 8 * stop]
            high, middle, low = thirds(strip)
            factors = jnp.concatenate([high, high, middle, high, low, middle], axis=1).astype(BF16)
        for k in range(start, stop):
            first = 8 * k
            block = inside(first, first + 8)
            rows = jnp.where(block, (lane - first == sub).astype(F32), tiles[k])
            ahead = k + 1 < count
            if ahead:
                after = jnp.where(block, 0.0, tiles[k + 1])
                side = [column(tiles[k + 1], first + j) for j in range(8)]
            scale = None
            for p in range(8):
                inverse = pl.reciprocal(head, approx=True)
                if p < 7:
                    element = row(pivot[p + 1], p)
                    head = row(pivot[p + 1], p + 1) - element * (element * inverse)
                factor = jnp.where(sub == p, 0.0, pivot[p]) * inverse
                picked = row(rows, p)
                if ahead:
                    edge = side[p]
                    factor_ahead = edge * inverse
                    if p == half:
                        coming = [column(after, first + 8 + j) for j in range(8)]
                    if p == 7:
                        element = row(edge, 0)
                        head = row(coming[0], 0) - element * (element * inverse)
                    if p >= half:
                        for j in range(8):
                            coming[j] = coming[j] - factor_ahead * row(edge, j)
                    after = after - factor_ahead * picked
                for j in range(p + 1, 8):
                    element = row(pivot[j], p)
                    pivot[j] = pivot[j] - factor * element
                    if ahead:
                        side[j] = side[j] - factor_ahead * element
                rows = rows - factor * picked
                scale = inverse if scale is None else jnp.where(sub == p, inverse, scale)
            rows = rows * scale
            picked = [row(rows, j) for j in range(8)]
            for g in range(start, last):
                if g == k:
                    tiles[g] = rows
                elif g == k + 1:
                    tiles[g] = after
                else:
                    terms = [column(tiles[g], first + j) * picked[j] for j in range(8)]
                    cleared = jnp.where(block, 0.0, tiles[g])
                    tiles[g] = cleared - tree(terms) if count <= panel else minus(cleared, terms)
            if ahead:
                pivot = coming
        solved = jnp.concatenate(tiles[start:stop], axis=0)
        if outside:
            high, middle, low = thirds(solved)
            right = jnp.concatenate([high, middle, high, low, high, middle], axis=0).astype(BF16)
            update = dot(factors, right)
            block = inside(8 * start, 8 * stop)
            for i, g in enumerate(outside):
                tiles[g] = jnp.where(block, 0.0, tiles[g]) - update[8 * i : 8 * i + 8]
        if left is not None:
            blanks = [jnp.zeros((rows, size), BF16) for rows in (8 * start, size - 8 * stop)]
            right = [
                jnp.concatenate([x for x in (blanks[0], part, blanks[1]) if x.shape[0]], axis=0)
                for part in split(solved)
            ]
            columns = lax.broadcasted_iota(jnp.int32, left.shape, 1)
            block = (columns >= 8 * start) & (columns < 8 * stop)
            left = jnp.where(block, 0.0, left) - product(split(left), right)
    if left is not None and not both:
        return left
    whole = jnp.concatenate(tiles, axis=0)
    return (whole, left) if both else whole


def build_kernel(label, flag, wave, given, operator, table_at, out, table, one, two, edge, sems):
    size = operator.shape[0]
    middle = LEAF + 128
    copies = [
        pltpu.make_async_copy(source, target, sems.at[i])
        for i, (source, target) in enumerate(
            (
                (operator.at[pl.ds(LEAF, 128)], one),
                (table_at, table),
                (operator.at[pl.ds(middle, size - middle)], two),
                (operator.at[pl.ds(0, LEAF)], edge),
                (given, out),
            )
        )
    ]
    flagged = flag[0, 0] > 0

    @pl.when(jnp.logical_not(flagged))
    def _():
        copies[4].start()
        copies[4].wait()

    @pl.when(flagged)
    def _():
        for copy in copies[:4]:
            copy.start()
        for copy in copies[:2]:
            copy.wait()
        shift = wave[0] * table[pl.ds(label[0, 0], 1), :]
        border, near, far = slice(0, LEAF), slice(LEAF, middle), slice(middle, size)

        def shifted(ref, span):
            block = ref[:, span]
            ids = lax.broadcasted_iota(jnp.int32, block.shape, 0)
            diagonal = ids == lax.broadcasted_iota(jnp.int32, block.shape, 1)
            return block - jnp.where(diagonal, shift[:, span], 0.0)

        right = split(one[:, border]), split(one[:, far])
        copies[2].wait()
        inverse, left = spd_inverse(shifted(one, near), two[:, near], both=True)
        copies[3].wait()
        left = split(left)
        inner = shifted(two, far) + product(left, right[1])
        coupled = split(two[:, border] + product(left, right[0]))
        left = split(edge[:, near])
        left = split(product(left, split(inverse)))
        merged = shifted(edge, border) - product(left, right[0])
        across = split(edge[:, far] - product(left, right[1]))
        inverse = split(spd_inverse(inner))
        solved = split(product(inverse, coupled))
        out[...] = merged - product(across, solved)


def halves(shape):
    return lax.broadcasted_iota(jnp.int32, shape, 1) < FACE


def turn(tile):
    return pltpu.roll(tile, FACE, 1)


def leaf_rows(place, mine, theirs):
    across, third, lead = place[0], place[1], place[2]
    is_alpha = lead == 0
    left = halves((FACE, 128))

    def load(alpha, block, tile):
        spot = pl.ds(pl.multiple_of(block * FACE, FACE), FACE)
        span = slice(128 * tile, 128 * tile + 128)
        own = is_alpha if alpha else jnp.logical_not(is_alpha)
        return jnp.where(own, mine[spot, span], theirs[spot, span])

    def alpha_rows(block):
        sides = load(True, block, 0)
        ends = load(True, block, 1)
        sides = jnp.where(across == 0, turn(sides), sides)
        tiles = (
            jnp.where(left, sides, 0.0),
            jnp.where(left, jnp.where(third == 0, 0.0, ends), sides),
            jnp.where(left & (third == 0), ends, 0.0),
        )
        return jnp.concatenate(tiles, axis=1), turn(ends)

    def beta_rows(block):
        sides = load(False, block, 0)
        ends = load(False, block, 1)
        other = turn(sides)
        near_far = jnp.where(across == 0, other, sides)
        far_near = jnp.where(across == 0, sides, other)
        flipped = turn(ends)
        tiles = (
            jnp.where(left, 0.0, far_near),
            jnp.where(left & (third == 0), flipped, 0.0),
            jnp.where(
                third == 0,
                jnp.where(left, 0.0, near_far),
                jnp.where(left, far_near, ends),
            ),
        )
        return jnp.concatenate(tiles, axis=1), ends

    return alpha_rows, beta_rows


def either(flag, one, other):
    return [jnp.where(flag, x, y) for x, y in zip(one, other)]


def stacked(one, two, start, stop):
    cut = one.shape[0]
    parts = []
    if start < cut:
        parts.append(one[start : min(stop, cut), :])
    if stop > cut:
        parts.append(two[max(start, cut) - cut : stop - cut, :])
    return jnp.concatenate(parts, axis=0)


def stack(one, two, start, value):
    cut = one.shape[0]
    stop = start + value.shape[0]
    if start < cut:
        one[start : min(stop, cut), :] = value[: cut - start]
    if stop > cut:
        two[max(start, cut) - cut : stop - cut, :] = value[max(cut - start, 0) :]


def first_kernel(place, mine, theirs, message_one, message_two, link, solved_high, solved_low):
    alpha_rows, beta_rows = leaf_rows(place, mine, theirs)
    near = jnp.where(place[0] == 0, 1, 0)
    tiles_a, meet_a = alpha_rows(3)
    tiles_b, meet_b = beta_rows(2)
    system = (meet_a + meet_b)[:, :FACE]
    right = split(tiles_a + tiles_b)
    parts = [alpha_rows(near), beta_rows(near), either(place[1] == 0, beta_rows(3), alpha_rows(2))]
    direct = jnp.concatenate([tiles for tiles, _ in parts], axis=0)
    coupling = split(jnp.concatenate([meet for _, meet in parts], axis=0)[:, :FACE])
    inverse = split(spd_inverse(system, panel=8))
    solved = split(product(inverse, right))
    merged = direct - product(coupling, solved)
    for i in range(3):
        stack(message_one, message_two, 128 * i, merged[0:128, 128 * i : 128 * i + 128])
    stack(message_one, message_two, 384, merged[128:192, 128:256])
    stack(message_one, message_two, 448, merged[128:192, 256:384])
    link[...] = merged[128:192, 0:128]
    solved_high[...], solved_low[...] = solved


def rows_kernel(place, mine, theirs, solved_high, solved_low, outer, direct, coupling):
    alpha_rows, beta_rows = leaf_rows(place, mine, theirs)
    third, lead = place[1], place[2]
    far = jnp.where(place[0] == 0, 0, 1)
    direct[0:64, :], coupling[0:64, :] = alpha_rows(far)
    at_two = alpha_rows(2)
    at_far = beta_rows(far)
    at_three = beta_rows(3)
    direct[64:128, :], coupling[64:128, :] = either(third == 0, at_two, at_far)
    direct[128:192, :], coupling[128:192, :] = either(third == 0, at_far, at_three)
    spot = pl.ds(pl.multiple_of(lead * 96, 32), 96)
    solved = solved_high[...], solved_low[...]
    outer[...] = direct[spot, :] - product(split(coupling[spot, :][:, :FACE]), solved)


def second_kernel(own, received, outer, inverse_high, inverse_low, outer_high, outer_low):
    outer_high[...], outer_low[...] = split(outer[:, 0:128])
    system = own[0:128, :] + received[0:128, :]
    inverse_high[...], inverse_low[...] = split(spd_inverse(system))


def assemble(alpha, beta):
    rows = (alpha or beta)[0].shape[0]
    left = halves((rows, 128))
    blank = jnp.zeros((rows, 128), F32)
    if alpha is None:
        tiles = (
            jnp.where(left, 0.0, turn(beta[0])),
            blank,
            jnp.where(left, 0.0, beta[0]),
            beta[1],
        )
        return jnp.concatenate(tiles, axis=1)
    turned = turn(alpha[1])
    middle = jnp.where(left, turn(alpha[0]), turned)
    if beta is None:
        tiles = jnp.where(left, alpha[0], 0.0), middle, jnp.where(left, turned, 0.0), blank
        return jnp.concatenate(tiles, axis=1)
    tiles = (
        jnp.where(left, alpha[0], turn(beta[0])),
        middle,
        jnp.where(left, turned, beta[0]),
        beta[1],
    )
    return jnp.concatenate(tiles, axis=1)


def exchange_kernel(
    place,
    own_one,
    own_two,
    received_one,
    received_two,
    link,
    inverse_high,
    inverse_low,
    message_one,
    message_two,
    right_high,
    right_low,
):
    is_alpha = place[0] == 0

    def both(mine, other):
        return jnp.where(is_alpha, mine, other), jnp.where(is_alpha, other, mine)

    def part(start, stop):
        return both(stacked(own_one, own_two, start, stop), stacked(received_one, received_two, start, stop))

    one, two = part(128, 256), part(256, 384)
    right = split(assemble((one[0], two[0]), (one[1], two[1])))
    face, back = part(384, 448), part(448, 512)
    direct = jnp.concatenate(
        [assemble((face[0], back[0]), None), assemble(None, (face[1], back[1]))], axis=0
    )
    mine = link[...]
    other = jnp.transpose(stacked(received_one, received_two, 128, 256))[0:FACE]
    coupling = jnp.concatenate(
        [jnp.where(is_alpha, mine, other), jnp.where(is_alpha, other, mine)], axis=0
    )
    solved = split(product(split(coupling), (inverse_high[...], inverse_low[...])))
    merged = direct - product(solved, right)
    for i in range(4):
        stack(message_one, message_two, 128 * i, merged[:, 128 * i : 128 * i + 128])
    right_high[...], right_low[...] = right


def rest_columns(one, two):
    return jnp.concatenate(
        [stacked(one, two, 128 * i, 128 * i + 128) for i in range(1, 4)], axis=1
    )


def outer_kernel(place, outer, outer_high, outer_low, inverse_high, inverse_low, right_high, right_low, rows):
    mine = outer[:, 128:256], outer[:, 256:384]
    direct = jnp.where(place[0] == 0, assemble(mine, None), assemble(None, mine))
    solved = split(product((outer_high[...], outer_low[...]), (inverse_high[...], inverse_low[...])))
    rows[...] = direct - product(solved, (right_high[...], right_low[...]))


def third_kernel(own_one, own_two, received, rows, half, solved_high, solved_low):
    right = split(rest_columns(own_one, own_two))
    system = own_one[0:128, :] + received[0:128, :]
    solved = split(spd_inverse(system, rows[:, 0:128]))
    half[...] = rows[:, 128:512] + product(solved, right)
    solved_high[...], solved_low[...] = solved


def last_kernel(
    place, half, received_one, received_two, solved_high, solved_low, out, other, sems
):
    third = place[1]
    width = 6 * FACE

    def copy(source, side, start, i):
        first = pl.multiple_of(side * width + start, 128)
        target = out.at[:, pl.ds(first, source.shape[1])]
        return pltpu.make_async_copy(source, target, sems.at[i])

    copies = [copy(half, third, 0, 0)]
    copies[0].start()
    solved = solved_high[...], solved_low[...]
    for i in range(3):
        right = split(stacked(received_one, received_two, 128 * i + 128, 128 * i + 256))
        other[i] = product(solved, right)
        copies.append(copy(other.at[i], 1 - third, 128 * i, i + 1))
        copies[-1].start()
    for x in copies:
        x.wait()


def shapes(*sizes):
    return [jax.ShapeDtypeStruct(size, F32) for size in sizes]


def pair(*size):
    return [jax.ShapeDtypeStruct(size, BF16)] * 2


def run(kernel, out_shape, *operands, scalars=1, out_space=pltpu.VMEM, **options):
    smem = pl.BlockSpec(memory_space=pltpu.SMEM)
    vmem = pl.BlockSpec(memory_space=pltpu.VMEM)
    return pl.pallas_call(
        kernel,
        out_shape=out_shape,
        in_specs=[smem] * scalars + [vmem] * (len(operands) - scalars),
        out_specs=[pl.BlockSpec(memory_space=out_space)] * len(out_shape),
        compiler_params=pltpu.CompilerParams(vmem_limit_bytes=32 * 1024 * 1024),
        **options,
    )(*operands)


def body(leaf_maps, leaf_operator, region_eps, wave_sq, region_labels, build_flags):
    across = lax.axis_index("bx") % 2
    upward = lax.axis_index("by")
    place = jnp.stack([across, upward // 2 % 2, upward % 2]).astype(jnp.int32)
    size = leaf_operator.shape[0]
    mine = pl.pallas_call(
        build_kernel,
        out_shape=jax.ShapeDtypeStruct((LEAF, LEAF), F32),
        in_specs=[pl.BlockSpec(memory_space=pltpu.SMEM)] * 3
        + [pl.BlockSpec(memory_space=pltpu.HBM)] * 3,
        out_specs=pl.BlockSpec(memory_space=pltpu.VMEM),
        scratch_shapes=[
            pltpu.VMEM(region_eps.shape, F32),
            pltpu.VMEM((128, size), F32),
            pltpu.VMEM((size - LEAF - 128, size), F32),
            pltpu.VMEM((LEAF, size), F32),
            pltpu.SemaphoreType.DMA((5,)),
        ],
        compiler_params=pltpu.CompilerParams(vmem_limit_bytes=32 * 1024 * 1024),
        name="leaf_build",
    )(
        region_labels,
        build_flags,
        wave_sq,
        *(
            pltpu.with_memory_space_constraint(x, pltpu.HBM)
            for x in (leaf_maps[0, 0], leaf_operator, region_eps)
        ),
    )
    theirs = swapped(mine, "by", 0)
    one, two, link, *solved = run(
        first_kernel,
        shapes((CUT_TWO, 128), (512 - CUT_TWO, 128), (FACE, 128)) + pair(FACE, 6 * FACE),
        place,
        mine,
        theirs,
        name="first_merge",
    )
    received_one = swapped(one, "bx", 0)
    received_two = swapped(two, "bx", 0)
    (outer,) = run(
        rows_kernel,
        shapes((96, 6 * FACE)),
        place,
        mine,
        theirs,
        *solved,
        scratch_shapes=[pltpu.VMEM((192, 6 * FACE), F32), pltpu.VMEM((192, 128), F32)],
        name="first_rows",
    )
    *inverse, outer_high, outer_low = run(
        second_kernel,
        pair(128, 128) + pair(96, 128),
        one,
        received_one,
        outer,
        scalars=0,
        cost_estimate=LONG,
        name="second_inverse",
    )
    one, two, *right = run(
        exchange_kernel,
        shapes((CUT_THREE, 128), (512 - CUT_THREE, 128)) + pair(128, 8 * FACE),
        place,
        one,
        two,
        received_one,
        received_two,
        link,
        *inverse,
        name="second_merge",
    )
    received_one = swapped(one, "by", 1)
    received_two = swapped(two, "by", 1)
    (rows,) = run(
        outer_kernel,
        shapes((96, 8 * FACE)),
        place,
        outer,
        outer_high,
        outer_low,
        *inverse,
        *right,
        name="second_rows",
    )
    half, *solved = run(
        third_kernel,
        shapes((96, 6 * FACE)) + pair(96, 128),
        one,
        two,
        received_one,
        rows,
        scalars=0,
        cost_estimate=LONG,
        name="third_inverse",
    )
    (result,) = run(
        last_kernel,
        shapes((96, 12 * FACE)),
        place,
        half,
        received_one,
        received_two,
        *solved,
        scratch_shapes=[pltpu.VMEM((3, 96, 128), F32), pltpu.SemaphoreType.DMA((4,))],
        out_space=pltpu.HBM,
        name="third_merge",
    )
    return result.reshape((1, 1, 96, 12 * FACE))


def solution(mesh):
    placed = (
        P(("freq", "bx"), "by", None, None),
        P(),
        P(),
        P("freq"),
        P("bx", "by"),
        P("bx", "by"),
    )
    return jax.shard_map(
        body,
        mesh=mesh,
        in_specs=placed,
        out_specs=P(("freq", "bx"), "by", None, None),
        check_vma=False,
    )
```

```python
import jax
import jax.numpy as jnp
from jax import lax
from jax.experimental import pallas as pl
from jax.experimental.pallas import tpu as pltpu
from jax.sharding import PartitionSpec as P

FACE = 64
LEAF = 4 * FACE
MESSAGE = 96 + 3 * 128
CUT_TWO, CUT_THREE = 184, 144
F32 = jnp.float32
BF16 = jnp.bfloat16


LONG = pl.CostEstimate(flops=10**10, bytes_accessed=10**8, transcendentals=10**6)


def swapped(shard, axis, stride):
    return lax.ppermute(shard, axis, [(i, i ^ 1 << stride) for i in range(lax.axis_size(axis))])


def split(x):
    high = x.astype(BF16)
    return high, (x - high.astype(F32)).astype(BF16)


def thirds(x):
    high = x.astype(BF16).astype(F32)
    rest = x - high
    middle = rest.astype(BF16).astype(F32)
    return high, middle, (rest - middle).astype(BF16).astype(F32)


def dot(a, b):
    return jnp.dot(a, b, preferred_element_type=F32)


def product(a, b):
    (a_high, a_low), (b_high, b_low) = a, b
    depth = a_high.shape[1]
    if depth % 128 and depth != FACE:
        return dot(a_high, b_high) + (dot(a_high, b_low) + dot(a_low, b_high))
    twice = dot(
        jnp.concatenate([a_high, a_low], axis=1), jnp.concatenate([b_high, b_high], axis=0)
    )
    return twice + dot(a_high, b_low)


def tree(terms):
    while len(terms) > 1:
        terms = [x + y for x, y in zip(terms[::2], terms[1::2])]
    return terms[0]


def minus(value, terms):
    for term in terms:
        value = value - term
    return value


def spd_inverse(matrix, left=None, both=False, panel=4, look=4, half=4):
    size = matrix.shape[0]
    shape = (8, size)
    count = size // 8
    tiles = [matrix[8 * g : 8 * g + 8] for g in range(count)]
    lane = lax.broadcasted_iota(jnp.int32, shape, 1)
    sub = lax.broadcasted_iota(jnp.int32, shape, 0)

    def column(tile, c):
        return jnp.broadcast_to(tile[:, c : c + 1], shape)

    def row(tile, r):
        return jnp.broadcast_to(tile[r : r + 1, :], shape)

    def inside(start, stop):
        return (lane >= start) & (lane < stop)

    pivot = [column(tiles[0], j) for j in range(8)]
    head = row(pivot[0], 0)
    for start in range(0, count, panel):
        stop = min(start + panel, count)
        last = min(stop + look, count)
        outside = [*range(last, count), *range(start if left is None or both else 0)]
        if outside:
            strip = jnp.concatenate([tiles[g] for g in outside], axis=0)[:, 8 * start : 8 * stop]
            high, middle, low = thirds(strip)
            factors = jnp.concatenate([high, high, middle, high, low, middle], axis=1).astype(BF16)
        for k in range(start, stop):
            first = 8 * k
            block = inside(first, first + 8)
            rows = jnp.where(block, (lane - first == sub).astype(F32), tiles[k])
            ahead = k + 1 < count
            if ahead:
                after = jnp.where(block, 0.0, tiles[k + 1])
                side = [column(tiles[k + 1], first + j) for j in range(8)]
            scale = None
            for p in range(8):
                inverse = pl.reciprocal(head, approx=True)
                if p < 7:
                    element = row(pivot[p + 1], p)
                    head = row(pivot[p + 1], p + 1) - element * (element * inverse)
                factor = jnp.where(sub == p, 0.0, pivot[p]) * inverse
                picked = row(rows, p)
                if ahead:
                    edge = side[p]
                    factor_ahead = edge * inverse
                    if p == half:
                        coming = [column(after, first + 8 + j) for j in range(8)]
                    if p == 7:
                        element = row(edge, 0)
                        head = row(coming[0], 0) - element * (element * inverse)
                    if p >= half:
                        for j in range(8):
                            coming[j] = coming[j] - factor_ahead * row(edge, j)
                    after = after - factor_ahead * picked
                for j in range(p + 1, 8):
                    element = row(pivot[j], p)
                    pivot[j] = pivot[j] - factor * element
                    if ahead:
                        side[j] = side[j] - factor_ahead * element
                rows = rows - factor * picked
                scale = inverse if scale is None else jnp.where(sub == p, inverse, scale)
            rows = rows * scale
            picked = [row(rows, j) for j in range(8)]
            for g in range(start, last):
                if g == k:
                    tiles[g] = rows
                elif g == k + 1:
                    tiles[g] = after
                else:
                    terms = [column(tiles[g], first + j) * picked[j] for j in range(8)]
                    cleared = jnp.where(block, 0.0, tiles[g])
                    tiles[g] = cleared - tree(terms) if count <= panel else minus(cleared, terms)
            if ahead:
                pivot = coming
        solved = jnp.concatenate(tiles[start:stop], axis=0)
        if outside:
            high, middle, low = thirds(solved)
            right = jnp.concatenate([high, middle, high, low, high, middle], axis=0).astype(BF16)
            update = dot(factors, right)
            block = inside(8 * start, 8 * stop)
            for i, g in enumerate(outside):
                tiles[g] = jnp.where(block, 0.0, tiles[g]) - update[8 * i : 8 * i + 8]
        if left is not None:
            blanks = [jnp.zeros((rows, size), BF16) for rows in (8 * start, size - 8 * stop)]
            right = [
                jnp.concatenate([x for x in (blanks[0], part, blanks[1]) if x.shape[0]], axis=0)
                for part in split(solved)
            ]
            columns = lax.broadcasted_iota(jnp.int32, left.shape, 1)
            block = (columns >= 8 * start) & (columns < 8 * stop)
            left = jnp.where(block, 0.0, left) - product(split(left), right)
    if left is not None and not both:
        return left
    whole = jnp.concatenate(tiles, axis=0)
    return (whole, left) if both else whole


def build_kernel(label, flag, wave, given, operator, table_at, out, table, one, two, edge, sems):
    size = operator.shape[0]
    middle = LEAF + 128
    copies = [
        pltpu.make_async_copy(source, target, sems.at[i])
        for i, (source, target) in enumerate(
            (
                (operator.at[pl.ds(LEAF, 128)], one),
                (table_at, table),
                (operator.at[pl.ds(middle, size - middle)], two),
                (operator.at[pl.ds(0, LEAF)], edge),
                (given, out),
            )
        )
    ]
    flagged = flag[0, 0] > 0

    @pl.when(jnp.logical_not(flagged))
    def _():
        copies[4].start()
        copies[4].wait()

    @pl.when(flagged)
    def _():
        for copy in copies[:4]:
            copy.start()
        for copy in copies[:2]:
            copy.wait()
        shift = wave[0] * table[pl.ds(label[0, 0], 1), :]
        border, near, far = slice(0, LEAF), slice(LEAF, middle), slice(middle, size)

        def shifted(ref, span):
            block = ref[:, span]
            ids = lax.broadcasted_iota(jnp.int32, block.shape, 0)
            diagonal = ids == lax.broadcasted_iota(jnp.int32, block.shape, 1)
            return block - jnp.where(diagonal, shift[:, span], 0.0)

        right = split(one[:, border]), split(one[:, far])
        copies[2].wait()
        inverse, left = spd_inverse(shifted(one, near), two[:, near], both=True)
        copies[3].wait()
        left = split(left)
        inner = shifted(two, far) + product(left, right[1])
        coupled = split(two[:, border] + product(left, right[0]))
        left = split(edge[:, near])
        left = split(product(left, split(inverse)))
        merged = shifted(edge, border) - product(left, right[0])
        across = split(edge[:, far] - product(left, right[1]))
        inverse = split(spd_inverse(inner))
        solved = split(product(inverse, coupled))
        out[...] = merged - product(across, solved)


def halves(shape):
    return lax.broadcasted_iota(jnp.int32, shape, 1) < FACE


def turn(tile):
    return pltpu.roll(tile, FACE, 1)


def leaf_rows(place, mine, theirs):
    across, third, lead = place[0], place[1], place[2]
    is_alpha = lead == 0
    left = halves((FACE, 128))

    def load(alpha, block, tile):
        spot = pl.ds(pl.multiple_of(block * FACE, FACE), FACE)
        span = slice(128 * tile, 128 * tile + 128)
        own = is_alpha if alpha else jnp.logical_not(is_alpha)
        return jnp.where(own, mine[spot, span], theirs[spot, span])

    def alpha_rows(block):
        sides = load(True, block, 0)
        ends = load(True, block, 1)
        sides = jnp.where(across == 0, turn(sides), sides)
        tiles = (
            jnp.where(left, sides, 0.0),
            jnp.where(left, jnp.where(third == 0, 0.0, ends), sides),
            jnp.where(left & (third == 0), ends, 0.0),
        )
        return jnp.concatenate(tiles, axis=1), turn(ends)

    def beta_rows(block):
        sides = load(False, block, 0)
        ends = load(False, block, 1)
        other = turn(sides)
        near_far = jnp.where(across == 0, other, sides)
        far_near = jnp.where(across == 0, sides, other)
        flipped = turn(ends)
        tiles = (
            jnp.where(left, 0.0, far_near),
            jnp.where(left & (third == 0), flipped, 0.0),
            jnp.where(
                third == 0,
                jnp.where(left, 0.0, near_far),
                jnp.where(left, far_near, ends),
            ),
        )
        return jnp.concatenate(tiles, axis=1), ends

    return alpha_rows, beta_rows


def either(flag, one, other):
    return [jnp.where(flag, x, y) for x, y in zip(one, other)]


def packed(system):
    low = jnp.where(halves((32, 128)), turn(system[64:96]), system[96:128])
    return jnp.concatenate([system[0:64], low], axis=0)


def unpacked(parts):
    top, low = parts[0:64], parts[64:96]
    across = jnp.transpose(jnp.concatenate([top, top], axis=0))[64:128]
    corner = jnp.concatenate([turn(low), low], axis=0)
    return jnp.concatenate([top, jnp.where(halves((64, 128)), across, corner)], axis=0)


def stacked(one, two, start, stop):
    cut = one.shape[0]
    parts = []
    if start < cut:
        parts.append(one[start : min(stop, cut), :])
    if stop > cut:
        parts.append(two[max(start, cut) - cut : stop - cut, :])
    return jnp.concatenate(parts, axis=0)


def stack(one, two, start, value):
    cut = one.shape[0]
    stop = start + value.shape[0]
    if start < cut:
        one[start : min(stop, cut), :] = value[: cut - start]
    if stop > cut:
        two[max(start, cut) - cut : stop - cut, :] = value[max(cut - start, 0) :]


def first_kernel(place, mine, theirs, message_one, message_two, link, solved_high, solved_low):
    alpha_rows, beta_rows = leaf_rows(place, mine, theirs)
    near = jnp.where(place[0] == 0, 1, 0)
    tiles_a, meet_a = alpha_rows(3)
    tiles_b, meet_b = beta_rows(2)
    system = (meet_a + meet_b)[:, :FACE]
    right = split(tiles_a + tiles_b)
    parts = [alpha_rows(near), beta_rows(near), either(place[1] == 0, beta_rows(3), alpha_rows(2))]
    direct = jnp.concatenate([tiles for tiles, _ in parts], axis=0)
    coupling = split(jnp.concatenate([meet for _, meet in parts], axis=0)[:, :FACE])
    inverse = split(spd_inverse(system, panel=8))
    solved = split(product(inverse, right))
    merged = direct - product(coupling, solved)
    stack(message_one, message_two, 0, packed(merged[0:128, 0:128]))
    stack(message_one, message_two, 96, merged[0:128, 128:256])
    stack(message_one, message_two, 224, merged[0:128, 256:384])
    stack(message_one, message_two, 352, merged[128:192, 128:256])
    stack(message_one, message_two, 416, merged[128:192, 256:384])
    link[...] = merged[128:192, 0:128]
    solved_high[...], solved_low[...] = solved


def rows_kernel(place, mine, theirs, solved_high, solved_low, outer, direct, coupling):
    alpha_rows, beta_rows = leaf_rows(place, mine, theirs)
    third, lead = place[1], place[2]
    far = jnp.where(place[0] == 0, 0, 1)
    direct[0:64, :], coupling[0:64, :] = alpha_rows(far)
    at_two = alpha_rows(2)
    at_far = beta_rows(far)
    at_three = beta_rows(3)
    direct[64:128, :], coupling[64:128, :] = either(third == 0, at_two, at_far)
    direct[128:192, :], coupling[128:192, :] = either(third == 0, at_far, at_three)
    spot = pl.ds(pl.multiple_of(lead * 96, 32), 96)
    solved = solved_high[...], solved_low[...]
    outer[...] = direct[spot, :] - product(split(coupling[spot, :][:, :FACE]), solved)


def second_kernel(own, received, outer, inverse_high, inverse_low, outer_high, outer_low):
    outer_high[...], outer_low[...] = split(outer[:, 0:128])
    system = unpacked(own[0:96, :] + received[0:96, :])
    inverse_high[...], inverse_low[...] = split(spd_inverse(system))


def assemble(alpha, beta):
    rows = (alpha or beta)[0].shape[0]
    left = halves((rows, 128))
    blank = jnp.zeros((rows, 128), F32)
    if alpha is None:
        tiles = (
            jnp.where(left, 0.0, turn(beta[0])),
            blank,
            jnp.where(left, 0.0, beta[0]),
            beta[1],
        )
        return jnp.concatenate(tiles, axis=1)
    turned = turn(alpha[1])
    middle = jnp.where(left, turn(alpha[0]), turned)
    if beta is None:
        tiles = jnp.where(left, alpha[0], 0.0), middle, jnp.where(left, turned, 0.0), blank
        return jnp.concatenate(tiles, axis=1)
    tiles = (
        jnp.where(left, alpha[0], turn(beta[0])),
        middle,
        jnp.where(left, turned, beta[0]),
        beta[1],
    )
    return jnp.concatenate(tiles, axis=1)


def exchange_kernel(
    place,
    own_one,
    own_two,
    received_one,
    received_two,
    link,
    inverse_high,
    inverse_low,
    message_one,
    message_two,
    right_high,
    right_low,
):
    is_alpha = place[0] == 0

    def both(mine, other):
        return jnp.where(is_alpha, mine, other), jnp.where(is_alpha, other, mine)

    def part(start, stop):
        return both(stacked(own_one, own_two, start, stop), stacked(received_one, received_two, start, stop))

    one, two = part(96, 224), part(224, 352)
    right = split(assemble((one[0], two[0]), (one[1], two[1])))
    face, back = part(352, 416), part(416, 480)
    direct = jnp.concatenate(
        [assemble((face[0], back[0]), None), assemble(None, (face[1], back[1]))], axis=0
    )
    mine = link[...]
    other = jnp.transpose(stacked(received_one, received_two, 96, 224))[0:FACE]
    coupling = jnp.concatenate(
        [jnp.where(is_alpha, mine, other), jnp.where(is_alpha, other, mine)], axis=0
    )
    solved = split(product(split(coupling), (inverse_high[...], inverse_low[...])))
    merged = direct - product(solved, right)
    stack(message_one, message_two, 0, packed(merged[:, 0:128]))
    for i in range(3):
        stack(message_one, message_two, 96 + 128 * i, merged[:, 128 * i + 128 : 128 * i + 256])
    right_high[...], right_low[...] = right


def rest_columns(one, two):
    return jnp.concatenate(
        [stacked(one, two, 128 * i + 96, 128 * i + 224) for i in range(3)], axis=1
    )


def outer_kernel(place, outer, outer_high, outer_low, inverse_high, inverse_low, right_high, right_low, rows):
    mine = outer[:, 128:256], outer[:, 256:384]
    direct = jnp.where(place[0] == 0, assemble(mine, None), assemble(None, mine))
    solved = split(product((outer_high[...], outer_low[...]), (inverse_high[...], inverse_low[...])))
    rows[...] = direct - product(solved, (right_high[...], right_low[...]))


def third_kernel(own_one, own_two, received, rows, half, solved_high, solved_low):
    right = split(rest_columns(own_one, own_two))
    system = unpacked(own_one[0:96, :] + received[0:96, :])
    solved = split(spd_inverse(system, rows[:, 0:128]))
    half[...] = rows[:, 128:512] + product(solved, right)
    solved_high[...], solved_low[...] = solved


def last_kernel(
    place, half, received_one, received_two, solved_high, solved_low, out, other, sems
):
    third = place[1]
    width = 6 * FACE

    def copy(source, side, start, i):
        first = pl.multiple_of(side * width + start, 128)
        target = out.at[:, pl.ds(first, source.shape[1])]
        return pltpu.make_async_copy(source, target, sems.at[i])

    copies = [copy(half, third, 0, 0)]
    copies[0].start()
    solved = solved_high[...], solved_low[...]
    for i in range(3):
        right = split(stacked(received_one, received_two, 128 * i + 96, 128 * i + 224))
        other[i] = product(solved, right)
        copies.append(copy(other.at[i], 1 - third, 128 * i, i + 1))
        copies[-1].start()
    for x in copies:
        x.wait()


def shapes(*sizes):
    return [jax.ShapeDtypeStruct(size, F32) for size in sizes]


def pair(*size):
    return [jax.ShapeDtypeStruct(size, BF16)] * 2


def run(kernel, out_shape, *operands, scalars=1, out_space=pltpu.VMEM, **options):
    smem = pl.BlockSpec(memory_space=pltpu.SMEM)
    vmem = pl.BlockSpec(memory_space=pltpu.VMEM)
    return pl.pallas_call(
        kernel,
        out_shape=out_shape,
        in_specs=[smem] * scalars + [vmem] * (len(operands) - scalars),
        out_specs=[pl.BlockSpec(memory_space=out_space)] * len(out_shape),
        compiler_params=pltpu.CompilerParams(vmem_limit_bytes=32 * 1024 * 1024),
        **options,
    )(*operands)


def body(leaf_maps, leaf_operator, region_eps, wave_sq, region_labels, build_flags):
    across = lax.axis_index("bx") % 2
    upward = lax.axis_index("by")
    place = jnp.stack([across, upward // 2 % 2, upward % 2]).astype(jnp.int32)
    size = leaf_operator.shape[0]
    mine = pl.pallas_call(
        build_kernel,
        out_shape=jax.ShapeDtypeStruct((LEAF, LEAF), F32),
        in_specs=[pl.BlockSpec(memory_space=pltpu.SMEM)] * 3
        + [pl.BlockSpec(memory_space=pltpu.HBM)] * 3,
        out_specs=pl.BlockSpec(memory_space=pltpu.VMEM),
        scratch_shapes=[
            pltpu.VMEM(region_eps.shape, F32),
            pltpu.VMEM((128, size), F32),
            pltpu.VMEM((size - LEAF - 128, size), F32),
            pltpu.VMEM((LEAF, size), F32),
            pltpu.SemaphoreType.DMA((5,)),
        ],
        compiler_params=pltpu.CompilerParams(vmem_limit_bytes=32 * 1024 * 1024),
        name="leaf_build",
    )(
        region_labels,
        build_flags,
        wave_sq,
        *(
            pltpu.with_memory_space_constraint(x, pltpu.HBM)
            for x in (leaf_maps[0, 0], leaf_operator, region_eps)
        ),
    )
    theirs = swapped(mine, "by", 0)
    one, two, link, *solved = run(
        first_kernel,
        shapes((CUT_TWO, 128), (MESSAGE - CUT_TWO, 128), (FACE, 128)) + pair(FACE, 6 * FACE),
        place,
        mine,
        theirs,
        name="first_merge",
    )
    received_one = swapped(one, "bx", 0)
    received_two = swapped(two, "bx", 0)
    (outer,) = run(
        rows_kernel,
        shapes((96, 6 * FACE)),
        place,
        mine,
        theirs,
        *solved,
        scratch_shapes=[pltpu.VMEM((192, 6 * FACE), F32), pltpu.VMEM((192, 128), F32)],
        name="first_rows",
    )
    *inverse, outer_high, outer_low = run(
        second_kernel,
        pair(128, 128) + pair(96, 128),
        one,
        received_one,
        outer,
        scalars=0,
        cost_estimate=LONG,
        name="second_inverse",
    )
    one, two, *right = run(
        exchange_kernel,
        shapes((CUT_THREE, 128), (MESSAGE - CUT_THREE, 128)) + pair(128, 8 * FACE),
        place,
        one,
        two,
        received_one,
        received_two,
        link,
        *inverse,
        name="second_merge",
    )
    received_one = swapped(one, "by", 1)
    received_two = swapped(two, "by", 1)
    (rows,) = run(
        outer_kernel,
        shapes((96, 8 * FACE)),
        place,
        outer,
        outer_high,
        outer_low,
        *inverse,
        *right,
        name="second_rows",
    )
    half, *solved = run(
        third_kernel,
        shapes((96, 6 * FACE)) + pair(96, 128),
        one,
        two,
        received_one,
        rows,
        scalars=0,
        cost_estimate=LONG,
        name="third_inverse",
    )
    (result,) = run(
        last_kernel,
        shapes((96, 12 * FACE)),
        place,
        half,
        received_one,
        received_two,
        *solved,
        scratch_shapes=[pltpu.VMEM((3, 96, 128), F32), pltpu.SemaphoreType.DMA((4,))],
        out_space=pltpu.HBM,
        name="third_merge",
    )
    return result.reshape((1, 1, 96, 12 * FACE))


def solution(mesh):
    placed = (
        P(("freq", "bx"), "by", None, None),
        P(),
        P(),
        P("freq"),
        P("bx", "by"),
        P("bx", "by"),
    )
    return jax.shard_map(
        body,
        mesh=mesh,
        in_specs=placed,
        out_specs=P(("freq", "bx"), "by", None, None),
        check_vma=False,
    )
```

```python
import jax
import jax.numpy as jnp
from jax import lax
from jax.experimental import pallas as pl
from jax.experimental.pallas import tpu as pltpu
from jax.sharding import PartitionSpec as P

FACE = 64
LEAF = 4 * FACE
MESSAGE = 96 + 3 * 128
CUT_TWO, CUT_THREE = 200, 160
F32 = jnp.float32
BF16 = jnp.bfloat16


LONG = pl.CostEstimate(flops=10**10, bytes_accessed=10**8, transcendentals=10**6)


def swapped(shard, axis, stride):
    return lax.ppermute(shard, axis, [(i, i ^ 1 << stride) for i in range(lax.axis_size(axis))])


def split(x):
    high = x.astype(BF16)
    return high, (x - high.astype(F32)).astype(BF16)


def thirds(x):
    high = x.astype(BF16).astype(F32)
    rest = x - high
    middle = rest.astype(BF16).astype(F32)
    return high, middle, (rest - middle).astype(BF16).astype(F32)


def dot(a, b):
    return jnp.dot(a, b, preferred_element_type=F32)


def product(a, b):
    (a_high, a_low), (b_high, b_low) = a, b
    depth = a_high.shape[1]
    if depth % 128 and depth != FACE:
        return dot(a_high, b_high) + (dot(a_high, b_low) + dot(a_low, b_high))
    twice = dot(
        jnp.concatenate([a_high, a_low], axis=1), jnp.concatenate([b_high, b_high], axis=0)
    )
    return twice + dot(a_high, b_low)


def tree(terms):
    while len(terms) > 1:
        terms = [x + y for x, y in zip(terms[::2], terms[1::2])]
    return terms[0]


def minus(value, terms):
    for term in terms:
        value = value - term
    return value


def spd_inverse(matrix, left=None, both=False, panel=4, look=4, half=4):
    size = matrix.shape[0]
    shape = (8, size)
    count = size // 8
    tiles = [matrix[8 * g : 8 * g + 8] for g in range(count)]
    lane = lax.broadcasted_iota(jnp.int32, shape, 1)
    sub = lax.broadcasted_iota(jnp.int32, shape, 0)

    def column(tile, c):
        return jnp.broadcast_to(tile[:, c : c + 1], shape)

    def row(tile, r):
        return jnp.broadcast_to(tile[r : r + 1, :], shape)

    def inside(start, stop):
        return (lane >= start) & (lane < stop)

    pivot = [column(tiles[0], j) for j in range(8)]
    head = row(pivot[0], 0)
    for start in range(0, count, panel):
        stop = min(start + panel, count)
        last = min(stop + look, count)
        outside = [*range(last, count), *range(start if left is None or both else 0)]
        if outside:
            strip = jnp.concatenate([tiles[g] for g in outside], axis=0)[:, 8 * start : 8 * stop]
            high, middle, low = thirds(strip)
            factors = jnp.concatenate([high, high, middle, high, low, middle], axis=1).astype(BF16)
        for k in range(start, stop):
            first = 8 * k
            block = inside(first, first + 8)
            rows = jnp.where(block, (lane - first == sub).astype(F32), tiles[k])
            ahead = k + 1 < count
            if ahead:
                after = jnp.where(block, 0.0, tiles[k + 1])
                side = [column(tiles[k + 1], first + j) for j in range(8)]
            scale = None
            for p in range(8):
                inverse = pl.reciprocal(head, approx=True)
                if p < 7:
                    element = row(pivot[p + 1], p)
                    head = row(pivot[p + 1], p + 1) - element * (element * inverse)
                factor = jnp.where(sub == p, 0.0, pivot[p]) * inverse
                picked = row(rows, p)
                if ahead:
                    edge = side[p]
                    factor_ahead = edge * inverse
                    if p == half:
                        coming = [column(after, first + 8 + j) for j in range(8)]
                    if p == 7:
                        element = row(edge, 0)
                        head = row(coming[0], 0) - element * (element * inverse)
                    if p >= half:
                        for j in range(8):
                            coming[j] = coming[j] - factor_ahead * row(edge, j)
                    after = after - factor_ahead * picked
                for j in range(p + 1, 8):
                    element = row(pivot[j], p)
                    pivot[j] = pivot[j] - factor * element
                    if ahead:
                        side[j] = side[j] - factor_ahead * element
                rows = rows - factor * picked
                scale = inverse if scale is None else jnp.where(sub == p, inverse, scale)
            rows = rows * scale
            picked = [row(rows, j) for j in range(8)]
            for g in range(start, last):
                if g == k:
                    tiles[g] = rows
                elif g == k + 1:
                    tiles[g] = after
                else:
                    terms = [column(tiles[g], first + j) * picked[j] for j in range(8)]
                    cleared = jnp.where(block, 0.0, tiles[g])
                    tiles[g] = cleared - tree(terms) if count <= panel else minus(cleared, terms)
            if ahead:
                pivot = coming
        solved = jnp.concatenate(tiles[start:stop], axis=0)
        if outside:
            high, middle, low = thirds(solved)
            right = jnp.concatenate([high, middle, high, low, high, middle], axis=0).astype(BF16)
            update = dot(factors, right)
            block = inside(8 * start, 8 * stop)
            for i, g in enumerate(outside):
                tiles[g] = jnp.where(block, 0.0, tiles[g]) - update[8 * i : 8 * i + 8]
        if left is not None:
            blanks = [jnp.zeros((rows, size), BF16) for rows in (8 * start, size - 8 * stop)]
            right = [
                jnp.concatenate([x for x in (blanks[0], part, blanks[1]) if x.shape[0]], axis=0)
                for part in split(solved)
            ]
            columns = lax.broadcasted_iota(jnp.int32, left.shape, 1)
            block = (columns >= 8 * start) & (columns < 8 * stop)
            left = jnp.where(block, 0.0, left) - product(split(left), right)
    if left is not None and not both:
        return left
    whole = jnp.concatenate(tiles, axis=0)
    return (whole, left) if both else whole


def build_kernel(label, flag, wave, given, operator, table_at, out, table, one, two, edge, sems):
    size = operator.shape[0]
    middle = LEAF + 128
    copies = [
        pltpu.make_async_copy(source, target, sems.at[i])
        for i, (source, target) in enumerate(
            (
                (operator.at[pl.ds(LEAF, 128)], one),
                (table_at, table),
                (operator.at[pl.ds(middle, size - middle)], two),
                (operator.at[pl.ds(0, LEAF)], edge),
                (given, out),
            )
        )
    ]
    flagged = flag[0, 0] > 0

    @pl.when(jnp.logical_not(flagged))
    def _():
        copies[4].start()
        copies[4].wait()

    @pl.when(flagged)
    def _():
        for copy in copies[:4]:
            copy.start()
        for copy in copies[:2]:
            copy.wait()
        shift = wave[0] * table[pl.ds(label[0, 0], 1), :]
        border, near, far = slice(0, LEAF), slice(LEAF, middle), slice(middle, size)

        def shifted(ref, span):
            block = ref[:, span]
            ids = lax.broadcasted_iota(jnp.int32, block.shape, 0)
            diagonal = ids == lax.broadcasted_iota(jnp.int32, block.shape, 1)
            return block - jnp.where(diagonal, shift[:, span], 0.0)

        right = split(one[:, border]), split(one[:, far])
        copies[2].wait()
        inverse, left = spd_inverse(shifted(one, near), two[:, near], both=True)
        copies[3].wait()
        left = split(left)
        inner = shifted(two, far) + product(left, right[1])
        coupled = split(two[:, border] + product(left, right[0]))
        left = split(edge[:, near])
        left = split(product(left, split(inverse)))
        merged = shifted(edge, border) - product(left, right[0])
        across = split(edge[:, far] - product(left, right[1]))
        inverse = split(spd_inverse(inner))
        solved = split(product(inverse, coupled))
        out[...] = merged - product(across, solved)


def halves(shape):
    return lax.broadcasted_iota(jnp.int32, shape, 1) < FACE


def turn(tile):
    return pltpu.roll(tile, FACE, 1)


def leaf_rows(place, mine, theirs):
    across, third, lead = place[0], place[1], place[2]
    is_alpha = lead == 0
    left = halves((FACE, 128))

    def load(alpha, block, tile):
        spot = pl.ds(pl.multiple_of(block * FACE, FACE), FACE)
        span = slice(128 * tile, 128 * tile + 128)
        own = is_alpha if alpha else jnp.logical_not(is_alpha)
        return jnp.where(own, mine[spot, span], theirs[spot, span])

    def alpha_rows(block):
        sides = load(True, block, 0)
        ends = load(True, block, 1)
        sides = jnp.where(across == 0, turn(sides), sides)
        tiles = (
            jnp.where(left, sides, 0.0),
            jnp.where(left, jnp.where(third == 0, 0.0, ends), sides),
            jnp.where(left & (third == 0), ends, 0.0),
        )
        return jnp.concatenate(tiles, axis=1), turn(ends)

    def beta_rows(block):
        sides = load(False, block, 0)
        ends = load(False, block, 1)
        other = turn(sides)
        near_far = jnp.where(across == 0, other, sides)
        far_near = jnp.where(across == 0, sides, other)
        flipped = turn(ends)
        tiles = (
            jnp.where(left, 0.0, far_near),
            jnp.where(left & (third == 0), flipped, 0.0),
            jnp.where(
                third == 0,
                jnp.where(left, 0.0, near_far),
                jnp.where(left, far_near, ends),
            ),
        )
        return jnp.concatenate(tiles, axis=1), ends

    return alpha_rows, beta_rows


def either(flag, one, other):
    return [jnp.where(flag, x, y) for x, y in zip(one, other)]


def packed(system):
    low = jnp.where(halves((32, 128)), turn(system[64:96]), system[96:128])
    return jnp.concatenate([system[0:64], low], axis=0)


def unpacked(parts):
    top, low = parts[0:64], parts[64:96]
    across = jnp.transpose(jnp.concatenate([top, top], axis=0))[64:128]
    corner = jnp.concatenate([turn(low), low], axis=0)
    return jnp.concatenate([top, jnp.where(halves((64, 128)), across, corner)], axis=0)


def stacked(one, two, start, stop):
    cut = one.shape[0]
    parts = []
    if start < cut:
        parts.append(one[start : min(stop, cut), :])
    if stop > cut:
        parts.append(two[max(start, cut) - cut : stop - cut, :])
    return jnp.concatenate(parts, axis=0)


def stack(one, two, start, value):
    cut = one.shape[0]
    stop = start + value.shape[0]
    if start < cut:
        one[start : min(stop, cut), :] = value[: cut - start]
    if stop > cut:
        two[max(start, cut) - cut : stop - cut, :] = value[max(cut - start, 0) :]


def first_kernel(place, mine, theirs, message_one, message_two, link, solved_high, solved_low):
    alpha_rows, beta_rows = leaf_rows(place, mine, theirs)
    near = jnp.where(place[0] == 0, 1, 0)
    tiles_a, meet_a = alpha_rows(3)
    tiles_b, meet_b = beta_rows(2)
    system = (meet_a + meet_b)[:, :FACE]
    right = split(tiles_a + tiles_b)
    parts = [alpha_rows(near), beta_rows(near), either(place[1] == 0, beta_rows(3), alpha_rows(2))]
    direct = jnp.concatenate([tiles for tiles, _ in parts], axis=0)
    coupling = split(jnp.concatenate([meet for _, meet in parts], axis=0)[:, :FACE])
    inverse = split(spd_inverse(system, panel=8))
    solved = split(product(inverse, right))
    merged = direct - product(coupling, solved)
    stack(message_one, message_two, 0, packed(merged[0:128, 0:128]))
    stack(message_one, message_two, 96, merged[0:128, 128:256])
    stack(message_one, message_two, 224, merged[0:128, 256:384])
    stack(message_one, message_two, 352, merged[128:192, 128:256])
    stack(message_one, message_two, 416, merged[128:192, 256:384])
    link[...] = merged[128:192, 0:128]
    solved_high[...], solved_low[...] = solved


def rows_kernel(place, mine, theirs, solved_high, solved_low, outer, direct, coupling):
    alpha_rows, beta_rows = leaf_rows(place, mine, theirs)
    third, lead = place[1], place[2]
    far = jnp.where(place[0] == 0, 0, 1)
    direct[0:64, :], coupling[0:64, :] = alpha_rows(far)
    at_two = alpha_rows(2)
    at_far = beta_rows(far)
    at_three = beta_rows(3)
    direct[64:128, :], coupling[64:128, :] = either(third == 0, at_two, at_far)
    direct[128:192, :], coupling[128:192, :] = either(third == 0, at_far, at_three)
    spot = pl.ds(pl.multiple_of(lead * 96, 32), 96)
    solved = solved_high[...], solved_low[...]
    outer[...] = direct[spot, :] - product(split(coupling[spot, :][:, :FACE]), solved)


def second_kernel(own, received, outer, inverse_high, inverse_low, outer_high, outer_low):
    outer_high[...], outer_low[...] = split(outer[:, 0:128])
    system = unpacked(own[0:96, :] + received[0:96, :])
    inverse_high[...], inverse_low[...] = split(spd_inverse(system))


def assemble(alpha, beta):
    rows = (alpha or beta)[0].shape[0]
    left = halves((rows, 128))
    blank = jnp.zeros((rows, 128), F32)
    if alpha is None:
        tiles = (
            jnp.where(left, 0.0, turn(beta[0])),
            blank,
            jnp.where(left, 0.0, beta[0]),
            beta[1],
        )
        return jnp.concatenate(tiles, axis=1)
    turned = turn(alpha[1])
    middle = jnp.where(left, turn(alpha[0]), turned)
    if beta is None:
        tiles = jnp.where(left, alpha[0], 0.0), middle, jnp.where(left, turned, 0.0), blank
        return jnp.concatenate(tiles, axis=1)
    tiles = (
        jnp.where(left, alpha[0], turn(beta[0])),
        middle,
        jnp.where(left, turned, beta[0]),
        beta[1],
    )
    return jnp.concatenate(tiles, axis=1)


def exchange_kernel(
    place,
    own_one,
    own_two,
    received_one,
    received_two,
    link,
    inverse_high,
    inverse_low,
    message_one,
    message_two,
    right_high,
    right_low,
):
    is_alpha = place[0] == 0

    def both(mine, other):
        return jnp.where(is_alpha, mine, other), jnp.where(is_alpha, other, mine)

    def part(start, stop):
        return both(stacked(own_one, own_two, start, stop), stacked(received_one, received_two, start, stop))

    one, two = part(96, 224), part(224, 352)
    right = split(assemble((one[0], two[0]), (one[1], two[1])))
    face, back = part(352, 416), part(416, 480)
    direct = jnp.concatenate(
        [assemble((face[0], back[0]), None), assemble(None, (face[1], back[1]))], axis=0
    )
    mine = link[...]
    other = jnp.transpose(stacked(received_one, received_two, 96, 224))[0:FACE]
    coupling = jnp.concatenate(
        [jnp.where(is_alpha, mine, other), jnp.where(is_alpha, other, mine)], axis=0
    )
    solved = split(product(split(coupling), (inverse_high[...], inverse_low[...])))
    merged = direct - product(solved, right)
    stack(message_one, message_two, 0, packed(merged[:, 0:128]))
    for i in range(3):
        stack(message_one, message_two, 96 + 128 * i, merged[:, 128 * i + 128 : 128 * i + 256])
    right_high[...], right_low[...] = right


def rest_columns(one, two):
    return jnp.concatenate(
        [stacked(one, two, 128 * i + 96, 128 * i + 224) for i in range(3)], axis=1
    )


def outer_kernel(place, outer, outer_high, outer_low, inverse_high, inverse_low, right_high, right_low, rows):
    mine = outer[:, 128:256], outer[:, 256:384]
    direct = jnp.where(place[0] == 0, assemble(mine, None), assemble(None, mine))
    solved = split(product((outer_high[...], outer_low[...]), (inverse_high[...], inverse_low[...])))
    rows[...] = direct - product(solved, (right_high[...], right_low[...]))


def third_kernel(own_one, own_two, received, rows, half, solved_high, solved_low):
    right = split(rest_columns(own_one, own_two))
    system = unpacked(own_one[0:96, :] + received[0:96, :])
    solved = split(spd_inverse(system, rows[:, 0:128]))
    half[...] = rows[:, 128:512] + product(solved, right)
    solved_high[...], solved_low[...] = solved


def last_kernel(
    place, half, received_one, received_two, solved_high, solved_low, out, other, sems
):
    third = place[1]
    width = 6 * FACE

    def copy(source, side, start, i):
        first = pl.multiple_of(side * width + start, 128)
        target = out.at[:, pl.ds(first, source.shape[1])]
        return pltpu.make_async_copy(source, target, sems.at[i])

    copies = [copy(half, third, 0, 0)]
    copies[0].start()
    solved = solved_high[...], solved_low[...]
    for i in range(3):
        right = split(stacked(received_one, received_two, 128 * i + 96, 128 * i + 224))
        other[i] = product(solved, right)
        copies.append(copy(other.at[i], 1 - third, 128 * i, i + 1))
        copies[-1].start()
    for x in copies:
        x.wait()


def shapes(*sizes):
    return [jax.ShapeDtypeStruct(size, F32) for size in sizes]


def pair(*size):
    return [jax.ShapeDtypeStruct(size, BF16)] * 2


def run(kernel, out_shape, *operands, scalars=1, out_space=pltpu.VMEM, **options):
    smem = pl.BlockSpec(memory_space=pltpu.SMEM)
    vmem = pl.BlockSpec(memory_space=pltpu.VMEM)
    return pl.pallas_call(
        kernel,
        out_shape=out_shape,
        in_specs=[smem] * scalars + [vmem] * (len(operands) - scalars),
        out_specs=[pl.BlockSpec(memory_space=out_space)] * len(out_shape),
        compiler_params=pltpu.CompilerParams(vmem_limit_bytes=32 * 1024 * 1024),
        **options,
    )(*operands)


def body(leaf_maps, leaf_operator, region_eps, wave_sq, region_labels, build_flags):
    across = lax.axis_index("bx") % 2
    upward = lax.axis_index("by")
    place = jnp.stack([across, upward // 2 % 2, upward % 2]).astype(jnp.int32)
    size = leaf_operator.shape[0]
    mine = pl.pallas_call(
        build_kernel,
        out_shape=jax.ShapeDtypeStruct((LEAF, LEAF), F32),
        in_specs=[pl.BlockSpec(memory_space=pltpu.SMEM)] * 3
        + [pl.BlockSpec(memory_space=pltpu.HBM)] * 3,
        out_specs=pl.BlockSpec(memory_space=pltpu.VMEM),
        scratch_shapes=[
            pltpu.VMEM(region_eps.shape, F32),
            pltpu.VMEM((128, size), F32),
            pltpu.VMEM((size - LEAF - 128, size), F32),
            pltpu.VMEM((LEAF, size), F32),
            pltpu.SemaphoreType.DMA((5,)),
        ],
        compiler_params=pltpu.CompilerParams(vmem_limit_bytes=32 * 1024 * 1024),
        name="leaf_build",
    )(
        region_labels,
        build_flags,
        wave_sq,
        *(
            pltpu.with_memory_space_constraint(x, pltpu.HBM)
            for x in (leaf_maps[0, 0], leaf_operator, region_eps)
        ),
    )
    theirs = swapped(mine, "by", 0)
    one, two, link, *solved = run(
        first_kernel,
        shapes((CUT_TWO, 128), (MESSAGE - CUT_TWO, 128), (FACE, 128)) + pair(FACE, 6 * FACE),
        place,
        mine,
        theirs,
        name="first_merge",
    )
    received_one = swapped(one, "bx", 0)
    received_two = swapped(two, "bx", 0)
    (outer,) = run(
        rows_kernel,
        shapes((96, 6 * FACE)),
        place,
        mine,
        theirs,
        *solved,
        scratch_shapes=[pltpu.VMEM((192, 6 * FACE), F32), pltpu.VMEM((192, 128), F32)],
        name="first_rows",
    )
    *inverse, outer_high, outer_low = run(
        second_kernel,
        pair(128, 128) + pair(96, 128),
        one,
        received_one,
        outer,
        scalars=0,
        cost_estimate=LONG,
        name="second_inverse",
    )
    one, two, *right = run(
        exchange_kernel,
        shapes((CUT_THREE, 128), (MESSAGE - CUT_THREE, 128)) + pair(128, 8 * FACE),
        place,
        one,
        two,
        received_one,
        received_two,
        link,
        *inverse,
        name="second_merge",
    )
    received_one = swapped(one, "by", 1)
    received_two = swapped(two, "by", 1)
    (rows,) = run(
        outer_kernel,
        shapes((96, 8 * FACE)),
        place,
        outer,
        outer_high,
        outer_low,
        *inverse,
        *right,
        name="second_rows",
    )
    half, *solved = run(
        third_kernel,
        shapes((96, 6 * FACE)) + pair(96, 128),
        one,
        two,
        received_one,
        rows,
        scalars=0,
        cost_estimate=LONG,
        name="third_inverse",
    )
    (result,) = run(
        last_kernel,
        shapes((96, 12 * FACE)),
        place,
        half,
        received_one,
        received_two,
        *solved,
        scratch_shapes=[pltpu.VMEM((3, 96, 128), F32), pltpu.SemaphoreType.DMA((4,))],
        out_space=pltpu.HBM,
        name="third_merge",
    )
    return result.reshape((1, 1, 96, 12 * FACE))


def solution(mesh):
    placed = (
        P(("freq", "bx"), "by", None, None),
        P(),
        P(),
        P("freq"),
        P("bx", "by"),
        P("bx", "by"),
    )
    return jax.shard_map(
        body,
        mesh=mesh,
        in_specs=placed,
        out_specs=P(("freq", "bx"), "by", None, None),
        check_vma=False,
    )
```

```python
import jax
import jax.numpy as jnp
from jax import lax
from jax.experimental import pallas as pl
from jax.experimental.pallas import tpu as pltpu
from jax.sharding import PartitionSpec as P

FACE = 64
LEAF = 4 * FACE
MESSAGE = 96 + 3 * 128
CUT_TWO, CUT_THREE = 200, 160
F32 = jnp.float32
BF16 = jnp.bfloat16


LONG = pl.CostEstimate(flops=10**10, bytes_accessed=10**8, transcendentals=10**6)


def swapped(shard, axis, stride):
    return lax.ppermute(shard, axis, [(i, i ^ 1 << stride) for i in range(lax.axis_size(axis))])


def split(x):
    high = x.astype(BF16)
    return high, (x - high.astype(F32)).astype(BF16)


def thirds(x):
    high = x.astype(BF16).astype(F32)
    rest = x - high
    middle = rest.astype(BF16).astype(F32)
    return high, middle, (rest - middle).astype(BF16).astype(F32)


def dot(a, b):
    return jnp.dot(a, b, preferred_element_type=F32)


def product(a, b):
    (a_high, a_low), (b_high, b_low) = a, b
    depth = a_high.shape[1]
    if depth % 128:
        return dot(a_high, b_high) + (dot(a_high, b_low) + dot(a_low, b_high))
    twice = dot(
        jnp.concatenate([a_high, a_low], axis=1), jnp.concatenate([b_high, b_high], axis=0)
    )
    return twice + dot(a_high, b_low)


def tree(terms):
    while len(terms) > 1:
        terms = [x + y for x, y in zip(terms[::2], terms[1::2])]
    return terms[0]


def minus(value, terms):
    for term in terms:
        value = value - term
    return value


def spd_inverse(matrix, left=None, both=False, panel=4, look=4, half=4):
    size = matrix.shape[0]
    shape = (8, size)
    count = size // 8
    tiles = [matrix[8 * g : 8 * g + 8] for g in range(count)]
    lane = lax.broadcasted_iota(jnp.int32, shape, 1)
    sub = lax.broadcasted_iota(jnp.int32, shape, 0)

    def column(tile, c):
        return jnp.broadcast_to(tile[:, c : c + 1], shape)

    def row(tile, r):
        return jnp.broadcast_to(tile[r : r + 1, :], shape)

    def inside(start, stop):
        return (lane >= start) & (lane < stop)

    pivot = [column(tiles[0], j) for j in range(8)]
    head = row(pivot[0], 0)
    for start in range(0, count, panel):
        stop = min(start + panel, count)
        last = min(stop + look, count)
        outside = [*range(last, count), *range(start if left is None or both else 0)]
        if outside:
            strip = jnp.concatenate([tiles[g] for g in outside], axis=0)[:, 8 * start : 8 * stop]
            high, middle, low = thirds(strip)
            factors = jnp.concatenate([high, high, middle, high, low, middle], axis=1).astype(BF16)
        for k in range(start, stop):
            first = 8 * k
            block = inside(first, first + 8)
            rows = jnp.where(block, (lane - first == sub).astype(F32), tiles[k])
            ahead = k + 1 < count
            if ahead:
                after = jnp.where(block, 0.0, tiles[k + 1])
                side = [column(tiles[k + 1], first + j) for j in range(8)]
            scale = None
            for p in range(8):
                inverse = pl.reciprocal(head, approx=True)
                if p < 7:
                    element = row(pivot[p + 1], p)
                    head = row(pivot[p + 1], p + 1) - element * (element * inverse)
                factor = jnp.where(sub == p, 0.0, pivot[p]) * inverse
                picked = row(rows, p)
                if ahead:
                    edge = side[p]
                    factor_ahead = edge * inverse
                    if p == half:
                        coming = [column(after, first + 8 + j) for j in range(8)]
                    if p == 7:
                        element = row(edge, 0)
                        head = row(coming[0], 0) - element * (element * inverse)
                    if p >= half:
                        for j in range(8):
                            coming[j] = coming[j] - factor_ahead * row(edge, j)
                    after = after - factor_ahead * picked
                for j in range(p + 1, 8):
                    element = row(pivot[j], p)
                    pivot[j] = pivot[j] - factor * element
                    if ahead:
                        side[j] = side[j] - factor_ahead * element
                rows = rows - factor * picked
                scale = inverse if scale is None else jnp.where(sub == p, inverse, scale)
            rows = rows * scale
            picked = [row(rows, j) for j in range(8)]
            for g in range(start, last):
                if g == k:
                    tiles[g] = rows
                elif g == k + 1:
                    tiles[g] = after
                else:
                    terms = [column(tiles[g], first + j) * picked[j] for j in range(8)]
                    cleared = jnp.where(block, 0.0, tiles[g])
                    tiles[g] = cleared - tree(terms) if count <= panel else minus(cleared, terms)
            if ahead:
                pivot = coming
        solved = jnp.concatenate(tiles[start:stop], axis=0)
        if outside:
            high, middle, low = thirds(solved)
            right = jnp.concatenate([high, middle, high, low, high, middle], axis=0).astype(BF16)
            update = dot(factors, right)
            block = inside(8 * start, 8 * stop)
            for i, g in enumerate(outside):
                tiles[g] = jnp.where(block, 0.0, tiles[g]) - update[8 * i : 8 * i + 8]
        if left is not None:
            blanks = [jnp.zeros((rows, size), BF16) for rows in (8 * start, size - 8 * stop)]
            right = [
                jnp.concatenate([x for x in (blanks[0], part, blanks[1]) if x.shape[0]], axis=0)
                for part in split(solved)
            ]
            columns = lax.broadcasted_iota(jnp.int32, left.shape, 1)
            block = (columns >= 8 * start) & (columns < 8 * stop)
            left = jnp.where(block, 0.0, left) - product(split(left), right)
    if left is not None and not both:
        return left
    whole = jnp.concatenate(tiles, axis=0)
    return (whole, left) if both else whole


def build_kernel(label, flag, wave, given, operator, table_at, out, table, one, two, edge, sems):
    size = operator.shape[0]
    middle = LEAF + 128
    copies = [
        pltpu.make_async_copy(source, target, sems.at[i])
        for i, (source, target) in enumerate(
            (
                (operator.at[pl.ds(LEAF, 128)], one),
                (table_at, table),
                (operator.at[pl.ds(middle, size - middle)], two),
                (operator.at[pl.ds(0, LEAF)], edge),
                (given, out),
            )
        )
    ]
    flagged = flag[0, 0] > 0

    @pl.when(jnp.logical_not(flagged))
    def _():
        copies[4].start()
        copies[4].wait()

    @pl.when(flagged)
    def _():
        for copy in copies[:4]:
            copy.start()
        for copy in copies[:2]:
            copy.wait()
        shift = wave[0] * table[pl.ds(label[0, 0], 1), :]
        border, near, far = slice(0, LEAF), slice(LEAF, middle), slice(middle, size)

        def shifted(ref, span):
            block = ref[:, span]
            ids = lax.broadcasted_iota(jnp.int32, block.shape, 0)
            diagonal = ids == lax.broadcasted_iota(jnp.int32, block.shape, 1)
            return block - jnp.where(diagonal, shift[:, span], 0.0)

        right = split(one[:, border]), split(one[:, far])
        copies[2].wait()
        inverse, left = spd_inverse(shifted(one, near), two[:, near], both=True)
        copies[3].wait()
        left = split(left)
        inner = shifted(two, far) + product(left, right[1])
        coupled = split(two[:, border] + product(left, right[0]))
        left = split(edge[:, near])
        left = split(product(left, split(inverse)))
        merged = shifted(edge, border) - product(left, right[0])
        across = split(edge[:, far] - product(left, right[1]))
        inverse = split(spd_inverse(inner))
        solved = split(product(inverse, coupled))
        out[...] = merged - product(across, solved)


def halves(shape):
    return lax.broadcasted_iota(jnp.int32, shape, 1) < FACE


def turn(tile):
    return pltpu.roll(tile, FACE, 1)


def leaf_rows(place, mine, theirs):
    across, third, lead = place[0], place[1], place[2]
    is_alpha = lead == 0
    left = halves((FACE, 128))

    def load(alpha, block, tile):
        spot = pl.ds(pl.multiple_of(block * FACE, FACE), FACE)
        span = slice(128 * tile, 128 * tile + 128)
        own = is_alpha if alpha else jnp.logical_not(is_alpha)
        return jnp.where(own, mine[spot, span], theirs[spot, span])

    def alpha_rows(block):
        sides = load(True, block, 0)
        ends = load(True, block, 1)
        sides = jnp.where(across == 0, turn(sides), sides)
        tiles = (
            jnp.where(left, sides, 0.0),
            jnp.where(left, jnp.where(third == 0, 0.0, ends), sides),
            jnp.where(left & (third == 0), ends, 0.0),
        )
        return jnp.concatenate(tiles, axis=1), turn(ends)

    def beta_rows(block):
        sides = load(False, block, 0)
        ends = load(False, block, 1)
        other = turn(sides)
        near_far = jnp.where(across == 0, other, sides)
        far_near = jnp.where(across == 0, sides, other)
        flipped = turn(ends)
        tiles = (
            jnp.where(left, 0.0, far_near),
            jnp.where(left & (third == 0), flipped, 0.0),
            jnp.where(
                third == 0,
                jnp.where(left, 0.0, near_far),
                jnp.where(left, far_near, ends),
            ),
        )
        return jnp.concatenate(tiles, axis=1), ends

    return alpha_rows, beta_rows


def either(flag, one, other):
    return [jnp.where(flag, x, y) for x, y in zip(one, other)]


def packed(system):
    low = jnp.where(halves((32, 128)), turn(system[64:96]), system[96:128])
    return jnp.concatenate([system[0:64], low], axis=0)


def unpacked(parts):
    top, low = parts[0:64], parts[64:96]
    across = jnp.transpose(jnp.concatenate([top, top], axis=0))[64:128]
    corner = jnp.concatenate([turn(low), low], axis=0)
    return jnp.concatenate([top, jnp.where(halves((64, 128)), across, corner)], axis=0)


def stacked(one, two, start, stop):
    cut = one.shape[0]
    parts = []
    if start < cut:
        parts.append(one[start : min(stop, cut), :])
    if stop > cut:
        parts.append(two[max(start, cut) - cut : stop - cut, :])
    return jnp.concatenate(parts, axis=0)


def stack(one, two, start, value):
    cut = one.shape[0]
    stop = start + value.shape[0]
    if start < cut:
        one[start : min(stop, cut), :] = value[: cut - start]
    if stop > cut:
        two[max(start, cut) - cut : stop - cut, :] = value[max(cut - start, 0) :]


def first_kernel(place, mine, theirs, message_one, message_two, link, solved_high, solved_low):
    alpha_rows, beta_rows = leaf_rows(place, mine, theirs)
    near = jnp.where(place[0] == 0, 1, 0)
    tiles_a, meet_a = alpha_rows(3)
    tiles_b, meet_b = beta_rows(2)
    system = (meet_a + meet_b)[:, :FACE]
    right = split(tiles_a + tiles_b)
    parts = [alpha_rows(near), beta_rows(near), either(place[1] == 0, beta_rows(3), alpha_rows(2))]
    direct = jnp.concatenate([tiles for tiles, _ in parts], axis=0)
    coupling = split(jnp.concatenate([meet for _, meet in parts], axis=0)[:, :FACE])
    inverse = split(spd_inverse(system, panel=8))
    solved = split(product(inverse, right))
    merged = direct - product(coupling, solved)
    stack(message_one, message_two, 0, packed(merged[0:128, 0:128]))
    stack(message_one, message_two, 96, merged[0:128, 128:256])
    stack(message_one, message_two, 224, merged[0:128, 256:384])
    stack(message_one, message_two, 352, merged[128:192, 128:256])
    stack(message_one, message_two, 416, merged[128:192, 256:384])
    link[...] = merged[128:192, 0:128]
    solved_high[...], solved_low[...] = solved


def rows_kernel(place, mine, theirs, solved_high, solved_low, outer, direct, coupling):
    alpha_rows, beta_rows = leaf_rows(place, mine, theirs)
    third, lead = place[1], place[2]
    far = jnp.where(place[0] == 0, 0, 1)
    direct[0:64, :], coupling[0:64, :] = alpha_rows(far)
    at_two = alpha_rows(2)
    at_far = beta_rows(far)
    at_three = beta_rows(3)
    direct[64:128, :], coupling[64:128, :] = either(third == 0, at_two, at_far)
    direct[128:192, :], coupling[128:192, :] = either(third == 0, at_far, at_three)
    spot = pl.ds(pl.multiple_of(lead * 96, 32), 96)
    solved = solved_high[...], solved_low[...]
    outer[...] = direct[spot, :] - product(split(coupling[spot, :][:, :FACE]), solved)


def second_kernel(own, received, outer, inverse_high, inverse_low, outer_high, outer_low):
    outer_high[...], outer_low[...] = split(outer[:, 0:128])
    system = unpacked(own[0:96, :] + received[0:96, :])
    inverse_high[...], inverse_low[...] = split(spd_inverse(system))


def assemble(alpha, beta):
    rows = (alpha or beta)[0].shape[0]
    left = halves((rows, 128))
    blank = jnp.zeros((rows, 128), F32)
    if alpha is None:
        tiles = (
            jnp.where(left, 0.0, turn(beta[0])),
            blank,
            jnp.where(left, 0.0, beta[0]),
            beta[1],
        )
        return jnp.concatenate(tiles, axis=1)
    turned = turn(alpha[1])
    middle = jnp.where(left, turn(alpha[0]), turned)
    if beta is None:
        tiles = jnp.where(left, alpha[0], 0.0), middle, jnp.where(left, turned, 0.0), blank
        return jnp.concatenate(tiles, axis=1)
    tiles = (
        jnp.where(left, alpha[0], turn(beta[0])),
        middle,
        jnp.where(left, turned, beta[0]),
        beta[1],
    )
    return jnp.concatenate(tiles, axis=1)


def exchange_kernel(
    place,
    own_one,
    own_two,
    received_one,
    received_two,
    link,
    inverse_high,
    inverse_low,
    message_one,
    message_two,
    right_high,
    right_low,
):
    is_alpha = place[0] == 0

    def both(mine, other):
        return jnp.where(is_alpha, mine, other), jnp.where(is_alpha, other, mine)

    def part(start, stop):
        return both(stacked(own_one, own_two, start, stop), stacked(received_one, received_two, start, stop))

    one, two = part(96, 224), part(224, 352)
    right = split(assemble((one[0], two[0]), (one[1], two[1])))
    face, back = part(352, 416), part(416, 480)
    direct = jnp.concatenate(
        [assemble((face[0], back[0]), None), assemble(None, (face[1], back[1]))], axis=0
    )
    mine = link[...]
    other = jnp.transpose(stacked(received_one, received_two, 96, 224))[0:FACE]
    coupling = jnp.concatenate(
        [jnp.where(is_alpha, mine, other), jnp.where(is_alpha, other, mine)], axis=0
    )
    solved = split(product(split(coupling), (inverse_high[...], inverse_low[...])))
    merged = direct - product(solved, right)
    stack(message_one, message_two, 0, packed(merged[:, 0:128]))
    for i in range(3):
        stack(message_one, message_two, 96 + 128 * i, merged[:, 128 * i + 128 : 128 * i + 256])
    right_high[...], right_low[...] = right


def rest_columns(one, two):
    return jnp.concatenate(
        [stacked(one, two, 128 * i + 96, 128 * i + 224) for i in range(3)], axis=1
    )


def outer_kernel(place, outer, outer_high, outer_low, inverse_high, inverse_low, right_high, right_low, rows):
    mine = outer[:, 128:256], outer[:, 256:384]
    direct = jnp.where(place[0] == 0, assemble(mine, None), assemble(None, mine))
    solved = split(product((outer_high[...], outer_low[...]), (inverse_high[...], inverse_low[...])))
    rows[...] = direct - product(solved, (right_high[...], right_low[...]))


def third_kernel(own_one, own_two, received, rows, half, solved_high, solved_low):
    right = split(rest_columns(own_one, own_two))
    system = unpacked(own_one[0:96, :] + received[0:96, :])
    solved = split(spd_inverse(system, rows[:, 0:128]))
    half[...] = rows[:, 128:512] + product(solved, right)
    solved_high[...], solved_low[...] = solved


def last_kernel(
    place, half, received_one, received_two, solved_high, solved_low, out, other, sems
):
    third = place[1]
    width = 6 * FACE

    def copy(source, side, start, i):
        first = pl.multiple_of(side * width + start, 128)
        target = out.at[:, pl.ds(first, source.shape[1])]
        return pltpu.make_async_copy(source, target, sems.at[i])

    copies = [copy(half, third, 0, 0)]
    copies[0].start()
    solved = solved_high[...], solved_low[...]
    for i in range(3):
        right = split(stacked(received_one, received_two, 128 * i + 96, 128 * i + 224))
        other[i] = product(solved, right)
        copies.append(copy(other.at[i], 1 - third, 128 * i, i + 1))
        copies[-1].start()
    for x in copies:
        x.wait()


def shapes(*sizes):
    return [jax.ShapeDtypeStruct(size, F32) for size in sizes]


def pair(*size):
    return [jax.ShapeDtypeStruct(size, BF16)] * 2


def run(kernel, out_shape, *operands, scalars=1, out_space=pltpu.VMEM, **options):
    smem = pl.BlockSpec(memory_space=pltpu.SMEM)
    vmem = pl.BlockSpec(memory_space=pltpu.VMEM)
    return pl.pallas_call(
        kernel,
        out_shape=out_shape,
        in_specs=[smem] * scalars + [vmem] * (len(operands) - scalars),
        out_specs=[pl.BlockSpec(memory_space=out_space)] * len(out_shape),
        compiler_params=pltpu.CompilerParams(vmem_limit_bytes=32 * 1024 * 1024),
        **options,
    )(*operands)


def body(leaf_maps, leaf_operator, region_eps, wave_sq, region_labels, build_flags):
    across = lax.axis_index("bx") % 2
    upward = lax.axis_index("by")
    place = jnp.stack([across, upward // 2 % 2, upward % 2]).astype(jnp.int32)
    size = leaf_operator.shape[0]
    mine = pl.pallas_call(
        build_kernel,
        out_shape=jax.ShapeDtypeStruct((LEAF, LEAF), F32),
        in_specs=[pl.BlockSpec(memory_space=pltpu.SMEM)] * 3
        + [pl.BlockSpec(memory_space=pltpu.HBM)] * 3,
        out_specs=pl.BlockSpec(memory_space=pltpu.VMEM),
        scratch_shapes=[
            pltpu.VMEM(region_eps.shape, F32),
            pltpu.VMEM((128, size), F32),
            pltpu.VMEM((size - LEAF - 128, size), F32),
            pltpu.VMEM((LEAF, size), F32),
            pltpu.SemaphoreType.DMA((5,)),
        ],
        compiler_params=pltpu.CompilerParams(vmem_limit_bytes=32 * 1024 * 1024),
        name="leaf_build",
    )(
        region_labels,
        build_flags,
        wave_sq,
        *(
            pltpu.with_memory_space_constraint(x, pltpu.HBM)
            for x in (leaf_maps[0, 0], leaf_operator, region_eps)
        ),
    )
    theirs = swapped(mine, "by", 0)
    one, two, link, *solved = run(
        first_kernel,
        shapes((CUT_TWO, 128), (MESSAGE - CUT_TWO, 128), (FACE, 128)) + pair(FACE, 6 * FACE),
        place,
        mine,
        theirs,
        name="first_merge",
    )
    received_one = swapped(one, "bx", 0)
    received_two = swapped(two, "bx", 0)
    (outer,) = run(
        rows_kernel,
        shapes((96, 6 * FACE)),
        place,
        mine,
        theirs,
        *solved,
        scratch_shapes=[pltpu.VMEM((192, 6 * FACE), F32), pltpu.VMEM((192, 128), F32)],
        name="first_rows",
    )
    *inverse, outer_high, outer_low = run(
        second_kernel,
        pair(128, 128) + pair(96, 128),
        one,
        received_one,
        outer,
        scalars=0,
        cost_estimate=LONG,
        name="second_inverse",
    )
    one, two, *right = run(
        exchange_kernel,
        shapes((CUT_THREE, 128), (MESSAGE - CUT_THREE, 128)) + pair(128, 8 * FACE),
        place,
        one,
        two,
        received_one,
        received_two,
        link,
        *inverse,
        name="second_merge",
    )
    received_one = swapped(one, "by", 1)
    received_two = swapped(two, "by", 1)
    (rows,) = run(
        outer_kernel,
        shapes((96, 8 * FACE)),
        place,
        outer,
        outer_high,
        outer_low,
        *inverse,
        *right,
        name="second_rows",
    )
    half, *solved = run(
        third_kernel,
        shapes((96, 6 * FACE)) + pair(96, 128),
        one,
        two,
        received_one,
        rows,
        scalars=0,
        cost_estimate=LONG,
        name="third_inverse",
    )
    (result,) = run(
        last_kernel,
        shapes((96, 12 * FACE)),
        place,
        half,
        received_one,
        received_two,
        *solved,
        scratch_shapes=[pltpu.VMEM((3, 96, 128), F32), pltpu.SemaphoreType.DMA((4,))],
        out_space=pltpu.HBM,
        name="third_merge",
    )
    return result.reshape((1, 1, 96, 12 * FACE))


def solution(mesh):
    placed = (
        P(("freq", "bx"), "by", None, None),
        P(),
        P(),
        P("freq"),
        P("bx", "by"),
        P("bx", "by"),
    )
    return jax.shard_map(
        body,
        mesh=mesh,
        in_specs=placed,
        out_specs=P(("freq", "bx"), "by", None, None),
        check_vma=False,
    )
```
